32 devices in a mesh: rep: 2 (over y), grid: 16 (over z, x, core).
Axes of the slice: x: 2, y: 2, z: 4, core: 2. Of those that a mesh axis runs over, the one named last changes fastest.
Arguments:
- pair_density: float32 [4, 2, 32, 32, 256], P('rep', None, 'grid'), parts along dimension 0, may hold values from -6 to 6
- moments: float32 [384, 2, 2, 25], P(('rep', 'grid')), parts along dimension 0, may hold values from -6 to 6
- shapes: float32 [2048, 25, 256], P(('rep', 'grid')), parts along dimension 0, may hold values from -2 to 2
- slot_atom: int32 [2048], P(('rep', 'grid')), parts along dimension 0, may hold values from 0 to 11
- slot_tile: int32 [2048, 1], P(('rep', 'grid')), parts along dimension 0, may hold values from 0 to 15; in each aligned block of 64 rows (0 to 63, 64 to 127, ...) at most 8 rows name the same one
- slot_row: int32 [2048], P(('rep', 'grid')), parts along dimension 0, may hold values from 0 to 63
- pair_table: int32 [2, 2], replicated, may hold values from 0 to 7
- k_fraction: float32 [8], replicated, may hold values from 0 to 1
Outputs:
- potential: float32 [4, 2, 32, 32, 256], P('rep', None, 'grid'), parts along dimension 0
The draws below stay inside these ranges and needn't reach their ends.
There are 2 independent parts, one for each index of `rep`. The reference program is written for one: setup_inputs(seed, part) draws one part's arguments, and reference() takes and returns one part's arrays. A program takes and returns all parts, laid end to end along the dimension named above; an argument that names none is the same for every part. Nothing has to cross between parts.
Inputs may be any that keep to these rules, and one draw needn't show every extreme that they name: `slot_tile`: among the slots of one device at most 8 name the same tile, and in every draw some device names some tile exactly 8 times.
All inputs are finite; a program needn't handle non-finite values.
Results may differ from the reference program's by a relative error of at most 0.0001.
Values sent between devices are 32-bit elements; how exact they have to be, the bound alone decides.
No kernel may reach another device: no remote copies, remote signals or barrier semaphores. Data moves between devices by JAX's collectives and lax.ppermute only.
A program may use at most 128 MiB of HBM per device.

```python
import math
from functools import partial
import jax
import jax.numpy as jnp
import numpy as np
from jax import lax

PAIRS = 2
CX = 2
NY = 32
NZ = 256
SLOT_DEV = 64
ATOM_DEV = 12
LM = 25
NK = 8
LEVELS = 3
SWEEPS = 2
COARSE_SWEEPS = 6
NX = 32
SLOTS = 1024
ATOMS = 192
CAP = 8
N_GRID = 16


def with_ends(values, rng, least, largest):
    shape = values.shape
    spot = [jax.random.randint(jax.random.fold_in(rng, axis), (), 0, shape[axis]) for axis in range(len(shape))]
    values = values.at[tuple(spot)].set(least)
    longest = shape.index(max(shape))
    spot[longest] = (spot[longest] + 1) % shape[longest]
    return values.at[tuple(spot)].set(largest)


def block_levels(key, extent, shards, low, top_value):
    level, own = 1.0, jax.random.fold_in(key, 6)
    for axis_at, parts in shards:
        heights = jnp.exp(jax.random.uniform(jax.random.fold_in(own, axis_at), (parts,), jnp.float32, low / len(shards), top_value / len(shards)))
        level = level * jnp.repeat(heights, extent[axis_at] // parts).reshape([-1 if axis == axis_at else 1 for axis in range(len(extent))])
    return level


def routed_block(key, own, number, rows, number_of, top, most, slope):
    sequence = jax.random.permutation(key, number_of)
    crowded, usual = portions_of(number_of, rows * top, most, slope, True), portions_of(number_of, rows * top, most, slope, False)
    places = jnp.arange(number_of)

    def named(lengths, rotation):
        used = int((lengths > 0).sum())
        fixed = max(1, used // 4)
        passed = fixed + (places - fixed + rotation * (used - fixed)) % max(1, number_of - fixed)
        return jnp.zeros((number_of,), jnp.int32).at[sequence[jnp.where(places < fixed, places, passed)]].set(jnp.asarray(lengths, jnp.int32))

    lengths = jnp.where(number % 4 == 0, named(crowded, number // 4), named(usual, number - number // 4 - 1))
    mixed = jax.random.permutation(jax.random.fold_in(own, 3), number_of)
    donor, taker = mixed[0:number_of // 2 * 2:2], mixed[1:number_of // 2 * 2:2]
    margin = jnp.minimum(lengths[donor] - 1, most - lengths[taker]) // 2
    margin = jnp.where((donor == sequence[0]) | (taker == sequence[0]) | (lengths[taker] == 0), 0, jnp.maximum(margin, 0))
    passed = jax.random.randint(jax.random.fold_in(own, 4), (number_of // 2,), 0, 1 << 20) % (margin + 1)
    lengths = lengths.at[donor].add(-passed).at[taker].add(passed)
    items = jnp.searchsorted(jnp.cumsum(lengths), jnp.arange(rows * top), side="right").astype(jnp.int32)
    listing = items.reshape(top, rows).T
    listing = listing[jax.random.permutation(jax.random.fold_in(own, 1), rows)]
    rotation = jax.random.randint(jax.random.fold_in(own, 2), (rows, 1), 0, top)
    return jnp.take_along_axis(listing, (jnp.arange(top)[None, :] + rotation) % top, axis=1)


def portions_of(count, total, limit, skew, full):
    portions = [(1 << 20) // math.isqrt(standing ** skew) + 1 for standing in range(1, count + 1)]
    largest = limit if full else min(limit, max(-(-total // count), total * portions[0] // sum(portions)))
    least = 1 if total - largest >= count - 1 else 0
    holding, surplus = [largest] + [least] * (count - 1), total - largest - least * (count - 1)
    while surplus > 0:
        free = [i for i in range(1, count) if holding[i] < largest] or [i for i in range(1, count) if holding[i] < limit]
        whole, budget = sum([portions[i] for i in free]), surplus
        for i in free:
            addition = min(limit - holding[i], max(1, budget * portions[i] // whole), surplus)
            holding[i] = holding[i] + addition
            surplus = surplus - addition
    return np.array(holding)


def centred(stream_key, extent, deviation, limit, cuts=(), kind=jnp.bfloat16):
    factor_of = block_levels(stream_key, extent, cuts, -0.22, 0.18) if cuts else 1.0
    array = jax.random.normal(stream_key, extent, jnp.float32) * deviation * factor_of
    return jnp.minimum(jnp.maximum(array, -limit), limit).astype(kind)


def setup_inputs(seed: int = 0, part: int = 0) -> dict:
    streams_of = jax.random.split(jax.random.key(seed), 9)
    own_keys = jax.random.split(jax.random.fold_in(streams_of[8], part), 9)
    pair_density = centred(own_keys[0], (PAIRS, 2, NX, NY, NZ), 1.0, 6.0, ((2, 16),), jnp.float32)
    moments = centred(own_keys[1], (ATOMS, PAIRS, 2, LM), 1.0, 6.0, ((0, 16),), jnp.float32)
    shapes = centred(own_keys[2], (SLOTS, LM, NZ), 0.3, 2.0, ((0, 16),), jnp.float32)
    slot_atom = with_ends(jax.random.randint(own_keys[3], (SLOTS,), 0, ATOM_DEV), jax.random.fold_in(own_keys[3], 1), 0, ATOM_DEV - 1).astype(jnp.int32)
    slot_tile_keys = jax.random.split(jax.random.fold_in(own_keys[4], 1), SLOTS // SLOT_DEV)
    slot_tile_turns = jax.random.permutation(jax.random.fold_in(own_keys[4], 3), SLOTS // SLOT_DEV)
    slot_tile = jax.vmap(lambda own, number: routed_block(jax.random.fold_in(own_keys[4], 2), own, number, SLOT_DEV, N_GRID, 1, CAP, 2))(slot_tile_keys, slot_tile_turns).reshape((SLOTS, 1))
    slot_row = with_ends(jax.random.randint(own_keys[5], (SLOTS,), 0, CX * NY), jax.random.fold_in(own_keys[5], 1), 0, (CX * NY) - 1).astype(jnp.int32)
    pair_table = with_ends(jax.random.randint(streams_of[6], (PAIRS, 2), 0, NK), jax.random.fold_in(streams_of[6], 1), 0, NK - 1).astype(jnp.int32)
    k_fraction = jnp.clip(jax.random.uniform(streams_of[7], (NK,), jnp.float32, 0.0, 1.0), 0.0, 1.0)
    return dict(pair_density=pair_density, moments=moments, shapes=shapes, slot_atom=slot_atom, slot_tile=slot_tile, slot_row=slot_row, pair_table=pair_table, k_fraction=k_fraction)


omega = 0.8
screen = 0.05
highest = lax.Precision.HIGHEST


def pair_phases(pair_table, k_fraction):
    angle = 6.283185307179586 * (k_fraction[pair_table[:, 0]] - k_fraction[pair_table[:, 1]])
    return jnp.cos(angle).reshape(-1, 1, 1, 1), jnp.sin(angle).reshape(-1, 1, 1, 1)


def rotate(values, cosine, sine):
    real_part = values[:, 0]
    imag_part = values[:, 1]
    return jnp.stack([cosine * real_part - sine * imag_part, sine * real_part + cosine * imag_part], axis=1)


def pad_planes(values, width, cosine, sine):
    before = rotate(values[:, :, -width:], cosine, -sine)
    after = rotate(values[:, :, :width], cosine, sine)
    return jnp.concatenate([before, values, after], axis=2)


def fine_apply(values, padded):
    planes = values.shape[2]
    nearest = padded[:, :, 1:planes + 1] + padded[:, :, 3:planes + 3]
    farther = padded[:, :, 0:planes] + padded[:, :, 4:planes + 4]
    for axis_id in (3, 4):
        nearest = nearest + jnp.roll(values, 1, axis_id) + jnp.roll(values, -1, axis_id)
        farther = farther + jnp.roll(values, 2, axis_id) + jnp.roll(values, -2, axis_id)
    return (7.5 + screen) * values - (4.0 / 3.0) * nearest + (1.0 / 12.0) * farther


def coarse_apply(values, padded, depth):
    scale_value = 1.0 / 4 ** depth
    planes = values.shape[2]
    nearest = padded[:, :, 0:planes] + padded[:, :, 2:planes + 2]
    for axis_id in (3, 4):
        nearest = nearest + jnp.roll(values, 1, axis_id) + jnp.roll(values, -1, axis_id)
    return (6.0 * scale_value + screen) * values - scale_value * nearest


def restrict_yz(values):
    sizes = values.shape
    blocks = values.reshape(sizes[0], sizes[1], sizes[2], sizes[3] // 2, 2, sizes[4] // 2, 2)
    return blocks.mean(axis=(4, 6))


def restrict_x(values):
    sizes = values.shape
    blocks = values.reshape(sizes[0], sizes[1], sizes[2] // 2, 2, sizes[3], sizes[4])
    return (blocks[:, :, :, 0] + blocks[:, :, :, 1]) * 0.5


def restrict(values):
    return restrict_x(restrict_yz(values))


def prolong(values):
    return jnp.repeat(jnp.repeat(jnp.repeat(values, 2, axis=2), 2, axis=3), 2, axis=4)


def relax(iterate, source, depth, padder, sweeps):
    diagonal_value = 6.0 / 4 ** depth + screen
    remaining = sweeps
    if iterate is None:
        iterate = omega * source / diagonal_value
        remaining = sweeps - 1
    for sweep_index in range(remaining):
        iterate = iterate + omega * (source - coarse_apply(iterate, padder(iterate), depth)) / diagonal_value
    return iterate


def whole_cycle(source, start_level, cosine, sine):
    padder = partial(pad_planes, width=1, cosine=cosine, sine=sine)
    sources = []
    iterates = []
    current = source
    for depth in range(start_level, LEVELS):
        iterate = relax(None, current, depth, padder, SWEEPS)
        residual = current - coarse_apply(iterate, padder(iterate), depth)
        sources.append(current)
        iterates.append(iterate)
        current = restrict(residual)
    iterate = relax(None, current, LEVELS, padder, COARSE_SWEEPS)
    for depth in range(LEVELS - 1, start_level - 1, -1):
        place = depth - start_level
        iterate = iterates[place] + prolong(iterate)
        iterate = relax(iterate, sources[place], depth, padder, SWEEPS)
    return iterate


def compensation(moments, shapes, slot_atom, slot_tile, slot_row):
    slot_count = shapes.shape[0]
    owner = jnp.arange(slot_count, dtype=jnp.int32) // SLOT_DEV
    atom_index = (owner * ATOM_DEV + slot_atom).astype(jnp.int32)
    chosen = moments[atom_index]
    rows = jnp.einsum("spcl,slz->pcsz", chosen, shapes, precision=highest)
    plane_index = slot_tile[:, 0] * CX + slot_row // NY
    line_index = slot_row % NY
    total = jnp.zeros((PAIRS, 2, NX, NY, NZ), jnp.float32)
    return total.at[:, :, plane_index, line_index, :].add(rows)


def reference(pair_density, moments, shapes, slot_atom, slot_tile, slot_row, pair_table, k_fraction):
    cosine, sine = pair_phases(pair_table, k_fraction)
    density = pair_density + compensation(moments, shapes, slot_atom, slot_tile, slot_row)
    fine_diagonal = 7.5 + screen
    iterate = omega * density / fine_diagonal
    for sweep_index in range(SWEEPS - 1):
        iterate = iterate + omega * (density - fine_apply(iterate, pad_planes(iterate, 2, cosine, sine))) / fine_diagonal
    residual = density - fine_apply(iterate, pad_planes(iterate, 2, cosine, sine))
    correction = whole_cycle(restrict(residual), 1, cosine, sine)
    iterate = iterate + prolong(correction)
    for sweep_index in range(SWEEPS):
        iterate = iterate + omega * (density - fine_apply(iterate, pad_planes(iterate, 2, cosine, sine))) / fine_diagonal
    return iterate
```

```python
import jax
import jax.numpy as jnp
from jax import lax
from jax.experimental import pallas as pl
from jax.experimental.pallas import tpu as pltpu
from jax.sharding import PartitionSpec as P

omega = 0.8
screen = 0.05
highest = lax.Precision.HIGHEST

fine_diagonal = 7.5 + screen
fine_scale = omega / fine_diagonal
fine_near = fine_scale * 4.0 / 3.0
fine_far = fine_scale / 12.0
keep = 1.0 - omega


def level_numbers(depth):
    quarter = 1.0 / 4**depth
    diagonal = 6.0 * quarter + screen
    return omega / diagonal, omega / diagonal * quarter


def each(count, body, most=16):
    if count <= most:
        for i in range(count):
            body(i)
    else:
        pl.loop(0, count, unroll=4)(body)


def dot(a, b):
    return jnp.dot(a, b, precision=highest, preferred_element_type=jnp.float32)


def pair_matrix(rows, columns, value):
    i = lax.broadcasted_iota(jnp.int32, (rows, columns), 0)
    j = lax.broadcasted_iota(jnp.int32, (rows, columns), 1)
    return jnp.where(i // 2 == j, value, 0.0)


def spread_matrix(rows, columns):
    i = lax.broadcasted_iota(jnp.int32, (rows, columns), 0)
    j = lax.broadcasted_iota(jnp.int32, (rows, columns), 1)
    return jnp.where(i == j // 2, 1.0, 0.0)


def roll(v, shift, axis):
    return pltpu.roll(v, shift % v.shape[axis], axis)


def smooth_fine(at, x, f):
    v = at(x, f)
    near = at(x - 1, f) + at(x + 1, f)
    far = at(x - 2, f) + at(x + 2, f)
    for axis in (0, 1):
        near = near + (roll(v, 1, axis) + roll(v, -1, axis))
        far = far + (roll(v, 2, axis) + roll(v, -2, axis))
    return keep * v + (fine_near * near - fine_far * far)


def rotated(real, imag, cosine, sine):
    return cosine * real - sine * imag, sine * real + cosine * imag


def place_planes(target, base, source, cosine, sine):
    for x in range(source.shape[0]):
        real, imag = rotated(source[x, 0], source[x, 1], cosine, sine)
        target[base + x, 0] = real
        target[base + x, 1] = imag


def place_halo(ext, middle, even_ref, odd_ref, cs_ref):
    position = lax.axis_index("grid")
    chips = lax.axis_size("grid") // 2
    core, chip = lax.rem(position, 2), lax.div(position, 2)
    cosine, sine = cs_ref[core], cs_ref[2 + core]
    first, last = chip == 0, chip == chips - 1
    low = (jnp.where(first, cosine, 1.0), jnp.where(first, -sine, 0.0))
    high = (jnp.where(last, cosine, 1.0), jnp.where(last, sine, 0.0))
    planes = even_ref.shape[0]
    parity = lax.rem(chip, 2)

    @pl.when(parity == 0)
    def _():
        place_planes(ext, middle - planes, odd_ref, *low)
        place_planes(ext, middle + planes, even_ref, *high)

    @pl.when(parity == 1)
    def _():
        place_planes(ext, middle - planes, even_ref, *low)
        place_planes(ext, middle + planes, odd_ref, *high)


def density_kernel(pd_ref, other_ref, received_ref, lines_ref, f_ref):
    core = lax.rem(lax.axis_index("grid"), 2)
    planes, _, lines, depth = f_ref.shape
    count = received_ref.shape[0]
    spread = (
        lax.broadcasted_iota(jnp.int32, (planes * lines, count), 0) == lines_ref[...]
    ).astype(jnp.float32)
    added = dot(spread, received_ref[...])
    for x in range(planes):
        for part in range(2):
            f_ref[x, part] = added[x * lines : (x + 1) * lines, part * depth : (part + 1) * depth]
    half = planes // 2
    for x in range(half):
        for part in range(2):
            f_ref[core * half + x, part] += pd_ref[core, part, x]
            f_ref[(1 - core) * half + x, part] += other_ref[part, x]


def source_kernel(even_ref, odd_ref, f_ref, cs_ref, s_ref, ext, b1, half):
    planes = f_ref.shape[0]
    lines, depth = f_ref.shape[2:]
    place_halo(ext, planes, even_ref, odd_ref, cs_ref)
    ext[planes : 2 * planes] = f_ref[...]
    for x in range(planes + 4):
        for part in range(2):
            b1[x, part] = smooth_fine(lambda i, p: ext[i, p], x + planes - 2, part)
    for i in range(planes // 2):
        for part in range(2):
            total = None
            for x in (2 * i, 2 * i + 1):
                value = smooth_fine(lambda i, p: b1[i, p], x + 2, part)
                total = value if total is None else total + value
            for h in range(2):
                half[(2 * i + part) * 2 + h] = total[:, h * 128 : (h + 1) * 128]
    rows = planes // 2 * 2
    left = [
        half[2 * r + h, pl.ds(0, lines // 2, 2)] + half[2 * r + h, pl.ds(1, lines // 2, 2)]
        for h in range(2)
        for r in range(rows)
    ]
    stacked = jnp.concatenate(left, axis=0)
    low, high = stacked[: rows * lines // 2], stacked[rows * lines // 2 :]
    matrix = pair_matrix(depth, depth // 2, 0.125)
    total = dot(low, matrix[:128]) + dot(high, matrix[128:])
    for r in range(rows):
        s_ref[r // 2, r % 2] = total[r * lines // 2 : (r + 1) * lines // 2]


def fine_kernel(
    even_ref, odd_ref, after_ref, before_ref, f_ref, cs_ref, own_ref, send_ref, ext, b1, b2, g
):
    position = lax.axis_index("grid")
    chips = lax.axis_size("grid") // 2
    core, chip = lax.rem(position, 2), lax.div(position, 2)
    cosine, sine = cs_ref[core], cs_ref[2 + core]
    planes = f_ref.shape[0]
    place_halo(ext, planes + 2, even_ref, odd_ref, cs_ref)
    ext[planes + 2 : 2 * planes + 2] = f_ref[...]
    first, last = chip < 2, chip >= chips - 2
    place_planes(
        ext, 0, before_ref, jnp.where(first, cosine, 1.0), jnp.where(first, -sine, 0.0)
    )
    place_planes(
        ext,
        3 * planes + 2,
        after_ref,
        jnp.where(last, cosine, 1.0),
        jnp.where(last, sine, 0.0),
    )
    for x in range(planes + 8):
        for part in range(2):
            b1[x, part] = smooth_fine(lambda i, p: ext[i, p], x + 2, part)
    for x in range(planes + 4):
        for part in range(2):
            b2[x, part] = smooth_fine(lambda i, p: b1[i, p], x + 2, part)
    for x in range(planes):
        for part in range(2):
            b3 = smooth_fine(lambda i, p: b2[i, p], x + 2, part)
            g[x, part] = fine_scale * (f_ref[x, part] + b1[x + 4, part] + b2[x + 2, part] + b3)
    half = planes // 2
    for x in range(half):
        own_ref[x] = g[core * half + x]
        send_ref[x] = g[(1 - core) * half + x]


def shift_z(v, step):
    width = v.shape[-1] // 2
    lane = lax.broadcasted_iota(jnp.int32, v.shape, len(v.shape) - 1)
    edge = 0 if step > 0 else width - 1
    inner = roll(v, step, 1)
    outer = roll(v, step + (width if step > 0 else -width), 1)
    return jnp.where(lane % width == edge, outer, inner)


def packed_sweep(values, count, depth, source, target, cosine, sine, residual=False):
    rate, near_rate = level_numbers(depth)
    real, imag = rotated(values[count, 0], values[count, 1], cosine, -sine)
    values[0, 0], values[0, 1] = real, imag
    real, imag = rotated(values[1, 0], values[1, 1], cosine, sine)
    values[count + 1, 0], values[count + 1, 1] = real, imag

    def body(x):
        for part in range(2):
            v = values[x + 1, part]
            near = values[x, part] + values[x + 2, part]
            near = near + (roll(v, 1, 0) + roll(v, -1, 0))
            near = near + (shift_z(v, 1) + shift_z(v, -1))
            if residual:
                target[x, part] = source[x, part] - omega / rate * v + near_rate / rate * near
            else:
                target[x + 1, part] = rate * source[x, part] + keep * v + near_rate * near

    each(count, body)


def first_sweep(values, count, depth, source):
    rate, _ = level_numbers(depth)

    def body(x):
        for part in range(2):
            values[x + 1, part] = rate * source[x, part]

    each(count, body)


def cycle_kernel(
    ag_ref, own_ref, other_ref, cs_ref, out_ref, u, v, r1, u2, v2, s2, r2, u3, v3, s3, w2, w1, e, b1
):
    position = lax.axis_index("grid")
    core = lax.rem(position, 2)
    count = u.shape[0] - 2
    lines, depth = u.shape[2:]
    rate, near_rate = level_numbers(1)
    cosines = [cs_ref[0], cs_ref[1]]
    sines = [cs_ref[2], cs_ref[3]]
    lane = lax.broadcasted_iota(jnp.int32, (8, 128), 1)
    lane_cosine = jnp.where(lane < 64, cosines[0], cosines[1])
    lane_sine = jnp.where(lane < 64, sines[0], sines[1])

    def source(x, f):
        return ag_ref[x // 2 * 2 + f // 2, x % 2, f % 2]

    def rims(values):
        for p in range(2):
            real, imag = rotated(
                values[count, 2 * p], values[count, 2 * p + 1], cosines[p], -sines[p]
            )
            values[0, 2 * p], values[0, 2 * p + 1] = real, imag
            real, imag = rotated(values[1, 2 * p], values[1, 2 * p + 1], cosines[p], sines[p])
            values[count + 1, 2 * p], values[count + 1, 2 * p + 1] = real, imag

    def sweep(values, target, residual=False):
        rims(values)

        def body(x):
            for f in range(4):
                a = values[x + 1, f]
                near = values[x, f] + values[x + 2, f]
                near = near + (roll(a, 1, 0) + roll(a, -1, 0))
                near = near + (roll(a, 1, 1) + roll(a, -1, 1))
                if residual:
                    target[x, f] = source(x, f) - omega / rate * a + near_rate / rate * near
                else:
                    target[x + 1, f] = rate * source(x, f) + keep * a + near_rate * near

        each(count, body)

    def start(x):
        for f in range(4):
            u[x + 1, f] = rate * source(x, f)

    each(count, start)
    sweep(u, v)
    sweep(v, r1, residual=True)

    count2 = count // 2
    i = lax.broadcasted_iota(jnp.int32, (128, 128), 0)
    j = lax.broadcasted_iota(jnp.int32, (128, 128), 1)
    down = [jnp.where(i // 2 + 64 * p == j, 0.125, 0.0) for p in range(2)]

    def lower(x):
        for f in range(4):
            r1[2 * x, f] = r1[2 * x, f] + r1[2 * x + 1, f]
        for part in range(2):
            total = None
            for p in range(2):
                f = 2 * p + part
                rows = r1[2 * x, f, pl.ds(0, 8, 2)] + r1[2 * x, f, pl.ds(1, 8, 2)]
                value = dot(rows, down[p])
                total = value if total is None else total + value
            s2[x, part] = total

    each(count2, lower)
    first_sweep(u2, count2, 2, s2)
    packed_sweep(u2, count2, 2, s2, v2, lane_cosine, lane_sine)

    packed_sweep(v2, count2, 2, s2, w2, lane_cosine, lane_sine, residual=True)

    count3 = count2 // 2
    down3 = jnp.where(i // 64 == j // 64, jnp.where(i % 64 // 2 == j % 32, 0.125, 0.0), 0.0)

    def lower3(x):
        for part in range(2):
            total = w2[2 * x, part] + w2[2 * x + 1, part]
            r2[x, part, 0:8] = total
            r2[x, part, 8:16] = total
            rows = r2[x, part, pl.ds(0, 8, 2)] + r2[x, part, pl.ds(1, 8, 2)]
            s3[x, part] = dot(rows, down3)

    each(count3, lower3)
    first_sweep(u3, count3, 3, s3)
    a, b = u3, v3
    for _ in range(5):
        packed_sweep(a, count3, 3, s3, b, lane_cosine, lane_sine)
        a, b = b, a

    up3 = jnp.where(i // 64 == j // 64, jnp.where(i % 64 == j % 64 // 2, 1.0, 0.0), 0.0)

    def raise3(x):
        for part in range(2):
            value = dot(a[x + 1, part], up3)
            r2[x, part, pl.ds(0, 8, 2)] = value
            r2[x, part, pl.ds(1, 8, 2)] = value
            value = r2[x, part, 0:8]
            for k in range(2):
                v2[2 * x + k + 1, part] = v2[2 * x + k + 1, part] + value

    each(count3, raise3)
    packed_sweep(v2, count2, 2, s2, u2, lane_cosine, lane_sine)
    packed_sweep(u2, count2, 2, s2, v2, lane_cosine, lane_sine)

    up = [jnp.where(i == j // 2 + 64 * p, 1.0, 0.0) for p in range(2)]

    def raise2(x):
        for part in range(2):
            for p in range(2):
                f = 2 * p + part
                value = dot(v2[x + 1, part], up[p])
                w1[x, f, pl.ds(0, 8, 2)] = value
                w1[x, f, pl.ds(1, 8, 2)] = value
                value = w1[x, f]
                for k in range(2):
                    v[2 * x + k + 1, f] = v[2 * x + k + 1, f] + value

    each(count2, raise2)
    sweep(v, u)
    sweep(u, v)

    matrix = spread_matrix(128, 256)
    planes = []
    for k in range(-2, 3):
        q = position + k
        low, high = q < 0, q >= count
        q = jnp.where(low, q + count, jnp.where(high, q - count, q))
        for p in range(2):
            cosine = jnp.where(low | high, cosines[p], 1.0)
            sine = jnp.where(low, -sines[p], jnp.where(high, sines[p], 0.0))
            planes.extend(rotated(v[q + 1, 2 * p], v[q + 1, 2 * p + 1], cosine, sine))
    wide = dot(jnp.concatenate(planes, axis=0), matrix)
    for k in range(5):
        for f in range(4):
            row = (4 * k + f) * lines
            for h in range(2):
                value = wide[row : row + lines, 128 * h : 128 * (h + 1)]
                e[(4 * k + f) * 2 + h, pl.ds(0, lines, 2)] = value
                e[(4 * k + f) * 2 + h, pl.ds(1, lines, 2)] = value

    def expanded(x, f):
        place = (4 * (x // 2) + f) * 2
        return jnp.concatenate([e[place], e[place + 1]], axis=1)

    for x in range(6):
        for f in range(4):
            b1[x, f] = smooth_fine(expanded, x + 2, f)
    half = own_ref.shape[0]
    for x in range(half):
        for part in range(2):
            out_ref[core, part, x] = own_ref[x, part]
            out_ref[1 - core, part, x] = other_ref[x, part]
    for x in range(half):
        for f in range(4):
            out_ref[f // 2, f % 2, x] += smooth_fine(lambda i, g: b1[i, g], x + 2, f)


def pair_phases(pair_table, k_fraction):
    kcount = k_fraction.shape[0]
    picks = pair_table[:, :, None] == jnp.arange(kcount, dtype=jnp.int32)[None, None, :]
    chosen = jnp.sum(jnp.where(picks, k_fraction[None, None, :], 0.0), axis=2)
    angle = 6.283185307179586 * (chosen[:, 0] - chosen[:, 1])
    return jnp.concatenate([jnp.cos(angle), jnp.sin(angle)])


def make_rows(moments, shapes, slot_atom, slot_tile, slot_row, tile_count):
    slot_count = shapes.shape[0]
    atom_count = moments.shape[0]
    capacity = max(2, 2 * slot_count // tile_count)
    atom_pick = (slot_atom[:, None] == jnp.arange(atom_count, dtype=jnp.int32)[None, :]).astype(
        jnp.float32
    )
    chosen = jnp.dot(atom_pick, moments.reshape(atom_count, -1), precision=highest)
    chosen = chosen.reshape(slot_count, moments.shape[1] * moments.shape[2], moments.shape[3])
    row_values = jnp.einsum("sfl,slz->sfz", chosen, shapes, precision=highest)
    tiles = slot_tile[:, 0]
    slot_ids = jnp.arange(slot_count, dtype=jnp.int32)
    before = (tiles[:, None] == tiles[None, :]) & (slot_ids[None, :] < slot_ids[:, None])
    ranks = jnp.sum(before.astype(jnp.int32), axis=1)
    places = tiles * capacity + ranks
    buckets = jnp.arange(tile_count * capacity, dtype=jnp.int32)
    pick = buckets[:, None] == places[None, :]
    targets = jnp.sum(jnp.where(pick, slot_row[None, :] + 1, 0), axis=1) - 1
    packed = jnp.dot(
        pick.astype(jnp.float32), row_values.reshape(slot_count, -1), precision=highest
    )
    packed = packed.reshape(tile_count // 2, 2 * capacity, 2, -1).transpose(0, 2, 1, 3)
    return packed.reshape(tile_count, 2 * capacity, -1), targets.reshape(tile_count, capacity)


def vmem(count):
    return [pl.BlockSpec(memory_space=pltpu.VMEM)] * count


smem = [pl.BlockSpec(memory_space=pltpu.SMEM)]


def call(kernel, out_shape, in_specs, scratch, flops):
    single = not isinstance(out_shape, (list, tuple))
    return pl.pallas_call(
        kernel,
        out_shape=out_shape,
        in_specs=in_specs,
        out_specs=vmem(1)[0] if single else vmem(len(out_shape)),
        scratch_shapes=[pltpu.VMEM(shape, jnp.float32) for shape in scratch],
        compiler_params=pltpu.CompilerParams(vmem_limit_bytes=48 * 2**20),
        cost_estimate=pl.CostEstimate(flops=flops, bytes_accessed=2**20, transcendentals=0),
    )


def shaped(*shape):
    return jax.ShapeDtypeStruct(shape, jnp.float32)


def per_device(
    pair_density, moments, shapes, slot_atom, slot_tile, slot_row, pair_table, k_fraction
):
    tile_count = lax.axis_size("grid")
    chips = tile_count // 2
    position = lax.axis_index("grid")
    core = position % 2
    chip = position // 2
    _, _, thick, lines, depth = pair_density.shape
    planes = 2 * thick
    devices = range(tile_count)

    def permute(value, target):
        return lax.ppermute(value, "grid", [(i, target(i)) for i in devices])

    def partner(i):
        return i ^ 1

    def even_side(i):
        return i ^ 2

    def odd_side(i):
        return (i // 2 + (1 if i // 2 % 2 else -1)) % chips * 2 + i % 2

    cs = pair_phases(pair_table, k_fraction)

    other = permute(lax.dynamic_index_in_dim(pair_density, 1 - core, 0, False), partner)
    packed, targets = make_rows(moments, shapes, slot_atom, slot_tile, slot_row, tile_count)
    every = lax.all_gather(targets, "grid", axis=0)
    mine = lax.dynamic_slice_in_dim(every, 2 * chip, 2, axis=1)
    tile_base = jnp.arange(2, dtype=jnp.int32)[None, :, None] * (thick * lines)
    line_ids = jnp.where(mine >= 0, mine + tile_base, -1).reshape(1, -1)
    received = lax.all_to_all(packed, "grid", split_axis=0, concat_axis=0, tiled=True)
    received = received.reshape(-1, received.shape[-1])

    block = (planes, 2, lines, depth)
    f = call(density_kernel, shaped(*block), vmem(4), [], 10**8)(
        pair_density, other, received, line_ids
    )
    even = permute(f, even_side)
    odd = permute(f, odd_side)
    after = permute(f[:thick], lambda i: (i - 4) % tile_count)
    before = permute(f[thick:], lambda i: (i + 4) % tile_count)
    source = call(
        source_kernel,
        shaped(planes // 2, 2, lines // 2, depth // 2),
        vmem(3) + smem,
        [
            (3 * planes, 2, lines, depth),
            (planes + 4, 2, lines, depth),
            (2 * planes, lines, 128),
        ],
        10**7,
    )(even, odd, f, cs)
    gathered = lax.all_gather(source, "grid", axis=0)
    own, send = call(
        fine_kernel,
        [shaped(thick, 2, lines, depth)] * 2,
        vmem(5) + smem,
        [
            (3 * planes + 4, 2, lines, depth),
            (planes + 8, 2, lines, depth),
            (planes + 4, 2, lines, depth),
            block,
        ],
        10**7,
    )(even, odd, after, before, f, cs)
    got = permute(send, partner)
    n1, n2, n3 = tile_count, tile_count // 2, tile_count // 4
    return call(
        cycle_kernel,
        shaped(*pair_density.shape),
        vmem(3) + smem,
        [
            (n1 + 2, 4, 16, 128),
            (n1 + 2, 4, 16, 128),
            (n1, 4, 16, 128),
            (n2 + 2, 2, 8, 128),
            (n2 + 2, 2, 8, 128),
            (n2, 2, 8, 128),
            (n2, 2, 16, 128),
            (n3 + 2, 2, 8, 128),
            (n3 + 2, 2, 8, 128),
            (n3, 2, 8, 128),
            (n2, 2, 8, 128),
            (n2, 4, 16, 128),
            (40, 32, 128),
            (6, 4, 32, 256),
        ],
        10**8,
    )(gathered, own, got, cs)


def solution(mesh):
    return jax.shard_map(
        per_device,
        mesh=mesh,
        in_specs=(
            P("rep", None, "grid", None, None),
            P(("rep", "grid"), None, None, None),
            P(("rep", "grid"), None, None),
            P(("rep", "grid")),
            P(("rep", "grid"), None),
            P(("rep", "grid")),
            P(),
            P(),
        ),
        out_specs=P("rep", None, "grid", None, None),
        check_vma=False,
    )
```

```python
import jax
import jax.numpy as jnp
from jax import lax
from jax.experimental import pallas as pl
from jax.experimental.pallas import tpu as pltpu
from jax.sharding import PartitionSpec as P

omega = 0.8
screen = 0.05
highest = lax.Precision.HIGHEST

fine_diagonal = 7.5 + screen
fine_scale = omega / fine_diagonal
fine_near = fine_scale * 4.0 / 3.0
fine_far = fine_scale / 12.0
keep = 1.0 - omega


def level_numbers(depth):
    quarter = 1.0 / 4**depth
    diagonal = 6.0 * quarter + screen
    return omega / diagonal, omega / diagonal * quarter


def each(count, body, most=16):
    if count <= most:
        for i in range(count):
            body(i)
    else:
        pl.loop(0, count, unroll=4)(body)


def dot(a, b):
    return jnp.dot(a, b, precision=highest, preferred_element_type=jnp.float32)


def pair_matrix(rows, columns, value):
    i = lax.broadcasted_iota(jnp.int32, (rows, columns), 0)
    j = lax.broadcasted_iota(jnp.int32, (rows, columns), 1)
    return jnp.where(i // 2 == j, value, 0.0)


def spread_matrix(rows, columns):
    i = lax.broadcasted_iota(jnp.int32, (rows, columns), 0)
    j = lax.broadcasted_iota(jnp.int32, (rows, columns), 1)
    return jnp.where(i == j // 2, 1.0, 0.0)


def roll(v, shift, axis):
    return pltpu.roll(v, shift % v.shape[axis], axis)


def smooth_fine(at, x, f):
    total = None
    for step, weight in ((1, fine_near), (2, -fine_far)):
        sides = [p for p in (at(x - step, f), at(x + step, f)) if p is not None]
        v = at(x, f)
        if v is not None:
            for axis in (0, 1):
                sides.append(roll(v, step, axis) + roll(v, -step, axis))
            if step == 1:
                total = keep * v
        if sides:
            part = weight * sum(sides[1:], sides[0])
            total = part if total is None else total + part
    return total


def rotated(real, imag, cosine, sine):
    return cosine * real - sine * imag, sine * real + cosine * imag


def place_planes(target, base, source, cosine, sine):
    for x in range(source.shape[0]):
        real, imag = rotated(source[x, 0], source[x, 1], cosine, sine)
        target[base + x, 0] = real
        target[base + x, 1] = imag


def place_halo(ext, middle, even_ref, odd_ref, cs_ref):
    position = lax.axis_index("grid")
    chips = lax.axis_size("grid") // 2
    core, chip = lax.rem(position, 2), lax.div(position, 2)
    cosine, sine = cs_ref[core], cs_ref[2 + core]
    first, last = chip == 0, chip == chips - 1
    low = (jnp.where(first, cosine, 1.0), jnp.where(first, -sine, 0.0))
    high = (jnp.where(last, cosine, 1.0), jnp.where(last, sine, 0.0))
    planes = even_ref.shape[0]
    parity = lax.rem(chip, 2)

    @pl.when(parity == 0)
    def _():
        place_planes(ext, middle - planes, odd_ref, *low)
        place_planes(ext, middle + planes, even_ref, *high)

    @pl.when(parity == 1)
    def _():
        place_planes(ext, middle - planes, even_ref, *low)
        place_planes(ext, middle + planes, odd_ref, *high)


def pack_kernel(rows_ref, column_ref, row_ref, line_ref, out_ref):
    slots = rows_ref.shape[0]
    tiles, height, _ = out_ref.shape
    ranks = (height - 8) // 4
    capacity = ranks // 2
    buckets = tiles * capacity
    chips = tiles // 2
    position = lax.axis_index("grid")
    i = lax.broadcasted_iota(jnp.int32, (slots, slots), 0)
    j = lax.broadcasted_iota(jnp.int32, (slots, slots), 1)
    ahead = jnp.where((column_ref[...] == row_ref[...]) & (i < j), 1.0, 0.0)
    rank = jnp.sum(ahead, axis=0, keepdims=True).astype(jnp.int32)
    place = row_ref[...] * capacity + rank
    bucket = lax.broadcasted_iota(jnp.int32, (buckets, slots), 0)
    pick = bucket == place
    packed = dot(pick.astype(jnp.float32), rows_ref[...])
    for chip in range(chips):
        for p in range(2):
            for q in range(4):
                out_ref[2 * chip + p, q * ranks : (q + 1) * ranks] = packed[
                    chip * ranks : (chip + 1) * ranks, (4 * p + q) * 128 : (4 * p + q + 1) * 128
                ]
    thick_lines = 64
    line = jnp.sum(jnp.where(pick, line_ref[...] + 1, 0).astype(jnp.float32), axis=1, keepdims=True)
    own = lax.broadcasted_iota(jnp.int32, (buckets, 1), 0) // capacity % 2
    line = jnp.where(line > 0, line + (own * thick_lines).astype(jnp.float32), 0.0)
    bucket = lax.broadcasted_iota(jnp.int32, (buckets, 128), 0)
    lane = lax.broadcasted_iota(jnp.int32, (buckets, 128), 1)
    start = lax.rem(position, 128 // ranks) * ranks
    spots = jnp.where(lane - start == bucket % ranks, line, 0.0)
    i = lax.broadcasted_iota(jnp.int32, (chips, buckets), 0)
    j = lax.broadcasted_iota(jnp.int32, (chips, buckets), 1)
    numbers = dot(jnp.where(i == j // ranks, 1.0, 0.0), spots)
    for chip in range(chips):
        value = jnp.broadcast_to(numbers[chip : chip + 1], (8, 128))
        for p in range(2):
            out_ref[2 * chip + p, 4 * ranks :] = value


def density_kernel(pd_ref, other_ref, received_ref, f_ref, inner_ref, outer_ref, b1, half):
    position = lax.axis_index("grid")
    core, side = lax.rem(position, 2), lax.rem(lax.div(position, 2), 2)
    planes, _, lines, depth = f_ref.shape
    sources, height, _ = received_ref.shape
    ranks = (height - 8) // 4
    group = 128 // ranks
    added = [None, None]
    for first in range(0, sources, group):
        count = min(group, sources - first)
        numbers = received_ref[first, 4 * ranks : 4 * ranks + 1]
        for k in range(1, count):
            numbers = numbers + received_ref[first + k, 4 * ranks : 4 * ranks + 1]
        line = lax.broadcasted_iota(jnp.int32, (planes * lines, 128), 0)
        spread = jnp.where(line == numbers.astype(jnp.int32) - 1, 1.0, 0.0)
        for part in range(2):
            values = jnp.concatenate(
                [
                    received_ref[first : first + count, q * ranks : (q + 1) * ranks].reshape(
                        count * ranks, 128
                    )
                    for q in (2 * part, 2 * part + 1)
                ],
                axis=1,
            )
            value = dot(spread[:, : count * ranks], values)
            added[part] = value if added[part] is None else added[part] + value
    for x in range(planes):
        for part in range(2):
            f_ref[x, part] = added[part][x * lines : (x + 1) * lines]
    thick = planes // 2
    for x in range(thick):
        for part in range(2):
            f_ref[core * thick + x, part] += pd_ref[core, part, x]
            f_ref[(1 - core) * thick + x, part] += other_ref[part, x]

    def density(x, part):
        return f_ref[x, part] if 0 <= x < planes else None

    def once(x, part):
        return b1[x + 2, part] if -2 <= x < planes + 2 else None

    for x in range(-2, planes + 2):
        for part in range(2):
            b1[x + 2, part] = smooth_fine(density, x, part)
    rows = (planes + 8) // 2 * 2
    for i in range(rows // 2):
        for part in range(2):
            total = smooth_fine(once, 2 * i - 4, part) + smooth_fine(once, 2 * i - 3, part)
            for h in range(2):
                half[(2 * i + part) * 2 + h] = total[:, h * 128 : (h + 1) * 128]
    matrix = pair_matrix(depth, depth // 2, 0.125)
    total = None
    for h in range(2):
        stacked = jnp.concatenate(
            [
                half[2 * r + h, pl.ds(0, lines // 2, 2)] + half[2 * r + h, pl.ds(1, lines // 2, 2)]
                for r in range(rows)
            ],
            axis=0,
        )
        value = dot(stacked, matrix[h * 128 : (h + 1) * 128])
        total = value if total is None else total + value

    def coarse(r):
        return total[r * lines // 2 : (r + 1) * lines // 2]

    @pl.when(side == 0)
    def _():
        for r in range(8):
            inner_ref[r // 2, r % 2] = coarse(4 + r)
        for r in range(4):
            outer_ref[r // 2, r % 2] = coarse(r)

    @pl.when(side == 1)
    def _():
        for r in range(8):
            inner_ref[r // 2, r % 2] = coarse(r)
        for r in range(4):
            outer_ref[r // 2, r % 2] = coarse(8 + r)


def source_kernel(own_ref, partner_ref, straight_ref, across_ref, cs_ref, s_ref):
    position = lax.axis_index("grid")
    blocks = lax.axis_size("grid") // 4
    core, side, block = lax.rem(position, 2), lax.rem(lax.div(position, 2), 2), lax.div(position, 4)
    cosine, sine = cs_ref[core], cs_ref[2 + core]
    first, last = block == 0, block == blocks - 1
    low = (jnp.where(first, cosine, 1.0), jnp.where(first, -sine, 0.0))
    high = (jnp.where(last, cosine, 1.0), jnp.where(last, sine, 0.0))

    def total(low_ref, high_ref):
        for x in range(4):
            source, (c, s) = (low_ref, low) if x < 2 else (high_ref, high)
            real, imag = rotated(source[x % 2, 0], source[x % 2, 1], c, s)
            s_ref[x, 0] = own_ref[x, 0] + partner_ref[x, 0] + real
            s_ref[x, 1] = own_ref[x, 1] + partner_ref[x, 1] + imag

    @pl.when(side == 0)
    def _():
        total(across_ref, straight_ref)

    @pl.when(side == 1)
    def _():
        total(straight_ref, across_ref)


def fine_kernel(
    even_ref, odd_ref, after_ref, before_ref, f_ref, cs_ref, own_ref, send_ref, ext, b1, b2, g
):
    position = lax.axis_index("grid")
    chips = lax.axis_size("grid") // 2
    core, chip = lax.rem(position, 2), lax.div(position, 2)
    cosine, sine = cs_ref[core], cs_ref[2 + core]
    planes = f_ref.shape[0]
    place_halo(ext, planes + 2, even_ref, odd_ref, cs_ref)
    ext[planes + 2 : 2 * planes + 2] = f_ref[...]
    first, last = chip < 2, chip >= chips - 2
    place_planes(
        ext, 0, before_ref, jnp.where(first, cosine, 1.0), jnp.where(first, -sine, 0.0)
    )
    place_planes(
        ext,
        3 * planes + 2,
        after_ref,
        jnp.where(last, cosine, 1.0),
        jnp.where(last, sine, 0.0),
    )
    for x in range(planes + 8):
        for part in range(2):
            b1[x, part] = smooth_fine(lambda i, p: ext[i, p], x + 2, part)
    for x in range(planes + 4):
        for part in range(2):
            b2[x, part] = smooth_fine(lambda i, p: b1[i, p], x + 2, part)
    for x in range(planes):
        for part in range(2):
            b3 = smooth_fine(lambda i, p: b2[i, p], x + 2, part)
            g[x, part] = fine_scale * (f_ref[x, part] + b1[x + 4, part] + b2[x + 2, part] + b3)
    half = planes // 2
    for x in range(half):
        own_ref[x] = g[core * half + x]
        send_ref[x] = g[(1 - core) * half + x]


def shift_z(v, step):
    width = v.shape[-1] // 2
    lane = lax.broadcasted_iota(jnp.int32, v.shape, len(v.shape) - 1)
    edge = 0 if step > 0 else width - 1
    inner = roll(v, step, 1)
    outer = roll(v, step + (width if step > 0 else -width), 1)
    return jnp.where(lane % width == edge, outer, inner)


def packed_sweep(values, count, depth, source, target, cosine, sine, residual=False):
    rate, near_rate = level_numbers(depth)
    values[0] = cosine * values[count] - sine * roll(values[count], 64, 1)
    values[count + 1] = cosine * values[1] + sine * roll(values[1], 64, 1)

    def body(x):
        v = values[x + 1]
        near = values[x] + values[x + 2]
        near = near + (roll(v, 1, 0) + roll(v, -1, 0))
        near = near + (shift_z(v, 1) + shift_z(v, -1))
        if residual:
            target[x] = source[x] - omega / rate * v + near_rate / rate * near
        else:
            target[x + 1] = rate * source[x] + keep * v + near_rate * near

    each(count, body)


def first_sweep(values, count, depth, source):
    rate, _ = level_numbers(depth)

    def body(x):
        values[x + 1] = rate * source[x]

    each(count, body)


def cycle_kernel(*refs):
    radix = len(refs) - 14
    pieces, refs = refs[:radix], refs[radix:]
    cs_ref, own_ref, send_ref, s, u, v, r1, s2, u2, v2, r2, s3, u3, v3 = refs
    position = lax.axis_index("grid")
    core, block = lax.rem(position, 2), lax.div(position, 4)
    count = s.shape[0]
    rate, near_rate = level_numbers(1)
    cosine, sine = cs_ref[core], cs_ref[2 + core]
    lane = lax.broadcasted_iota(jnp.int32, (8, 128), 1)
    lane_sine = jnp.where(lane < 64, -sine, sine)

    length = count // radix
    digit = lax.div(block, length // 4)
    for k, piece in enumerate(pieces):
        s[pl.ds(lax.rem(digit + k, radix) * length, length)] = piece[...]

    def sweep(values, target, residual=False):
        values[0, 0], values[0, 1] = rotated(values[count, 0], values[count, 1], cosine, -sine)
        values[count + 1, 0], values[count + 1, 1] = rotated(
            values[1, 0], values[1, 1], cosine, sine
        )

        def body(x):
            for f in range(2):
                a = values[x + 1, f]
                near = values[x, f] + values[x + 2, f]
                near = near + (roll(a, 1, 0) + roll(a, -1, 0))
                near = near + (roll(a, 1, 1) + roll(a, -1, 1))
                if residual:
                    target[x, f] = s[x, f] - omega / rate * a + near_rate / rate * near
                else:
                    target[x + 1, f] = rate * s[x, f] + keep * a + near_rate * near

        each(count, body)

    def start(x):
        for f in range(2):
            u[x + 1, f] = rate * s[x, f]

    each(count, start)
    sweep(u, v)
    sweep(v, r1, residual=True)

    count2 = count // 2
    i = lax.broadcasted_iota(jnp.int32, (128, 128), 0)
    j = lax.broadcasted_iota(jnp.int32, (128, 128), 1)
    rows = []
    for f in range(2):

        def lower(x):
            r1[2 * x, f] = r1[2 * x, f] + r1[2 * x + 1, f]
            r2[x, 8 * f : 8 * f + 8] = r1[2 * x, f, pl.ds(0, 8, 2)] + r1[2 * x, f, pl.ds(1, 8, 2)]

        each(count2, lower)
        rows.append(r2[:, 8 * f : 8 * f + 8].reshape(count2 * 8, 128))
    lowered = sum(
        dot(rows[f], jnp.where(i // 2 + 64 * f == j, 0.125, 0.0)) for f in range(2)
    )
    s2[...] = lowered.reshape(count2, 8, 128)
    first_sweep(u2, count2, 2, s2)
    packed_sweep(u2, count2, 2, s2, v2, cosine, lane_sine)
    packed_sweep(v2, count2, 2, s2, u2, cosine, lane_sine, residual=True)

    count3 = count2 // 2

    def lower3(x):
        total = u2[2 * x] + u2[2 * x + 1]
        r2[x, 0:8] = total
        r2[x, 8:16] = total
        s3[x] = r2[x, pl.ds(0, 8, 2)] + r2[x, pl.ds(1, 8, 2)]

    each(count3, lower3)
    same = i // 64 == j // 64
    lowered = dot(
        s3[...].reshape(count3 * 8, 128), jnp.where(same & (i % 64 // 2 == j % 32), 0.125, 0.0)
    )
    s3[...] = lowered.reshape(count3, 8, 128)
    first_sweep(u3, count3, 3, s3)
    a, b = u3, v3
    for _ in range(5):
        packed_sweep(a, count3, 3, s3, b, cosine, lane_sine)
        a, b = b, a

    raised = dot(
        a[1 : count3 + 1].reshape(count3 * 8, 128),
        jnp.where(same & (i % 64 == j % 64 // 2), 1.0, 0.0),
    )
    s3[...] = raised.reshape(count3, 8, 128)

    def raise3(x):
        r2[x, pl.ds(0, 8, 2)] = s3[x]
        r2[x, pl.ds(1, 8, 2)] = s3[x]
        for k in range(2):
            v2[2 * x + k + 1] = v2[2 * x + k + 1] + r2[x, 0:8]

    each(count3, raise3)
    packed_sweep(v2, count2, 2, s2, u2, cosine, lane_sine)
    packed_sweep(u2, count2, 2, s2, v2, cosine, lane_sine)

    rows = v2[1 : count2 + 1].reshape(count2 * 8, 128)
    for f in range(2):
        raised = dot(rows, jnp.where(i == j // 2 + 64 * f, 1.0, 0.0))
        s2[...] = raised.reshape(count2, 8, 128)

        def raise2(x):
            r1[x, f, pl.ds(0, 8, 2)] = s2[x]
            r1[x, f, pl.ds(1, 8, 2)] = s2[x]
            for k in range(2):
                v[2 * x + k + 1, f] = v[2 * x + k + 1, f] + r1[x, f]

        each(count2, raise2)
    sweep(v, u)
    sweep(u, v)

    for target, tile in ((own_ref, position), (send_ref, position + 1 - 2 * core)):
        for k in range(5):
            q = tile + k - 2
            low, high = q < 0, q >= count
            q = jnp.where(low, q + count, jnp.where(high, q - count, q))
            c = jnp.where(low | high, cosine, 1.0)
            t = jnp.where(low, -sine, jnp.where(high, sine, 0.0))
            target[k, 0], target[k, 1] = rotated(v[q + 1, 0], v[q + 1, 1], c, t)


def correct(w_ref, g_ref, e, b1, store):
    lines = w_ref.shape[2]
    wide = dot(w_ref[...].reshape(10 * lines, 128), spread_matrix(128, 256))
    for r in range(10):
        for h in range(2):
            value = wide[r * lines : (r + 1) * lines, 128 * h : 128 * (h + 1)]
            e[2 * r + h, pl.ds(0, lines, 2)] = value
            e[2 * r + h, pl.ds(1, lines, 2)] = value

    def expanded(x, f):
        place = (2 * (x // 2) + f) * 2
        return jnp.concatenate([e[place], e[place + 1]], axis=1)

    for x in range(6):
        for f in range(2):
            b1[x, f] = smooth_fine(expanded, x + 2, f)
    for x in range(2):
        for f in range(2):
            store(f, x, g_ref[x, f] + smooth_fine(lambda i, g: b1[i, g], x + 2, f))


def own_kernel(w_ref, g_ref, out_ref, e, b1):
    def store(part, x, value):
        out_ref[part, x] = value

    correct(w_ref, g_ref, e, b1, store)


def output_kernel(own_ref, w_ref, g_ref, out_ref, e, b1):
    core = lax.rem(lax.axis_index("grid"), 2)
    out_ref[core] = own_ref[...]

    def store(part, x, value):
        out_ref[1 - core, part, x] = value

    correct(w_ref, g_ref, e, b1, store)


def pair_phases(pair_table, k_fraction):
    kcount = k_fraction.shape[0]
    picks = pair_table[:, :, None] == jnp.arange(kcount, dtype=jnp.int32)[None, None, :]
    chosen = jnp.sum(jnp.where(picks, k_fraction[None, None, :], 0.0), axis=2)
    angle = 6.283185307179586 * (chosen[:, 0] - chosen[:, 1])
    return jnp.concatenate([jnp.cos(angle), jnp.sin(angle)])


def make_rows(moments, shapes, slot_atom):
    slot_count = shapes.shape[0]
    atom_count = moments.shape[0]
    atom_pick = (slot_atom[:, None] == jnp.arange(atom_count, dtype=jnp.int32)[None, :]).astype(
        jnp.float32
    )
    chosen = jnp.dot(atom_pick, moments.reshape(atom_count, -1), precision=highest)
    chosen = chosen.reshape(slot_count, moments.shape[1] * moments.shape[2], moments.shape[3])
    return jnp.einsum("sfl,slz->sfz", chosen, shapes, precision=highest).reshape(slot_count, -1)


def gather_blocks(value, blocks, block, permute_block):
    stride = 1
    while True:
        radix = min(4, blocks // stride)
        digit = block // stride % radix

        def towards(k):
            def target(b):
                own = b // stride % radix
                return b + ((own - k) % radix - own) * stride

            return target

        pieces = [value] + [permute_block(value, towards(k)) for k in range(1, radix)]
        stride *= radix
        if stride == blocks:
            return pieces
        stacked = jnp.roll(jnp.stack(pieces), digit, axis=0)
        value = stacked.reshape(-1, *value.shape[1:])


def vmem(count):
    return [pl.BlockSpec(memory_space=pltpu.VMEM)] * count


smem = [pl.BlockSpec(memory_space=pltpu.SMEM)]


def call(kernel, out_shape, in_specs, scratch, flops):
    single = not isinstance(out_shape, (list, tuple))
    return pl.pallas_call(
        kernel,
        out_shape=out_shape,
        in_specs=in_specs,
        out_specs=vmem(1)[0] if single else vmem(len(out_shape)),
        scratch_shapes=[pltpu.VMEM(shape, jnp.float32) for shape in scratch],
        compiler_params=pltpu.CompilerParams(vmem_limit_bytes=48 * 2**20),
        cost_estimate=pl.CostEstimate(flops=flops, bytes_accessed=2**20, transcendentals=0),
    )


def shaped(*shape):
    return jax.ShapeDtypeStruct(shape, jnp.float32)


def per_device(
    pair_density, moments, shapes, slot_atom, slot_tile, slot_row, pair_table, k_fraction
):
    tile_count = lax.axis_size("grid")
    chips, blocks = tile_count // 2, tile_count // 4
    position = lax.axis_index("grid")
    core, block = position % 2, position // 4
    _, _, thick, lines, depth = pair_density.shape
    planes = 2 * thick
    slot_count = shapes.shape[0]
    capacity = max(2, 2 * slot_count // tile_count)
    devices = range(tile_count)

    def permute(value, target):
        return lax.ppermute(value, "grid", [(i, target(i)) for i in devices])

    def permute_block(value, target):
        return permute(value, lambda i: target(i // 4) * 4 + i % 4)

    def partner(i):
        return i ^ 1

    def even_side(i):
        return i ^ 2

    def odd_side(i):
        return (i // 2 + (1 if i // 2 % 2 else -1)) % chips * 2 + i % 2

    def next_block(i):
        return (i + (4 if i // 2 % 2 else -4)) % tile_count

    cs = pair_phases(pair_table, k_fraction)

    other = permute(lax.dynamic_index_in_dim(pair_density, 1 - core, 0, False), partner)
    rows = make_rows(moments, shapes, slot_atom)
    packed = call(pack_kernel, shaped(tile_count, 8 * capacity + 8, 128), vmem(4), [], 10**8)(
        rows, slot_tile, slot_tile.reshape(1, -1), slot_row.reshape(1, -1)
    )
    received = lax.all_to_all(packed, "grid", split_axis=0, concat_axis=0, tiled=True)

    full = (2, lines, depth)
    small = (2, lines // 2, depth // 2)
    f, inner, outer = call(
        density_kernel,
        [shaped(planes, *full), shaped(4, *small), shaped(2, *small)],
        vmem(3),
        [(planes + 4, *full), (2 * (planes + 8), lines, 128)],
        10**8,
    )(pair_density, other, received)
    source = call(source_kernel, shaped(4, *small), vmem(4) + smem, [], 10**6)(
        inner, permute(inner, even_side), permute(outer, next_block), permute(outer, odd_side), cs
    )
    pieces = gather_blocks(source, blocks, block, permute_block)

    even = permute(f, even_side)
    odd = permute(f, odd_side)
    after = permute(f[:thick], lambda i: (i - 4) % tile_count)
    before = permute(f[thick:], lambda i: (i + 4) % tile_count)
    own, send = call(
        fine_kernel,
        [shaped(thick, *full)] * 2,
        vmem(5) + smem,
        [(3 * planes + 4, *full), (planes + 8, *full), (planes + 4, *full), (planes, *full)],
        10**7,
    )(even, odd, after, before, f, cs)
    got = permute(send, partner)

    n1, n2, n3 = tile_count, tile_count // 2, tile_count // 4
    tile = (8, 128)
    w_own, w_send = call(
        cycle_kernel,
        [shaped(5, *small)] * 2,
        vmem(len(pieces)) + smem,
        [
            (n1, *small),
            (n1 + 2, *small),
            (n1 + 2, *small),
            (n1, *small),
            (n2, *tile),
            (n2 + 2, *tile),
            (n2 + 2, *tile),
            (n2, 16, 128),
            (n3, *tile),
            (n3 + 2, *tile),
            (n3 + 2, *tile),
        ],
        10**8,
    )(*pieces, cs)
    w_got = permute(w_send, partner)
    scratch = [(20, lines, 128), (6, *full)]
    result = call(own_kernel, shaped(2, thick, lines, depth), vmem(2), scratch, 10**7)(w_own, own)
    return call(output_kernel, shaped(*pair_density.shape), vmem(3), scratch, 10**7)(
        result, w_got, got
    )


def solution(mesh):
    return jax.shard_map(
        per_device,
        mesh=mesh,
        in_specs=(
            P("rep", None, "grid", None, None),
            P(("rep", "grid"), None, None, None),
            P(("rep", "grid"), None, None),
            P(("rep", "grid")),
            P(("rep", "grid"), None),
            P(("rep", "grid")),
            P(),
            P(),
        ),
        out_specs=P("rep", None, "grid", None, None),
        check_vma=False,
    )
```

```python
import jax
import jax.numpy as jnp
from jax import lax
from jax.experimental import pallas as pl
from jax.experimental.pallas import tpu as pltpu
from jax.sharding import PartitionSpec as P

omega = 0.8
screen = 0.05
highest = lax.Precision.HIGHEST

fine_diagonal = 7.5 + screen
fine_scale = omega / fine_diagonal
fine_near = fine_scale * 4.0 / 3.0
fine_far = fine_scale / 12.0
keep = 1.0 - omega


def level_numbers(depth):
    quarter = 1.0 / 4**depth
    diagonal = 6.0 * quarter + screen
    return omega / diagonal, omega / diagonal * quarter


def each(count, body, most=16):
    if count <= most:
        for i in range(count):
            body(i)
    else:
        pl.loop(0, count, unroll=4)(body)


def dot(a, b):
    return jnp.dot(a, b, precision=highest, preferred_element_type=jnp.float32)


def pair_matrix(rows, columns, value):
    i = lax.broadcasted_iota(jnp.int32, (rows, columns), 0)
    j = lax.broadcasted_iota(jnp.int32, (rows, columns), 1)
    return jnp.where(i // 2 == j, value, 0.0)


def spread_matrix(rows, columns):
    i = lax.broadcasted_iota(jnp.int32, (rows, columns), 0)
    j = lax.broadcasted_iota(jnp.int32, (rows, columns), 1)
    return jnp.where(i == j // 2, 1.0, 0.0)


def roll(v, shift, axis):
    return pltpu.roll(v, shift % v.shape[axis], axis)


def smooth_fine(at, x, f):
    total = None
    for step, weight in ((1, fine_near), (2, -fine_far)):
        sides = [p for p in (at(x - step, f), at(x + step, f)) if p is not None]
        v = at(x, f)
        if v is not None:
            for axis in (0, 1):
                sides.append(roll(v, step, axis) + roll(v, -step, axis))
            if step == 1:
                total = keep * v
        if sides:
            part = weight * sum(sides[1:], sides[0])
            total = part if total is None else total + part
    return total


def rotated(real, imag, cosine, sine):
    return cosine * real - sine * imag, sine * real + cosine * imag


def place_planes(target, base, source, cosine, sine):
    for x in range(source.shape[0]):
        real, imag = rotated(source[x, 0], source[x, 1], cosine, sine)
        target[base + x, 0] = real
        target[base + x, 1] = imag


def place_halo(ext, middle, even_ref, odd_ref, cs_ref):
    position = lax.axis_index("grid")
    chips = lax.axis_size("grid") // 2
    core, chip = lax.rem(position, 2), lax.div(position, 2)
    cosine, sine = cs_ref[core], cs_ref[2 + core]
    first, last = chip == 0, chip == chips - 1
    low = (jnp.where(first, cosine, 1.0), jnp.where(first, -sine, 0.0))
    high = (jnp.where(last, cosine, 1.0), jnp.where(last, sine, 0.0))
    planes = even_ref.shape[0]
    parity = lax.rem(chip, 2)

    @pl.when(parity == 0)
    def _():
        place_planes(ext, middle - planes, odd_ref, *low)
        place_planes(ext, middle + planes, even_ref, *high)

    @pl.when(parity == 1)
    def _():
        place_planes(ext, middle - planes, even_ref, *low)
        place_planes(ext, middle + planes, odd_ref, *high)


def pack_kernel(rows_ref, column_ref, row_ref, line_ref, out_ref):
    slots = rows_ref.shape[0]
    tiles, height, _ = out_ref.shape
    ranks = (height - 8) // 4
    capacity = ranks // 2
    buckets = tiles * capacity
    chips = tiles // 2
    position = lax.axis_index("grid")
    i = lax.broadcasted_iota(jnp.int32, (slots, slots), 0)
    j = lax.broadcasted_iota(jnp.int32, (slots, slots), 1)
    ahead = jnp.where((column_ref[...] == row_ref[...]) & (i < j), 1.0, 0.0)
    rank = jnp.sum(ahead, axis=0, keepdims=True).astype(jnp.int32)
    place = row_ref[...] * capacity + rank
    bucket = lax.broadcasted_iota(jnp.int32, (buckets, slots), 0)
    pick = bucket == place
    packed = dot(pick.astype(jnp.float32), rows_ref[...])
    for chip in range(chips):
        for p in range(2):
            for q in range(4):
                out_ref[2 * chip + p, q * ranks : (q + 1) * ranks] = packed[
                    chip * ranks : (chip + 1) * ranks, (4 * p + q) * 128 : (4 * p + q + 1) * 128
                ]
    thick_lines = 64
    line = jnp.sum(jnp.where(pick, line_ref[...] + 1, 0).astype(jnp.float32), axis=1, keepdims=True)
    own = lax.broadcasted_iota(jnp.int32, (buckets, 1), 0) // capacity % 2
    line = jnp.where(line > 0, line + (own * thick_lines).astype(jnp.float32), 0.0)
    bucket = lax.broadcasted_iota(jnp.int32, (buckets, 128), 0)
    lane = lax.broadcasted_iota(jnp.int32, (buckets, 128), 1)
    start = lax.rem(position, 128 // ranks) * ranks
    spots = jnp.where(lane - start == bucket % ranks, line, 0.0)
    i = lax.broadcasted_iota(jnp.int32, (chips, buckets), 0)
    j = lax.broadcasted_iota(jnp.int32, (chips, buckets), 1)
    numbers = dot(jnp.where(i == j // ranks, 1.0, 0.0), spots)
    for chip in range(chips):
        value = jnp.broadcast_to(numbers[chip : chip + 1], (8, 128))
        for p in range(2):
            out_ref[2 * chip + p, 4 * ranks :] = value


def density_kernel(pd_ref, other_ref, received_ref, f_ref, straight_ref, across_ref, b1, half):
    position = lax.axis_index("grid")
    core, side = lax.rem(position, 2), lax.rem(lax.div(position, 2), 2)
    planes, _, lines, depth = f_ref.shape
    sources, height, _ = received_ref.shape
    ranks = (height - 8) // 4
    group = 128 // ranks
    added = [None, None]
    for first in range(0, sources, group):
        count = min(group, sources - first)
        numbers = received_ref[first, 4 * ranks : 4 * ranks + 1]
        for k in range(1, count):
            numbers = numbers + received_ref[first + k, 4 * ranks : 4 * ranks + 1]
        line = lax.broadcasted_iota(jnp.int32, (planes * lines, 128), 0)
        spread = jnp.where(line == numbers.astype(jnp.int32) - 1, 1.0, 0.0)
        for part in range(2):
            values = jnp.concatenate(
                [
                    received_ref[first : first + count, q * ranks : (q + 1) * ranks].reshape(
                        count * ranks, 128
                    )
                    for q in (2 * part, 2 * part + 1)
                ],
                axis=1,
            )
            value = dot(spread[:, : count * ranks], values)
            added[part] = value if added[part] is None else added[part] + value
    for x in range(planes):
        for part in range(2):
            f_ref[x, part] = added[part][x * lines : (x + 1) * lines]
    thick = planes // 2
    for x in range(thick):
        for part in range(2):
            f_ref[core * thick + x, part] += pd_ref[core, part, x]
            f_ref[(1 - core) * thick + x, part] += other_ref[part, x]

    def density(x, part):
        return f_ref[x, part] if 0 <= x < planes else None

    def once(x, part):
        return b1[x + 2, part] if -2 <= x < planes + 2 else None

    def outer(base, first_plane, one):
        for x in range(one, one + 4):
            for part in range(2):
                b1[x + 2, part] = smooth_fine(density, x, part)
        for i in range(2):
            for part in range(2):
                x = base + 2 * i
                total = smooth_fine(once, x, part) + smooth_fine(once, x + 1, part)
                for h in range(2):
                    half[(2 * i + part) * 2 + h] = total[:, h * 128 : (h + 1) * 128]
        for r, value in enumerate(lowered(half, 4, lines, depth)):
            straight_ref[8 + r // 2, r % 2 * 16 : r % 2 * 16 + 16] = value
        for x in range(2):
            for part in range(2):
                for h in range(2):
                    straight_ref[(2 * x + part) * 2 + h] = f_ref[
                        first_plane + x, part, :, h * 128 : (h + 1) * 128
                    ]
        other = planes - 2 - first_plane
        for x in range(2):
            across_ref[x] = f_ref[other + x]

    @pl.when(side == 0)
    def _():
        outer(-4, 0, -2)

    @pl.when(side == 1)
    def _():
        outer(planes, planes - 2, planes - 2)


def lowered(half, rows, lines, depth):
    matrix = pair_matrix(depth, depth // 2, 0.125)
    total = None
    for h in range(2):
        stacked = jnp.concatenate(
            [
                half[2 * r + h, pl.ds(0, lines // 2, 2)] + half[2 * r + h, pl.ds(1, lines // 2, 2)]
                for r in range(rows)
            ],
            axis=0,
        )
        value = dot(stacked, matrix[h * 128 : (h + 1) * 128])
        total = value if total is None else total + value
    return [total[r * lines // 2 : (r + 1) * lines // 2] for r in range(rows)]


def source_kernel(even_ref, odd_ref, straight_ref, f_ref, cs_ref, s_ref, ext, b1, half):
    position = lax.axis_index("grid")
    blocks = lax.axis_size("grid") // 4
    core, side, block = lax.rem(position, 2), lax.rem(lax.div(position, 2), 2), lax.div(position, 4)
    cosine, sine = cs_ref[core], cs_ref[2 + core]
    planes = f_ref.shape[0]
    lines, depth = f_ref.shape[2:]
    first, last = block == 0, block == blocks - 1
    low = (jnp.where(first, cosine, 1.0), jnp.where(first, -sine, 0.0))
    high = (jnp.where(last, cosine, 1.0), jnp.where(last, sine, 0.0))

    @pl.when(side == 0)
    def _():
        place_planes(ext, 0, odd_ref, *low)
        ext[planes : 2 * planes] = f_ref[...]
        ext[2 * planes : 3 * planes] = even_ref[...]
        ext[3 * planes :] = jnp.zeros((planes, 2, lines, depth), jnp.float32)

    @pl.when(side == 1)
    def _():
        ext[:planes] = jnp.zeros((planes, 2, lines, depth), jnp.float32)
        ext[planes : 2 * planes] = even_ref[...]
        ext[2 * planes : 3 * planes] = f_ref[...]
        place_planes(ext, 3 * planes, odd_ref, *high)

    for x in range(2 * planes + 4):
        for part in range(2):
            b1[x, part] = smooth_fine(lambda i, p: ext[i, p], x + planes - 2, part)
    for i in range(planes):
        for part in range(2):
            total = smooth_fine(lambda i, p: b1[i, p], 2 * i + 2, part) + smooth_fine(
                lambda i, p: b1[i, p], 2 * i + 3, part
            )
            for h in range(2):
                half[(2 * i + part) * 2 + h] = total[:, h * 128 : (h + 1) * 128]
    for r, value in enumerate(lowered(half, 2 * planes, lines, depth)):
        s_ref[r // 2, r % 2] = value

    def add(base, c, t):
        for x in range(2):
            real, imag = rotated(straight_ref[8 + x, 0:16], straight_ref[8 + x, 16:32], c, t)
            s_ref[base + x, 0] += real
            s_ref[base + x, 1] += imag

    @pl.when(side == 0)
    def _():
        add(2, *high)

    @pl.when(side == 1)
    def _():
        add(0, *low)


def fine_kernel(
    even_ref, odd_ref, straight_ref, across_ref, f_ref, cs_ref, own_ref, send_ref, ext, b1, b2, g
):
    position = lax.axis_index("grid")
    chips = lax.axis_size("grid") // 2
    core, chip = lax.rem(position, 2), lax.div(position, 2)
    cosine, sine = cs_ref[core], cs_ref[2 + core]
    planes = f_ref.shape[0]
    place_halo(ext, planes + 2, even_ref, odd_ref, cs_ref)
    ext[planes + 2 : 2 * planes + 2] = f_ref[...]
    first, last = chip < 2, chip >= chips - 2
    low = (jnp.where(first, cosine, 1.0), jnp.where(first, -sine, 0.0))
    high = (jnp.where(last, cosine, 1.0), jnp.where(last, sine, 0.0))

    def place_straight(base, c, t):
        for x in range(2):
            real, imag = [
                jnp.concatenate([straight_ref[4 * x + 2 * p], straight_ref[4 * x + 2 * p + 1]], axis=1)
                for p in range(2)
            ]
            ext[base + x, 0], ext[base + x, 1] = rotated(real, imag, c, t)

    @pl.when(lax.rem(chip, 2) == 0)
    def _():
        place_planes(ext, 0, across_ref, *low)
        place_straight(3 * planes + 2, *high)

    @pl.when(lax.rem(chip, 2) == 1)
    def _():
        place_straight(0, *low)
        place_planes(ext, 3 * planes + 2, across_ref, *high)

    for x in range(planes + 8):
        for part in range(2):
            b1[x, part] = smooth_fine(lambda i, p: ext[i, p], x + 2, part)
    for x in range(planes + 4):
        for part in range(2):
            b2[x, part] = smooth_fine(lambda i, p: b1[i, p], x + 2, part)
    for x in range(planes):
        for part in range(2):
            b3 = smooth_fine(lambda i, p: b2[i, p], x + 2, part)
            g[x, part] = fine_scale * (f_ref[x, part] + b1[x + 4, part] + b2[x + 2, part] + b3)
    half = planes // 2
    for x in range(half):
        own_ref[x] = g[core * half + x]
        send_ref[x] = g[(1 - core) * half + x]


def shift_z(v, step):
    width = v.shape[-1] // 2
    lane = lax.broadcasted_iota(jnp.int32, v.shape, len(v.shape) - 1)
    edge = 0 if step > 0 else width - 1
    inner = roll(v, step, 1)
    outer = roll(v, step + (width if step > 0 else -width), 1)
    return jnp.where(lane % width == edge, outer, inner)


def packed_sweep(values, count, depth, source, target, cosine, sine, residual=False):
    rate, near_rate = level_numbers(depth)
    values[0] = cosine * values[count] - sine * roll(values[count], 64, 1)
    values[count + 1] = cosine * values[1] + sine * roll(values[1], 64, 1)

    def body(x):
        v = values[x + 1]
        near = values[x] + values[x + 2]
        near = near + (roll(v, 1, 0) + roll(v, -1, 0))
        near = near + (shift_z(v, 1) + shift_z(v, -1))
        if residual:
            target[x] = source[x] - omega / rate * v + near_rate / rate * near
        else:
            target[x + 1] = rate * source[x] + keep * v + near_rate * near

    each(count, body)


def first_sweep(values, count, depth, source):
    rate, _ = level_numbers(depth)

    def body(x):
        values[x + 1] = rate * source[x]

    each(count, body)


def cycle_kernel(*refs):
    radix = len(refs) - 14
    pieces, refs = refs[:radix], refs[radix:]
    cs_ref, own_ref, send_ref, s, u, v, r1, s2, u2, v2, r2, s3, u3, v3 = refs
    position = lax.axis_index("grid")
    core, block = lax.rem(position, 2), lax.div(position, 4)
    count = s.shape[0]
    rate, near_rate = level_numbers(1)
    cosine, sine = cs_ref[core], cs_ref[2 + core]
    lane = lax.broadcasted_iota(jnp.int32, (8, 128), 1)
    lane_sine = jnp.where(lane < 64, -sine, sine)

    length = count // radix
    digit = lax.div(block, length // 4)
    for k, piece in enumerate(pieces):
        s[pl.ds(lax.rem(digit + k, radix) * length, length)] = piece[...]

    def sweep(values, target, residual=False):
        values[0, 0], values[0, 1] = rotated(values[count, 0], values[count, 1], cosine, -sine)
        values[count + 1, 0], values[count + 1, 1] = rotated(
            values[1, 0], values[1, 1], cosine, sine
        )

        def body(x):
            for f in range(2):
                a = values[x + 1, f]
                near = values[x, f] + values[x + 2, f]
                near = near + (roll(a, 1, 0) + roll(a, -1, 0))
                near = near + (roll(a, 1, 1) + roll(a, -1, 1))
                if residual:
                    target[x, f] = s[x, f] - omega / rate * a + near_rate / rate * near
                else:
                    target[x + 1, f] = rate * s[x, f] + keep * a + near_rate * near

        each(count, body)

    def start(x):
        for f in range(2):
            u[x + 1, f] = rate * s[x, f]

    each(count, start)
    sweep(u, v)
    sweep(v, r1, residual=True)

    count2 = count // 2
    i = lax.broadcasted_iota(jnp.int32, (128, 128), 0)
    j = lax.broadcasted_iota(jnp.int32, (128, 128), 1)
    rows = []
    for f in range(2):

        def lower(x):
            r1[2 * x, f] = r1[2 * x, f] + r1[2 * x + 1, f]
            r2[x, 8 * f : 8 * f + 8] = r1[2 * x, f, pl.ds(0, 8, 2)] + r1[2 * x, f, pl.ds(1, 8, 2)]

        each(count2, lower)
        rows.append(r2[:, 8 * f : 8 * f + 8].reshape(count2 * 8, 128))
    lowered = sum(
        dot(rows[f], jnp.where(i // 2 + 64 * f == j, 0.125, 0.0)) for f in range(2)
    )
    s2[...] = lowered.reshape(count2, 8, 128)
    first_sweep(u2, count2, 2, s2)
    packed_sweep(u2, count2, 2, s2, v2, cosine, lane_sine)
    packed_sweep(v2, count2, 2, s2, u2, cosine, lane_sine, residual=True)

    count3 = count2 // 2

    def lower3(x):
        total = u2[2 * x] + u2[2 * x + 1]
        r2[x, 0:8] = total
        r2[x, 8:16] = total
        s3[x] = r2[x, pl.ds(0, 8, 2)] + r2[x, pl.ds(1, 8, 2)]

    each(count3, lower3)
    same = i // 64 == j // 64
    lowered = dot(
        s3[...].reshape(count3 * 8, 128), jnp.where(same & (i % 64 // 2 == j % 32), 0.125, 0.0)
    )
    s3[...] = lowered.reshape(count3, 8, 128)
    first_sweep(u3, count3, 3, s3)
    a, b = u3, v3
    for _ in range(5):
        packed_sweep(a, count3, 3, s3, b, cosine, lane_sine)
        a, b = b, a

    raised = dot(
        a[1 : count3 + 1].reshape(count3 * 8, 128),
        jnp.where(same & (i % 64 == j % 64 // 2), 1.0, 0.0),
    )
    s3[...] = raised.reshape(count3, 8, 128)

    def raise3(x):
        r2[x, pl.ds(0, 8, 2)] = s3[x]
        r2[x, pl.ds(1, 8, 2)] = s3[x]
        for k in range(2):
            v2[2 * x + k + 1] = v2[2 * x + k + 1] + r2[x, 0:8]

    each(count3, raise3)
    packed_sweep(v2, count2, 2, s2, u2, cosine, lane_sine)
    packed_sweep(u2, count2, 2, s2, v2, cosine, lane_sine)

    rows = v2[1 : count2 + 1].reshape(count2 * 8, 128)
    for f in range(2):
        raised = dot(rows, jnp.where(i == j // 2 + 64 * f, 1.0, 0.0))
        s2[...] = raised.reshape(count2, 8, 128)

        def raise2(x):
            r1[x, f, pl.ds(0, 8, 2)] = s2[x]
            r1[x, f, pl.ds(1, 8, 2)] = s2[x]
            for k in range(2):
                v[2 * x + k + 1, f] = v[2 * x + k + 1, f] + r1[x, f]

        each(count2, raise2)
    sweep(v, u)
    sweep(u, v)

    for target, tile in ((own_ref, position), (send_ref, position + 1 - 2 * core)):
        for k in range(5):
            q = tile + k - 2
            low, high = q < 0, q >= count
            q = jnp.where(low, q + count, jnp.where(high, q - count, q))
            c = jnp.where(low | high, cosine, 1.0)
            t = jnp.where(low, -sine, jnp.where(high, sine, 0.0))
            target[k, 0], target[k, 1] = rotated(v[q + 1, 0], v[q + 1, 1], c, t)


def correct(w_ref, g_ref, e, b1, store):
    lines = w_ref.shape[2]
    wide = dot(w_ref[...].reshape(10 * lines, 128), spread_matrix(128, 256))
    for r in range(10):
        for h in range(2):
            value = wide[r * lines : (r + 1) * lines, 128 * h : 128 * (h + 1)]
            e[2 * r + h, pl.ds(0, lines, 2)] = value
            e[2 * r + h, pl.ds(1, lines, 2)] = value

    def expanded(x, f):
        place = (2 * (x // 2) + f) * 2
        return jnp.concatenate([e[place], e[place + 1]], axis=1)

    for x in range(6):
        for f in range(2):
            b1[x, f] = smooth_fine(expanded, x + 2, f)
    for x in range(2):
        for f in range(2):
            store(f, x, g_ref[x, f] + smooth_fine(lambda i, g: b1[i, g], x + 2, f))


def own_kernel(w_ref, g_ref, out_ref, e, b1):
    def store(part, x, value):
        out_ref[part, x] = value

    correct(w_ref, g_ref, e, b1, store)


def output_kernel(own_ref, w_ref, g_ref, out_ref, e, b1):
    core = lax.rem(lax.axis_index("grid"), 2)
    out_ref[core] = own_ref[...]

    def store(part, x, value):
        out_ref[1 - core, part, x] = value

    correct(w_ref, g_ref, e, b1, store)


def pair_phases(pair_table, k_fraction):
    kcount = k_fraction.shape[0]
    picks = pair_table[:, :, None] == jnp.arange(kcount, dtype=jnp.int32)[None, None, :]
    chosen = jnp.sum(jnp.where(picks, k_fraction[None, None, :], 0.0), axis=2)
    angle = 6.283185307179586 * (chosen[:, 0] - chosen[:, 1])
    return jnp.concatenate([jnp.cos(angle), jnp.sin(angle)])


def make_rows(moments, shapes, slot_atom):
    slot_count = shapes.shape[0]
    atom_count = moments.shape[0]
    atom_pick = (slot_atom[:, None] == jnp.arange(atom_count, dtype=jnp.int32)[None, :]).astype(
        jnp.float32
    )
    chosen = jnp.dot(atom_pick, moments.reshape(atom_count, -1), precision=highest)
    chosen = chosen.reshape(slot_count, moments.shape[1] * moments.shape[2], moments.shape[3])
    return jnp.einsum("sfl,slz->sfz", chosen, shapes, precision=highest).reshape(slot_count, -1)


def gather_blocks(value, blocks, block, permute_block):
    stride = 1
    while True:
        radix = min(4, blocks // stride)
        digit = block // stride % radix

        def towards(k):
            def target(b):
                own = b // stride % radix
                return b + ((own - k) % radix - own) * stride

            return target

        pieces = [value] + [permute_block(value, towards(k)) for k in range(1, radix)]
        stride *= radix
        if stride == blocks:
            return pieces
        stacked = jnp.roll(jnp.stack(pieces), digit, axis=0)
        value = stacked.reshape(-1, *value.shape[1:])


def vmem(count):
    return [pl.BlockSpec(memory_space=pltpu.VMEM)] * count


smem = [pl.BlockSpec(memory_space=pltpu.SMEM)]


def call(kernel, out_shape, in_specs, scratch, flops):
    single = not isinstance(out_shape, (list, tuple))
    return pl.pallas_call(
        kernel,
        out_shape=out_shape,
        in_specs=in_specs,
        out_specs=vmem(1)[0] if single else vmem(len(out_shape)),
        scratch_shapes=[pltpu.VMEM(shape, jnp.float32) for shape in scratch],
        compiler_params=pltpu.CompilerParams(vmem_limit_bytes=48 * 2**20),
        cost_estimate=pl.CostEstimate(flops=flops, bytes_accessed=2**20, transcendentals=0),
    )


def shaped(*shape):
    return jax.ShapeDtypeStruct(shape, jnp.float32)


def per_device(
    pair_density, moments, shapes, slot_atom, slot_tile, slot_row, pair_table, k_fraction
):
    tile_count = lax.axis_size("grid")
    chips, blocks = tile_count // 2, tile_count // 4
    position = lax.axis_index("grid")
    core, block = position % 2, position // 4
    _, _, thick, lines, depth = pair_density.shape
    planes = 2 * thick
    slot_count = shapes.shape[0]
    capacity = max(2, 2 * slot_count // tile_count)
    devices = range(tile_count)

    def permute(value, target):
        return lax.ppermute(value, "grid", [(i, target(i)) for i in devices])

    def permute_block(value, target):
        return permute(value, lambda i: target(i // 4) * 4 + i % 4)

    def partner(i):
        return i ^ 1

    def even_side(i):
        return i ^ 2

    def odd_side(i):
        return (i // 2 + (1 if i // 2 % 2 else -1)) % chips * 2 + i % 2

    def next_block(i):
        return (i + (4 if i // 2 % 2 else -4)) % tile_count

    cs = pair_phases(pair_table, k_fraction)

    other = permute(lax.dynamic_index_in_dim(pair_density, 1 - core, 0, False), partner)
    rows = make_rows(moments, shapes, slot_atom)
    packed = call(pack_kernel, shaped(tile_count, 8 * capacity + 8, 128), vmem(4), [], 10**8)(
        rows, slot_tile, slot_tile.reshape(1, -1), slot_row.reshape(1, -1)
    )
    received = lax.all_to_all(packed, "grid", split_axis=0, concat_axis=0, tiled=True)

    full = (2, lines, depth)
    small = (2, lines // 2, depth // 2)
    f, straight, across = call(
        density_kernel,
        [shaped(planes, *full), shaped(10, lines, 128), shaped(2, *full)],
        vmem(3),
        [(planes + 4, *full), (8, lines, 128)],
        10**8,
    )(pair_density, other, received)
    even = permute(f, even_side)
    odd = permute(f, odd_side)
    straight = permute(straight, next_block)
    across = permute(across, lambda i: (i + (-4 if i // 2 % 2 else 4)) % tile_count)
    source = call(
        source_kernel,
        shaped(planes, *small),
        vmem(4) + smem,
        [(4 * planes, *full), (2 * planes + 4, *full), (4 * planes, lines, 128)],
        10**7,
    )(even, odd, straight, f, cs)
    pieces = gather_blocks(source, blocks, block, permute_block)
    own, send = call(
        fine_kernel,
        [shaped(thick, *full)] * 2,
        vmem(5) + smem,
        [(3 * planes + 4, *full), (planes + 8, *full), (planes + 4, *full), (planes, *full)],
        10**7,
    )(even, odd, straight, across, f, cs)
    got = permute(send, partner)

    n1, n2, n3 = tile_count, tile_count // 2, tile_count // 4
    tile = (8, 128)
    w_own, w_send = call(
        cycle_kernel,
        [shaped(5, *small)] * 2,
        vmem(len(pieces)) + smem,
        [
            (n1, *small),
            (n1 + 2, *small),
            (n1 + 2, *small),
            (n1, *small),
            (n2, *tile),
            (n2 + 2, *tile),
            (n2 + 2, *tile),
            (n2, 16, 128),
            (n3, *tile),
            (n3 + 2, *tile),
            (n3 + 2, *tile),
        ],
        10**8,
    )(*pieces, cs)
    w_got = permute(w_send, partner)
    scratch = [(20, lines, 128), (6, *full)]
    result = call(own_kernel, shaped(2, thick, lines, depth), vmem(2), scratch, 10**7)(w_own, own)
    return call(output_kernel, shaped(*pair_density.shape), vmem(3), scratch, 10**7)(
        result, w_got, got
    )


def solution(mesh):
    return jax.shard_map(
        per_device,
        mesh=mesh,
        in_specs=(
            P("rep", None, "grid", None, None),
            P(("rep", "grid"), None, None, None),
            P(("rep", "grid"), None, None),
            P(("rep", "grid")),
            P(("rep", "grid"), None),
            P(("rep", "grid")),
            P(),
            P(),
        ),
        out_specs=P("rep", None, "grid", None, None),
        check_vma=False,
    )
```

```python
import jax
import jax.numpy as jnp
from jax import lax
from jax.experimental import pallas as pl
from jax.experimental.pallas import tpu as pltpu
from jax.sharding import PartitionSpec as P

omega = 0.8
screen = 0.05
highest = lax.Precision.HIGHEST

fine_diagonal = 7.5 + screen
fine_scale = omega / fine_diagonal
fine_near = fine_scale * 4.0 / 3.0
fine_far = fine_scale / 12.0
keep = 1.0 - omega


def level_numbers(depth):
    quarter = 1.0 / 4**depth
    diagonal = 6.0 * quarter + screen
    return omega / diagonal, omega / diagonal * quarter


def each(count, body, most=16):
    if count <= most:
        for i in range(count):
            body(i)
    else:
        pl.loop(0, count, unroll=4)(body)


def dot(a, b):
    return jnp.dot(a, b, precision=highest, preferred_element_type=jnp.float32)


def pair_matrix(rows, columns, value):
    i = lax.broadcasted_iota(jnp.int32, (rows, columns), 0)
    j = lax.broadcasted_iota(jnp.int32, (rows, columns), 1)
    return jnp.where(i // 2 == j, value, 0.0)


def spread_matrix(rows, columns):
    i = lax.broadcasted_iota(jnp.int32, (rows, columns), 0)
    j = lax.broadcasted_iota(jnp.int32, (rows, columns), 1)
    return jnp.where(i == j // 2, 1.0, 0.0)


def roll(v, shift, axis):
    return pltpu.roll(v, shift % v.shape[axis], axis)


def smooth_fine(at, x, f):
    total = None
    for step, weight in ((1, fine_near), (2, -fine_far)):
        sides = [p for p in (at(x - step, f), at(x + step, f)) if p is not None]
        v = at(x, f)
        if v is not None:
            for axis in (0, 1):
                sides.append(roll(v, step, axis) + roll(v, -step, axis))
            if step == 1:
                total = keep * v
        if sides:
            part = weight * sum(sides[1:], sides[0])
            total = part if total is None else total + part
    return total


def rotated(real, imag, cosine, sine):
    return cosine * real - sine * imag, sine * real + cosine * imag


def place_planes(target, base, source, cosine, sine):
    for x in range(source.shape[0]):
        real, imag = rotated(source[x, 0], source[x, 1], cosine, sine)
        target[base + x, 0] = real
        target[base + x, 1] = imag


def place_halo(ext, middle, even_ref, odd_ref, cs_ref):
    position = lax.axis_index("grid")
    chips = lax.axis_size("grid") // 2
    core, chip = lax.rem(position, 2), lax.div(position, 2)
    cosine, sine = cs_ref[core], cs_ref[2 + core]
    first, last = chip == 0, chip == chips - 1
    low = (jnp.where(first, cosine, 1.0), jnp.where(first, -sine, 0.0))
    high = (jnp.where(last, cosine, 1.0), jnp.where(last, sine, 0.0))
    planes = even_ref.shape[0]
    parity = lax.rem(chip, 2)

    @pl.when(parity == 0)
    def _():
        place_planes(ext, middle - planes, odd_ref, *low)
        place_planes(ext, middle + planes, even_ref, *high)

    @pl.when(parity == 1)
    def _():
        place_planes(ext, middle - planes, even_ref, *low)
        place_planes(ext, middle + planes, odd_ref, *high)


def pack_kernel(rows_ref, column_ref, row_ref, line_ref, out_ref):
    slots = rows_ref.shape[0]
    tiles, height, _ = out_ref.shape
    ranks = (height - 8) // 4
    capacity = ranks // 2
    buckets = tiles * capacity
    chips = tiles // 2
    position = lax.axis_index("grid")
    i = lax.broadcasted_iota(jnp.int32, (slots, slots), 0)
    j = lax.broadcasted_iota(jnp.int32, (slots, slots), 1)
    ahead = jnp.where((column_ref[...] == row_ref[...]) & (i < j), 1.0, 0.0)
    rank = jnp.sum(ahead, axis=0, keepdims=True).astype(jnp.int32)
    place = row_ref[...] * capacity + rank
    bucket = lax.broadcasted_iota(jnp.int32, (buckets, slots), 0)
    pick = bucket == place
    packed = dot(pick.astype(jnp.float32), rows_ref[...])
    for chip in range(chips):
        for p in range(2):
            for q in range(4):
                out_ref[2 * chip + p, q * ranks : (q + 1) * ranks] = packed[
                    chip * ranks : (chip + 1) * ranks, (4 * p + q) * 128 : (4 * p + q + 1) * 128
                ]
    thick_lines = 64
    line = jnp.sum(jnp.where(pick, line_ref[...] + 1, 0).astype(jnp.float32), axis=1, keepdims=True)
    own = lax.broadcasted_iota(jnp.int32, (buckets, 1), 0) // capacity % 2
    line = jnp.where(line > 0, line + (own * thick_lines).astype(jnp.float32), 0.0)
    bucket = lax.broadcasted_iota(jnp.int32, (buckets, 128), 0)
    lane = lax.broadcasted_iota(jnp.int32, (buckets, 128), 1)
    start = lax.rem(position, 128 // ranks) * ranks
    spots = jnp.where(lane - start == bucket % ranks, line, 0.0)
    i = lax.broadcasted_iota(jnp.int32, (chips, buckets), 0)
    j = lax.broadcasted_iota(jnp.int32, (chips, buckets), 1)
    numbers = dot(jnp.where(i == j // ranks, 1.0, 0.0), spots)
    for chip in range(chips):
        value = jnp.broadcast_to(numbers[chip : chip + 1], (8, 128))
        for p in range(2):
            out_ref[2 * chip + p, 4 * ranks :] = value


def density_kernel(pd_ref, other_ref, received_ref, f_ref):
    core = lax.rem(lax.axis_index("grid"), 2)
    planes, _, lines, depth = f_ref.shape
    sources, height, _ = received_ref.shape
    ranks = (height - 8) // 4
    group = 128 // ranks
    added = [None, None]
    for first in range(0, sources, group):
        count = min(group, sources - first)
        numbers = received_ref[first, 4 * ranks : 4 * ranks + 1]
        for k in range(1, count):
            numbers = numbers + received_ref[first + k, 4 * ranks : 4 * ranks + 1]
        line = lax.broadcasted_iota(jnp.int32, (planes * lines, 128), 0)
        spread = jnp.where(line == numbers.astype(jnp.int32) - 1, 1.0, 0.0)
        for part in range(2):
            values = jnp.concatenate(
                [
                    received_ref[first : first + count, q * ranks : (q + 1) * ranks].reshape(
                        count * ranks, 128
                    )
                    for q in (2 * part, 2 * part + 1)
                ],
                axis=1,
            )
            value = dot(spread[:, : count * ranks], values)
            added[part] = value if added[part] is None else added[part] + value
    for x in range(planes):
        for part in range(2):
            f_ref[x, part] = added[part][x * lines : (x + 1) * lines]
    thick = planes // 2
    for x in range(thick):
        for part in range(2):
            f_ref[core * thick + x, part] += pd_ref[core, part, x]
            f_ref[(1 - core) * thick + x, part] += other_ref[part, x]


def lowered(half, rows, lines, depth):
    matrix = pair_matrix(depth, depth // 2, 0.125)
    total = None
    for h in range(2):
        stacked = jnp.concatenate(
            [
                half[2 * r + h, pl.ds(0, lines // 2, 2)] + half[2 * r + h, pl.ds(1, lines // 2, 2)]
                for r in range(rows)
            ],
            axis=0,
        )
        value = dot(stacked, matrix[h * 128 : (h + 1) * 128])
        total = value if total is None else total + value
    return [total[r * lines // 2 : (r + 1) * lines // 2] for r in range(rows)]


def convolve(a, b):
    out = {}
    for i, x in a.items():
        for j, y in b.items():
            out[i + j] = out.get(i + j, 0.0) + x * y
    return out


along = {-2: -fine_far, -1: fine_near, 1: fine_near, 2: -fine_far}
powers = [{0: 1.0}, along, convolve(along, along)]
averaged = [convolve(power, {0: 0.5, 1: 0.5}) for power in powers]


def taps(distance, power):
    total = jnp.zeros(distance.shape, jnp.float32)
    for offset, value in averaged[power].items():
        total = jnp.where(distance == offset, value, total)
    return total


def coarse_kernel(
    rows_ref, tile_ref, line_ref, pd_ref, cs_ref, keep_ref, send_ref, ext, weights, b1, half
):
    position = lax.axis_index("grid")
    core = lax.rem(position, 2)
    slots = rows_ref.shape[0]
    count = keep_ref.shape[0]
    thick, lines, depth = pd_ref.shape[2:]
    small_lines, small_depth = lines // 2, depth // 2
    total = count + 4

    i = lax.broadcasted_iota(jnp.int32, (depth, small_depth), 0)
    j = lax.broadcasted_iota(jnp.int32, (depth, small_depth), 1)
    distance = lax.rem(i - 2 * j + depth + depth // 2, depth) - depth // 2
    matrix = jnp.concatenate([taps(distance, power) for power in range(3)], axis=1)
    stacked = jnp.concatenate(
        [rows_ref[:, f * depth : (f + 1) * depth] for f in range(4)], axis=0
    )
    cells = dot(stacked, matrix)
    values = [
        jnp.concatenate(
            [
                cells[f * slots : (f + 1) * slots, k * small_depth : (k + 1) * small_depth]
                for f in range(4)
            ],
            axis=1,
        )
        for k in range(3)
    ]

    plane = tile_ref[...] * thick + line_ref[...] // lines
    line = line_ref[...] % lines
    i = lax.broadcasted_iota(jnp.int32, (weights.shape[1], slots), 0)
    for power in range(3):
        weights[power] = taps(plane - 2 * (i - 2), power)
    j = lax.broadcasted_iota(jnp.int32, (small_lines, slots), 0)
    distance = lax.rem(line - 2 * j + lines + lines // 2, lines) - lines // 2
    q = [taps(distance, power) for power in range(3)]
    mixed = [keep * keep * q[0] + 2.0 * keep * q[1] + q[2], 2.0 * keep * q[0] + 2.0 * q[1], q[0]]
    chunk = total if total <= 20 else 12

    def body(first):
        parts = [[], [], []]
        for k in range(chunk):
            p = [weights[power, pl.ds(first * chunk + k, 1)] for power in range(3)]
            parts[0].append(p[0] * mixed[0] + p[1] * mixed[1] + p[2] * mixed[2])
            parts[1].append(p[0] * mixed[1] + 2.0 * p[1] * mixed[2])
            parts[2].append(p[0] * mixed[2])
        out = sum(dot(jnp.concatenate(parts[k], axis=0), values[k]) for k in range(3))
        for k in range(chunk):
            for f in range(4):
                ext[first * chunk + k, f] = out[
                    k * small_lines : (k + 1) * small_lines,
                    f * small_depth : (f + 1) * small_depth,
                ]

    each(total // chunk, body, 1)

    def tile(x, f):
        return pd_ref[f // 2, f % 2, x] if 0 <= x < thick else None

    def once(x, f):
        return b1[x + 2, f] if -2 <= x < thick + 2 else None

    for x in range(-2, thick + 2):
        for f in range(4):
            b1[x + 2, f] = smooth_fine(tile, x, f)
    for i in range(5):
        for f in range(4):
            both = smooth_fine(once, 2 * i - 4, f) + smooth_fine(once, 2 * i - 3, f)
            for h in range(2):
                half[(4 * i + f) * 2 + h] = both[:, h * 128 : (h + 1) * 128]
    for r, value in enumerate(lowered(half, 20, lines, depth)):
        ext[position + r // 4, r % 4] += value

    for p in range(2):
        cosine, sine = cs_ref[p], cs_ref[2 + p]
        for k in range(2):
            for source, target, sign in ((k, count + k, sine), (count + 2 + k, 2 + k, -sine)):
                real, imag = rotated(ext[source, 2 * p], ext[source, 2 * p + 1], cosine, sign)
                ext[target, 2 * p] += real
                ext[target, 2 * p + 1] += imag

    def deliver(x):
        for part in range(2):
            keep_ref[x, part] = ext[x + 2, 2 * core + part]
            send_ref[x, part] = ext[x + 2, 2 * (1 - core) + part]

    each(count, deliver)


def fine_kernel(
    even_ref, odd_ref, after_ref, before_ref, f_ref, cs_ref, own_ref, send_ref, ext, b1, b2, g
):
    position = lax.axis_index("grid")
    chips = lax.axis_size("grid") // 2
    core, chip = lax.rem(position, 2), lax.div(position, 2)
    cosine, sine = cs_ref[core], cs_ref[2 + core]
    planes = f_ref.shape[0]
    place_halo(ext, planes + 2, even_ref, odd_ref, cs_ref)
    ext[planes + 2 : 2 * planes + 2] = f_ref[...]
    first, last = chip < 2, chip >= chips - 2
    place_planes(
        ext, 0, before_ref, jnp.where(first, cosine, 1.0), jnp.where(first, -sine, 0.0)
    )
    place_planes(
        ext,
        3 * planes + 2,
        after_ref,
        jnp.where(last, cosine, 1.0),
        jnp.where(last, sine, 0.0),
    )
    for x in range(planes + 8):
        for part in range(2):
            b1[x, part] = smooth_fine(lambda i, p: ext[i, p], x + 2, part)
    for x in range(planes + 4):
        for part in range(2):
            b2[x, part] = smooth_fine(lambda i, p: b1[i, p], x + 2, part)
    for x in range(planes):
        for part in range(2):
            b3 = smooth_fine(lambda i, p: b2[i, p], x + 2, part)
            g[x, part] = fine_scale * (f_ref[x, part] + b1[x + 4, part] + b2[x + 2, part] + b3)
    half = planes // 2
    for x in range(half):
        own_ref[x] = g[core * half + x]
        send_ref[x] = g[(1 - core) * half + x]


def shift_z(v, step):
    width = v.shape[-1] // 2
    lane = lax.broadcasted_iota(jnp.int32, v.shape, len(v.shape) - 1)
    edge = 0 if step > 0 else width - 1
    inner = roll(v, step, 1)
    outer = roll(v, step + (width if step > 0 else -width), 1)
    return jnp.where(lane % width == edge, outer, inner)


def packed_sweep(values, count, depth, source, target, cosine, sine, residual=False):
    rate, near_rate = level_numbers(depth)
    values[0] = cosine * values[count] - sine * roll(values[count], 64, 1)
    values[count + 1] = cosine * values[1] + sine * roll(values[1], 64, 1)

    def body(x):
        v = values[x + 1]
        near = values[x] + values[x + 2]
        near = near + (roll(v, 1, 0) + roll(v, -1, 0))
        near = near + (shift_z(v, 1) + shift_z(v, -1))
        if residual:
            target[x] = source[x] - omega / rate * v + near_rate / rate * near
        else:
            target[x + 1] = rate * source[x] + keep * v + near_rate * near

    each(count, body)


def first_sweep(values, count, depth, source):
    rate, _ = level_numbers(depth)

    def body(x):
        values[x + 1] = rate * source[x]

    each(count, body)


def cycle_kernel(*refs):
    radix = len(refs) - 14
    pieces, refs = refs[:radix], refs[radix:]
    cs_ref, own_ref, send_ref, s, u, v, r1, s2, u2, v2, r2, s3, u3, v3 = refs
    position = lax.axis_index("grid")
    core, block = lax.rem(position, 2), lax.div(position, 4)
    count = s.shape[0]
    rate, near_rate = level_numbers(1)
    cosine, sine = cs_ref[core], cs_ref[2 + core]
    lane = lax.broadcasted_iota(jnp.int32, (8, 128), 1)
    lane_sine = jnp.where(lane < 64, -sine, sine)

    length = count // radix
    digit = lax.div(block, length // 4)
    for k, piece in enumerate(pieces):
        s[pl.ds(lax.rem(digit + k, radix) * length, length)] = piece[...]

    def sweep(values, target, residual=False):
        values[0, 0], values[0, 1] = rotated(values[count, 0], values[count, 1], cosine, -sine)
        values[count + 1, 0], values[count + 1, 1] = rotated(
            values[1, 0], values[1, 1], cosine, sine
        )

        def body(x):
            for f in range(2):
                a = values[x + 1, f]
                near = values[x, f] + values[x + 2, f]
                near = near + (roll(a, 1, 0) + roll(a, -1, 0))
                near = near + (roll(a, 1, 1) + roll(a, -1, 1))
                if residual:
                    target[x, f] = s[x, f] - omega / rate * a + near_rate / rate * near
                else:
                    target[x + 1, f] = rate * s[x, f] + keep * a + near_rate * near

        each(count, body)

    def start(x):
        for f in range(2):
            u[x + 1, f] = rate * s[x, f]

    each(count, start)
    sweep(u, v)
    sweep(v, r1, residual=True)

    count2 = count // 2
    i = lax.broadcasted_iota(jnp.int32, (128, 128), 0)
    j = lax.broadcasted_iota(jnp.int32, (128, 128), 1)
    rows = []
    for f in range(2):

        def lower(x):
            r1[2 * x, f] = r1[2 * x, f] + r1[2 * x + 1, f]
            r2[x, 8 * f : 8 * f + 8] = r1[2 * x, f, pl.ds(0, 8, 2)] + r1[2 * x, f, pl.ds(1, 8, 2)]

        each(count2, lower)
        rows.append(r2[:, 8 * f : 8 * f + 8].reshape(count2 * 8, 128))
    lowered = sum(
        dot(rows[f], jnp.where(i // 2 + 64 * f == j, 0.125, 0.0)) for f in range(2)
    )
    s2[...] = lowered.reshape(count2, 8, 128)
    first_sweep(u2, count2, 2, s2)
    packed_sweep(u2, count2, 2, s2, v2, cosine, lane_sine)
    packed_sweep(v2, count2, 2, s2, u2, cosine, lane_sine, residual=True)

    count3 = count2 // 2

    def lower3(x):
        total = u2[2 * x] + u2[2 * x + 1]
        r2[x, 0:8] = total
        r2[x, 8:16] = total
        s3[x] = r2[x, pl.ds(0, 8, 2)] + r2[x, pl.ds(1, 8, 2)]

    each(count3, lower3)
    same = i // 64 == j // 64
    lowered = dot(
        s3[...].reshape(count3 * 8, 128), jnp.where(same & (i % 64 // 2 == j % 32), 0.125, 0.0)
    )
    s3[...] = lowered.reshape(count3, 8, 128)
    first_sweep(u3, count3, 3, s3)
    a, b = u3, v3
    for _ in range(5):
        packed_sweep(a, count3, 3, s3, b, cosine, lane_sine)
        a, b = b, a

    raised = dot(
        a[1 : count3 + 1].reshape(count3 * 8, 128),
        jnp.where(same & (i % 64 == j % 64 // 2), 1.0, 0.0),
    )
    s3[...] = raised.reshape(count3, 8, 128)

    def raise3(x):
        r2[x, pl.ds(0, 8, 2)] = s3[x]
        r2[x, pl.ds(1, 8, 2)] = s3[x]
        for k in range(2):
            v2[2 * x + k + 1] = v2[2 * x + k + 1] + r2[x, 0:8]

    each(count3, raise3)
    packed_sweep(v2, count2, 2, s2, u2, cosine, lane_sine)
    packed_sweep(u2, count2, 2, s2, v2, cosine, lane_sine)

    rows = v2[1 : count2 + 1].reshape(count2 * 8, 128)
    for f in range(2):
        raised = dot(rows, jnp.where(i == j // 2 + 64 * f, 1.0, 0.0))
        s2[...] = raised.reshape(count2, 8, 128)

        def raise2(x):
            r1[x, f, pl.ds(0, 8, 2)] = s2[x]
            r1[x, f, pl.ds(1, 8, 2)] = s2[x]
            for k in range(2):
                v[2 * x + k + 1, f] = v[2 * x + k + 1, f] + r1[x, f]

        each(count2, raise2)
    sweep(v, u)
    sweep(u, v)

    for target, tile in ((own_ref, position), (send_ref, position + 1 - 2 * core)):
        for k in range(5):
            q = tile + k - 2
            low, high = q < 0, q >= count
            q = jnp.where(low, q + count, jnp.where(high, q - count, q))
            c = jnp.where(low | high, cosine, 1.0)
            t = jnp.where(low, -sine, jnp.where(high, sine, 0.0))
            target[k, 0], target[k, 1] = rotated(v[q + 1, 0], v[q + 1, 1], c, t)


def correct(w_ref, g_ref, e, b1, store):
    lines = w_ref.shape[2]
    wide = dot(w_ref[...].reshape(10 * lines, 128), spread_matrix(128, 256))
    for r in range(10):
        for h in range(2):
            value = wide[r * lines : (r + 1) * lines, 128 * h : 128 * (h + 1)]
            e[2 * r + h, pl.ds(0, lines, 2)] = value
            e[2 * r + h, pl.ds(1, lines, 2)] = value

    def expanded(x, f):
        place = (2 * (x // 2) + f) * 2
        return jnp.concatenate([e[place], e[place + 1]], axis=1)

    for x in range(6):
        for f in range(2):
            b1[x, f] = smooth_fine(expanded, x + 2, f)
    for x in range(2):
        for f in range(2):
            store(f, x, g_ref[x, f] + smooth_fine(lambda i, g: b1[i, g], x + 2, f))


def own_kernel(w_ref, g_ref, out_ref, e, b1):
    def store(part, x, value):
        out_ref[part, x] = value

    correct(w_ref, g_ref, e, b1, store)


def output_kernel(own_ref, w_ref, g_ref, out_ref, e, b1):
    core = lax.rem(lax.axis_index("grid"), 2)
    out_ref[core] = own_ref[...]

    def store(part, x, value):
        out_ref[1 - core, part, x] = value

    correct(w_ref, g_ref, e, b1, store)


def pair_phases(pair_table, k_fraction):
    kcount = k_fraction.shape[0]
    picks = pair_table[:, :, None] == jnp.arange(kcount, dtype=jnp.int32)[None, None, :]
    chosen = jnp.sum(jnp.where(picks, k_fraction[None, None, :], 0.0), axis=2)
    angle = 6.283185307179586 * (chosen[:, 0] - chosen[:, 1])
    return jnp.concatenate([jnp.cos(angle), jnp.sin(angle)])


def make_rows(moments, shapes, slot_atom):
    slot_count = shapes.shape[0]
    atom_count = moments.shape[0]
    atom_pick = (slot_atom[:, None] == jnp.arange(atom_count, dtype=jnp.int32)[None, :]).astype(
        jnp.float32
    )
    chosen = jnp.dot(atom_pick, moments.reshape(atom_count, -1), precision=highest)
    chosen = chosen.reshape(slot_count, moments.shape[1] * moments.shape[2], moments.shape[3])
    return jnp.einsum("sfl,slz->sfz", chosen, shapes, precision=highest).reshape(slot_count, -1)


def block_steps(blocks):
    steps, stride = [], 1
    while stride < blocks:
        steps.append((stride, min(4, blocks // stride)))
        stride *= steps[-1][1]
    return steps


def further(k, stride, radix):
    def target(b):
        digit = b // stride % radix
        return b + ((digit + k) % radix - digit) * stride

    return target


def scatter_blocks(value, blocks, block, permute_block):
    for stride, radix in reversed(block_steps(blocks)):
        parts = value.reshape(radix, -1, *value.shape[1:])
        digit = block // stride % radix
        pieces = [
            lax.dynamic_index_in_dim(parts, (digit + k) % radix, 0, False) for k in range(radix)
        ]
        value = sum(
            [permute_block(pieces[k], further(k, stride, radix)) for k in range(1, radix)],
            pieces[0],
        )
    return value


def gather_blocks(value, blocks, block, permute_block):
    steps = block_steps(blocks)
    for stride, radix in steps:
        pieces = [value] + [
            permute_block(value, further(-k, stride, radix)) for k in range(1, radix)
        ]
        if (stride, radix) == steps[-1]:
            return pieces
        stacked = jnp.roll(jnp.stack(pieces), block // stride % radix, axis=0)
        value = stacked.reshape(-1, *value.shape[1:])


def vmem(count):
    return [pl.BlockSpec(memory_space=pltpu.VMEM)] * count


smem = [pl.BlockSpec(memory_space=pltpu.SMEM)]


def call(kernel, out_shape, in_specs, scratch, flops):
    single = not isinstance(out_shape, (list, tuple))
    return pl.pallas_call(
        kernel,
        out_shape=out_shape,
        in_specs=in_specs,
        out_specs=vmem(1)[0] if single else vmem(len(out_shape)),
        scratch_shapes=[pltpu.VMEM(shape, jnp.float32) for shape in scratch],
        compiler_params=pltpu.CompilerParams(vmem_limit_bytes=48 * 2**20),
        cost_estimate=pl.CostEstimate(flops=flops, bytes_accessed=2**20, transcendentals=0),
    )


def shaped(*shape):
    return jax.ShapeDtypeStruct(shape, jnp.float32)


def per_device(
    pair_density, moments, shapes, slot_atom, slot_tile, slot_row, pair_table, k_fraction
):
    tile_count = lax.axis_size("grid")
    chips, blocks = tile_count // 2, tile_count // 4
    position = lax.axis_index("grid")
    core, block = position % 2, position // 4
    _, _, thick, lines, depth = pair_density.shape
    planes = 2 * thick
    slot_count = shapes.shape[0]
    capacity = max(2, 2 * slot_count // tile_count)
    devices = range(tile_count)

    def permute(value, target):
        return lax.ppermute(value, "grid", [(i, target(i)) for i in devices])

    def permute_block(value, target):
        return permute(value, lambda i: target(i // 4) * 4 + i % 4)

    def partner(i):
        return i ^ 1

    def even_side(i):
        return i ^ 2

    def odd_side(i):
        return (i // 2 + (1 if i // 2 % 2 else -1)) % chips * 2 + i % 2

    cs = pair_phases(pair_table, k_fraction)

    other = permute(lax.dynamic_index_in_dim(pair_density, 1 - core, 0, False), partner)
    rows = make_rows(moments, shapes, slot_atom)
    tile_row, line_row = slot_tile.reshape(1, -1), slot_row.reshape(1, -1)
    packed = call(pack_kernel, shaped(tile_count, 8 * capacity + 8, 128), vmem(4), [], 10**8)(
        rows, slot_tile, tile_row, line_row
    )
    received = lax.all_to_all(packed, "grid", split_axis=0, concat_axis=0, tiled=True)

    full = (2, lines, depth)
    small = (2, lines // 2, depth // 2)
    kept, sent = call(
        coarse_kernel,
        [shaped(tile_count, *small)] * 2,
        vmem(4) + smem,
        [
            (tile_count + 4, 4, lines // 2, depth // 2),
            (3, (tile_count + 11) // 8 * 8, slot_count),
            (thick + 4, 4, lines, depth),
            (40, lines, 128),
        ],
        10**8,
    )(rows, tile_row, line_row, pair_density, cs)
    kept = kept + permute(sent, partner)
    kept = kept + permute(kept, even_side)
    source = scatter_blocks(kept, blocks, block, permute_block)
    pieces = gather_blocks(source, blocks, block, permute_block)

    f = call(density_kernel, shaped(planes, *full), vmem(3), [], 10**7)(
        pair_density, other, received
    )
    even = permute(f, even_side)
    odd = permute(f, odd_side)
    after = permute(f[:thick], lambda i: (i - 4) % tile_count)
    before = permute(f[thick:], lambda i: (i + 4) % tile_count)
    own, send = call(
        fine_kernel,
        [shaped(thick, *full)] * 2,
        vmem(5) + smem,
        [(3 * planes + 4, *full), (planes + 8, *full), (planes + 4, *full), (planes, *full)],
        10**7,
    )(even, odd, after, before, f, cs)
    got = permute(send, partner)

    n1, n2, n3 = tile_count, tile_count // 2, tile_count // 4
    tile = (8, 128)
    w_own, w_send = call(
        cycle_kernel,
        [shaped(5, *small)] * 2,
        vmem(len(pieces)) + smem,
        [
            (n1, *small),
            (n1 + 2, *small),
            (n1 + 2, *small),
            (n1, *small),
            (n2, *tile),
            (n2 + 2, *tile),
            (n2 + 2, *tile),
            (n2, 16, 128),
            (n3, *tile),
            (n3 + 2, *tile),
            (n3 + 2, *tile),
        ],
        10**8,
    )(*pieces, cs)
    w_got = permute(w_send, partner)
    scratch = [(20, lines, 128), (6, *full)]
    result = call(own_kernel, shaped(2, thick, lines, depth), vmem(2), scratch, 10**7)(w_own, own)
    return call(output_kernel, shaped(*pair_density.shape), vmem(3), scratch, 10**7)(
        result, w_got, got
    )


def solution(mesh):
    return jax.shard_map(
        per_device,
        mesh=mesh,
        in_specs=(
            P("rep", None, "grid", None, None),
            P(("rep", "grid"), None, None, None),
            P(("rep", "grid"), None, None),
            P(("rep", "grid")),
            P(("rep", "grid"), None),
            P(("rep", "grid")),
            P(),
            P(),
        ),
        out_specs=P("rep", None, "grid", None, None),
        check_vma=False,
    )
```

```python
import jax
import jax.numpy as jnp
from jax import lax
from jax.experimental import pallas as pl
from jax.experimental.pallas import tpu as pltpu
from jax.sharding import PartitionSpec as P

omega = 0.8
screen = 0.05
highest = lax.Precision.HIGHEST

fine_diagonal = 7.5 + screen
fine_scale = omega / fine_diagonal
fine_near = fine_scale * 4.0 / 3.0
fine_far = fine_scale / 12.0
keep = 1.0 - omega


def level_numbers(depth):
    quarter = 1.0 / 4**depth
    diagonal = 6.0 * quarter + screen
    return omega / diagonal, omega / diagonal * quarter


def each(count, body, most=16):
    if count <= most:
        for i in range(count):
            body(i)
    else:
        pl.loop(0, count, unroll=4)(body)


def dot(a, b):
    return jnp.dot(a, b, precision=highest, preferred_element_type=jnp.float32)


def pair_matrix(rows, columns, value):
    i = lax.broadcasted_iota(jnp.int32, (rows, columns), 0)
    j = lax.broadcasted_iota(jnp.int32, (rows, columns), 1)
    return jnp.where(i // 2 == j, value, 0.0)


def spread_matrix(rows, columns):
    i = lax.broadcasted_iota(jnp.int32, (rows, columns), 0)
    j = lax.broadcasted_iota(jnp.int32, (rows, columns), 1)
    return jnp.where(i == j // 2, 1.0, 0.0)


def roll(v, shift, axis):
    return pltpu.roll(v, shift % v.shape[axis], axis)


def smooth_fine(at, x, f):
    total = None
    for step, weight in ((1, fine_near), (2, -fine_far)):
        sides = [p for p in (at(x - step, f), at(x + step, f)) if p is not None]
        v = at(x, f)
        if v is not None:
            for axis in (0, 1):
                sides.append(roll(v, step, axis) + roll(v, -step, axis))
            if step == 1:
                total = keep * v
        if sides:
            part = weight * sum(sides[1:], sides[0])
            total = part if total is None else total + part
    return total


def rotated(real, imag, cosine, sine):
    return cosine * real - sine * imag, sine * real + cosine * imag


def place_planes(target, base, source, cosine, sine):
    for x in range(source.shape[0]):
        real, imag = rotated(source[x, 0], source[x, 1], cosine, sine)
        target[base + x, 0] = real
        target[base + x, 1] = imag


def place_halo(ext, middle, even_ref, odd_ref, cs_ref):
    position = lax.axis_index("grid")
    chips = lax.axis_size("grid") // 2
    core, chip = lax.rem(position, 2), lax.div(position, 2)
    cosine, sine = cs_ref[core], cs_ref[2 + core]
    first, last = chip == 0, chip == chips - 1
    low = (jnp.where(first, cosine, 1.0), jnp.where(first, -sine, 0.0))
    high = (jnp.where(last, cosine, 1.0), jnp.where(last, sine, 0.0))
    planes = even_ref.shape[0]
    parity = lax.rem(chip, 2)

    @pl.when(parity == 0)
    def _():
        place_planes(ext, middle - planes, odd_ref, *low)
        place_planes(ext, middle + planes, even_ref, *high)

    @pl.when(parity == 1)
    def _():
        place_planes(ext, middle - planes, even_ref, *low)
        place_planes(ext, middle + planes, odd_ref, *high)


def as_column(row):
    n = row.shape[1]
    i = lax.broadcasted_iota(jnp.int32, (n, n), 0)
    j = lax.broadcasted_iota(jnp.int32, (n, n), 1)
    return jnp.sum(jnp.where(i == j, row, 0.0), axis=1, keepdims=True)


def rows_kernel(moments_ref, shapes_ref, atom_ref, tile_ref, line_ref, keep_ref, send_ref, rows):
    core = lax.rem(lax.axis_index("grid"), 2)
    slots, channels, depth = shapes_ref.shape
    atoms = moments_ref.shape[0]
    atom = as_column(atom_ref[...].astype(jnp.float32))
    picks = [jnp.where(atom == float(a), 1.0, 0.0) for a in range(atoms)]
    chosen = []
    for f in range(4):
        total = None
        for a in range(atoms):
            value = picks[a] * moments_ref[a, f // 2, f % 2 : f % 2 + 1]
            total = value if total is None else total + value
        chosen.append(total)
    for i in range(slots // 8):
        near = slice(8 * i, 8 * i + 8)
        totals = [None] * 4
        for channel in range(channels):
            shape = shapes_ref[near, channel]
            for f in range(4):
                value = chosen[f][near, channel : channel + 1] * shape
                totals[f] = value if totals[f] is None else totals[f] + value
        for f in range(4):
            rows[f // 2, near, f % 2 * depth : (f % 2 + 1) * depth] = totals[f]
    keep_ref[...] = rows[core]
    send_ref[0:slots] = rows[1 - core]
    send_ref[slots:] = jnp.zeros((8, 2 * depth), jnp.float32)
    number = (tile_ref[...] * 64 + line_ref[...]).astype(jnp.float32)
    send_ref[slots : slots + 1, 0:slots] = number


def pack_kernel(own_ref, got_ref, tile_ref, line_ref, *out_refs):
    slots = own_ref.shape[0]
    apart = len(out_refs) > 1
    height = out_refs[0].shape[-2]
    ranks = (height - 8) // 4
    capacity = ranks // 4
    chips = lax.axis_size("grid") // 2
    chip = lax.div(lax.axis_index("grid"), 2)
    number = (tile_ref[...] * 64 + line_ref[...]).astype(jnp.float32)
    number = jnp.concatenate([number, got_ref[slots : slots + 1, 0:slots]], axis=1).astype(jnp.int32)
    tile, line = number // 64, number % 128 + 1
    column = as_column(tile.astype(jnp.float32)).astype(jnp.int32)
    i = lax.broadcasted_iota(jnp.int32, (2 * slots, 2 * slots), 0)
    j = lax.broadcasted_iota(jnp.int32, (2 * slots, 2 * slots), 1)
    ahead = jnp.where((column == tile) & (i < j) & (i // slots == j // slots), 1.0, 0.0)
    rank = jnp.sum(ahead, axis=0, keepdims=True).astype(jnp.int32)
    device = lax.broadcasted_iota(jnp.int32, (1, 2 * slots), 1) // slots
    place = tile // 2 * ranks + (2 * device + tile % 2) * capacity + rank
    r = lax.broadcasted_iota(jnp.int32, (ranks, 2 * slots), 0)
    targets = [lax.bitwise_xor(chip, k) if apart else k for k in range(chips)]
    pick = jnp.concatenate([jnp.where(place == r + target * ranks, 1.0, 0.0) for target in targets])
    rows = jnp.concatenate([own_ref[...], got_ref[0:slots]], axis=0)
    packed = dot(pick, rows)
    lines = jnp.sum(pick * line.astype(jnp.float32), axis=1, keepdims=True)
    bucket = lax.broadcasted_iota(jnp.int32, (chips * ranks, 128), 0)
    lane = lax.broadcasted_iota(jnp.int32, (chips * ranks, 128), 1)
    spot = bucket // ranks if apart else chip
    spots = jnp.where(lane == spot % (128 // ranks) * ranks + bucket % ranks, lines, 0.0)
    i = lax.broadcasted_iota(jnp.int32, (chips, chips * ranks), 0)
    j = lax.broadcasted_iota(jnp.int32, (chips, chips * ranks), 1)
    numbers = dot(jnp.where(i == j // ranks, 1.0, 0.0), spots)
    for k in range(chips):
        out = out_refs[k] if apart else out_refs[0].at[k]
        for q in range(4):
            out[q * ranks : (q + 1) * ranks] = packed[
                k * ranks : (k + 1) * ranks, q * 128 : (q + 1) * 128
            ]
        out[4 * ranks :] = jnp.broadcast_to(numbers[k : k + 1], (8, 128))


def density_kernel(*refs):
    pd_ref, other_ref = refs[:2]
    f_ref, straight_ref, across_ref, b1, half = refs[-5:]
    pieces = refs[2:-5]
    position = lax.axis_index("grid")
    core, side = lax.rem(position, 2), lax.rem(lax.div(position, 2), 2)
    planes, _, lines, depth = f_ref.shape
    sources = lax.axis_size("grid") // 2
    height = pieces[0].shape[-2]
    ranks = (height - 8) // 4
    group = 128 // ranks

    def received(source, start, stop):
        if len(pieces) > 1:
            return pieces[source][start:stop]
        return pieces[0][source, start:stop]

    added = [None, None]
    for first in range(0, sources, group):
        members = range(first, min(first + group, sources))
        numbers = sum(received(k, 4 * ranks, 4 * ranks + 1) for k in members)
        line = lax.broadcasted_iota(jnp.int32, (planes * lines, 128), 0)
        spread = jnp.where(line == numbers.astype(jnp.int32) - 1, 1.0, 0.0)
        for part in range(2):
            values = jnp.concatenate(
                [
                    jnp.concatenate(
                        [received(k, q * ranks, (q + 1) * ranks) for k in members], axis=0
                    )
                    for q in (2 * part, 2 * part + 1)
                ],
                axis=1,
            )
            value = dot(spread[:, : len(members) * ranks], values)
            added[part] = value if added[part] is None else added[part] + value
    for x in range(planes):
        for part in range(2):
            f_ref[x, part] = added[part][x * lines : (x + 1) * lines]
    thick = planes // 2
    for x in range(thick):
        for part in range(2):
            f_ref[core * thick + x, part] += pd_ref[core, part, x]
            f_ref[(1 - core) * thick + x, part] += other_ref[part, x]

    def density(x, part):
        return f_ref[x, part] if 0 <= x < planes else None

    def once(x, part):
        return b1[x + 2, part] if -2 <= x < planes + 2 else None

    def outer(base, first_plane, one):
        for x in range(one, one + 4):
            for part in range(2):
                b1[x + 2, part] = smooth_fine(density, x, part)
        for i in range(2):
            for part in range(2):
                x = base + 2 * i
                total = smooth_fine(once, x, part) + smooth_fine(once, x + 1, part)
                for h in range(2):
                    half[(2 * i + part) * 2 + h] = total[:, h * 128 : (h + 1) * 128]
        for r, value in enumerate(lowered(half, 4, lines, depth)):
            straight_ref[8 + r // 2, r % 2 * 16 : r % 2 * 16 + 16] = value
        for x in range(2):
            for part in range(2):
                for h in range(2):
                    straight_ref[(2 * x + part) * 2 + h] = f_ref[
                        first_plane + x, part, :, h * 128 : (h + 1) * 128
                    ]
        other = planes - 2 - first_plane
        for x in range(2):
            across_ref[x] = f_ref[other + x]

    @pl.when(side == 0)
    def _():
        outer(-4, 0, -2)

    @pl.when(side == 1)
    def _():
        outer(planes, planes - 2, planes - 2)


def lowered(half, rows, lines, depth):
    matrix = pair_matrix(depth, depth // 2, 0.125)
    total = None
    for h in range(2):
        stacked = jnp.concatenate(
            [
                half[2 * r + h, pl.ds(0, lines // 2, 2)] + half[2 * r + h, pl.ds(1, lines // 2, 2)]
                for r in range(rows)
            ],
            axis=0,
        )
        value = dot(stacked, matrix[h * 128 : (h + 1) * 128])
        total = value if total is None else total + value
    return [total[r * lines // 2 : (r + 1) * lines // 2] for r in range(rows)]


def source_kernel(even_ref, odd_ref, straight_ref, f_ref, cs_ref, s_ref, ext, b1, half):
    position = lax.axis_index("grid")
    blocks = lax.axis_size("grid") // 4
    core, side, block = lax.rem(position, 2), lax.rem(lax.div(position, 2), 2), lax.div(position, 4)
    cosine, sine = cs_ref[core], cs_ref[2 + core]
    planes = f_ref.shape[0]
    lines, depth = f_ref.shape[2:]
    first, last = block == 0, block == blocks - 1
    low = (jnp.where(first, cosine, 1.0), jnp.where(first, -sine, 0.0))
    high = (jnp.where(last, cosine, 1.0), jnp.where(last, sine, 0.0))

    @pl.when(side == 0)
    def _():
        place_planes(ext, 0, odd_ref, *low)
        ext[planes : 2 * planes] = f_ref[...]
        ext[2 * planes : 3 * planes] = even_ref[...]
        ext[3 * planes :] = jnp.zeros((planes, 2, lines, depth), jnp.float32)

    @pl.when(side == 1)
    def _():
        ext[:planes] = jnp.zeros((planes, 2, lines, depth), jnp.float32)
        ext[planes : 2 * planes] = even_ref[...]
        ext[2 * planes : 3 * planes] = f_ref[...]
        place_planes(ext, 3 * planes, odd_ref, *high)

    for x in range(2 * planes + 4):
        for part in range(2):
            b1[x, part] = smooth_fine(lambda i, p: ext[i, p], x + planes - 2, part)
    for i in range(planes):
        for part in range(2):
            total = smooth_fine(lambda i, p: b1[i, p], 2 * i + 2, part) + smooth_fine(
                lambda i, p: b1[i, p], 2 * i + 3, part
            )
            for h in range(2):
                half[(2 * i + part) * 2 + h] = total[:, h * 128 : (h + 1) * 128]
    for r, value in enumerate(lowered(half, 2 * planes, lines, depth)):
        s_ref[r // 2, r % 2] = value

    def add(base, c, t):
        for x in range(2):
            real, imag = rotated(straight_ref[8 + x, 0:16], straight_ref[8 + x, 16:32], c, t)
            s_ref[base + x, 0] += real
            s_ref[base + x, 1] += imag

    @pl.when(side == 0)
    def _():
        add(2, *high)

    @pl.when(side == 1)
    def _():
        add(0, *low)


def fine_kernel(
    even_ref, odd_ref, straight_ref, across_ref, f_ref, cs_ref, own_ref, send_ref, ext, b1, b2, g
):
    position = lax.axis_index("grid")
    chips = lax.axis_size("grid") // 2
    core, chip = lax.rem(position, 2), lax.div(position, 2)
    cosine, sine = cs_ref[core], cs_ref[2 + core]
    planes = f_ref.shape[0]
    place_halo(ext, planes + 2, even_ref, odd_ref, cs_ref)
    ext[planes + 2 : 2 * planes + 2] = f_ref[...]
    first, last = chip < 2, chip >= chips - 2
    low = (jnp.where(first, cosine, 1.0), jnp.where(first, -sine, 0.0))
    high = (jnp.where(last, cosine, 1.0), jnp.where(last, sine, 0.0))

    def place_straight(base, c, t):
        for x in range(2):
            real, imag = [
                jnp.concatenate([straight_ref[4 * x + 2 * p], straight_ref[4 * x + 2 * p + 1]], axis=1)
                for p in range(2)
            ]
            ext[base + x, 0], ext[base + x, 1] = rotated(real, imag, c, t)

    @pl.when(lax.rem(chip, 2) == 0)
    def _():
        place_planes(ext, 0, across_ref, *low)
        place_straight(3 * planes + 2, *high)

    @pl.when(lax.rem(chip, 2) == 1)
    def _():
        place_straight(0, *low)
        place_planes(ext, 3 * planes + 2, across_ref, *high)

    for x in range(planes + 8):
        for part in range(2):
            b1[x, part] = smooth_fine(lambda i, p: ext[i, p], x + 2, part)
    for x in range(planes + 4):
        for part in range(2):
            b2[x, part] = smooth_fine(lambda i, p: b1[i, p], x + 2, part)
    for x in range(planes):
        for part in range(2):
            b3 = smooth_fine(lambda i, p: b2[i, p], x + 2, part)
            g[x, part] = fine_scale * (f_ref[x, part] + b1[x + 4, part] + b2[x + 2, part] + b3)
    half = planes // 2
    for x in range(half):
        own_ref[x] = g[core * half + x]
        send_ref[x] = g[(1 - core) * half + x]


def shift_z(v, step):
    width = v.shape[-1] // 2
    lane = lax.broadcasted_iota(jnp.int32, v.shape, len(v.shape) - 1)
    edge = 0 if step > 0 else width - 1
    inner = roll(v, step, 1)
    outer = roll(v, step + (width if step > 0 else -width), 1)
    return jnp.where(lane % width == edge, outer, inner)


def packed_sweep(values, count, depth, source, target, cosine, sine, residual=False):
    rate, near_rate = level_numbers(depth)
    values[0] = cosine * values[count] - sine * roll(values[count], 64, 1)
    values[count + 1] = cosine * values[1] + sine * roll(values[1], 64, 1)

    def body(x):
        v = values[x + 1]
        near = values[x] + values[x + 2]
        near = near + (roll(v, 1, 0) + roll(v, -1, 0))
        near = near + (shift_z(v, 1) + shift_z(v, -1))
        if residual:
            target[x] = source[x] - omega / rate * v + near_rate / rate * near
        else:
            target[x + 1] = rate * source[x] + keep * v + near_rate * near

    each(count, body)


def first_sweep(values, count, depth, source):
    rate, _ = level_numbers(depth)

    def body(x):
        values[x + 1] = rate * source[x]

    each(count, body)


def cycle_kernel(*refs):
    radix = len(refs) - 14
    pieces, refs = refs[:radix], refs[radix:]
    cs_ref, own_ref, send_ref, s, u, v, r1, s2, u2, v2, r2, s3, u3, v3 = refs
    position = lax.axis_index("grid")
    core, block = lax.rem(position, 2), lax.div(position, 4)
    count = s.shape[0]
    rate, near_rate = level_numbers(1)
    cosine, sine = cs_ref[core], cs_ref[2 + core]
    lane = lax.broadcasted_iota(jnp.int32, (8, 128), 1)
    lane_sine = jnp.where(lane < 64, -sine, sine)

    length = count // radix
    digit = lax.div(block, length // 4)
    for k, piece in enumerate(pieces):
        s[pl.ds(lax.bitwise_xor(lax.rem(digit, radix), k) * length, length)] = piece[...]

    def sweep(values, target, residual=False):
        values[0, 0], values[0, 1] = rotated(values[count, 0], values[count, 1], cosine, -sine)
        values[count + 1, 0], values[count + 1, 1] = rotated(
            values[1, 0], values[1, 1], cosine, sine
        )

        def body(x):
            for f in range(2):
                a = values[x + 1, f]
                near = values[x, f] + values[x + 2, f]
                near = near + (roll(a, 1, 0) + roll(a, -1, 0))
                near = near + (roll(a, 1, 1) + roll(a, -1, 1))
                if residual:
                    target[x, f] = s[x, f] - omega / rate * a + near_rate / rate * near
                else:
                    target[x + 1, f] = rate * s[x, f] + keep * a + near_rate * near

        each(count, body)

    def start(x):
        for f in range(2):
            u[x + 1, f] = rate * s[x, f]

    each(count, start)
    sweep(u, v)
    sweep(v, r1, residual=True)

    count2 = count // 2
    i = lax.broadcasted_iota(jnp.int32, (128, 128), 0)
    j = lax.broadcasted_iota(jnp.int32, (128, 128), 1)
    rows = []
    for f in range(2):

        def lower(x):
            r1[2 * x, f] = r1[2 * x, f] + r1[2 * x + 1, f]
            r2[x, 8 * f : 8 * f + 8] = r1[2 * x, f, pl.ds(0, 8, 2)] + r1[2 * x, f, pl.ds(1, 8, 2)]

        each(count2, lower)
        rows.append(r2[:, 8 * f : 8 * f + 8].reshape(count2 * 8, 128))
    lowered = sum(
        dot(rows[f], jnp.where(i // 2 + 64 * f == j, 0.125, 0.0)) for f in range(2)
    )
    s2[...] = lowered.reshape(count2, 8, 128)
    first_sweep(u2, count2, 2, s2)
    packed_sweep(u2, count2, 2, s2, v2, cosine, lane_sine)
    packed_sweep(v2, count2, 2, s2, u2, cosine, lane_sine, residual=True)

    count3 = count2 // 2

    def lower3(x):
        total = u2[2 * x] + u2[2 * x + 1]
        r2[x, 0:8] = total
        r2[x, 8:16] = total
        s3[x] = r2[x, pl.ds(0, 8, 2)] + r2[x, pl.ds(1, 8, 2)]

    each(count3, lower3)
    same = i // 64 == j // 64
    lowered = dot(
        s3[...].reshape(count3 * 8, 128), jnp.where(same & (i % 64 // 2 == j % 32), 0.125, 0.0)
    )
    s3[...] = lowered.reshape(count3, 8, 128)
    first_sweep(u3, count3, 3, s3)
    a, b = u3, v3
    for _ in range(5):
        packed_sweep(a, count3, 3, s3, b, cosine, lane_sine)
        a, b = b, a

    raised = dot(
        a[1 : count3 + 1].reshape(count3 * 8, 128),
        jnp.where(same & (i % 64 == j % 64 // 2), 1.0, 0.0),
    )
    s3[...] = raised.reshape(count3, 8, 128)

    def raise3(x):
        r2[x, pl.ds(0, 8, 2)] = s3[x]
        r2[x, pl.ds(1, 8, 2)] = s3[x]
        for k in range(2):
            v2[2 * x + k + 1] = v2[2 * x + k + 1] + r2[x, 0:8]

    each(count3, raise3)
    packed_sweep(v2, count2, 2, s2, u2, cosine, lane_sine)
    packed_sweep(u2, count2, 2, s2, v2, cosine, lane_sine)

    rows = v2[1 : count2 + 1].reshape(count2 * 8, 128)
    for f in range(2):
        raised = dot(rows, jnp.where(i == j // 2 + 64 * f, 1.0, 0.0))
        s2[...] = raised.reshape(count2, 8, 128)

        def raise2(x):
            r1[x, f, pl.ds(0, 8, 2)] = s2[x]
            r1[x, f, pl.ds(1, 8, 2)] = s2[x]
            for k in range(2):
                v[2 * x + k + 1, f] = v[2 * x + k + 1, f] + r1[x, f]

        each(count2, raise2)
    sweep(v, u)
    sweep(u, v)

    for target, tile in ((own_ref, position), (send_ref, position + 1 - 2 * core)):
        for k in range(5):
            q = tile + k - 2
            low, high = q < 0, q >= count
            q = jnp.where(low, q + count, jnp.where(high, q - count, q))
            c = jnp.where(low | high, cosine, 1.0)
            t = jnp.where(low, -sine, jnp.where(high, sine, 0.0))
            target[k, 0], target[k, 1] = rotated(v[q + 1, 0], v[q + 1, 1], c, t)


def correct(w_ref, g_ref, e, b1, store):
    lines = w_ref.shape[2]
    wide = dot(w_ref[...].reshape(10 * lines, 128), spread_matrix(128, 256))
    for r in range(10):
        for h in range(2):
            value = wide[r * lines : (r + 1) * lines, 128 * h : 128 * (h + 1)]
            e[2 * r + h, pl.ds(0, lines, 2)] = value
            e[2 * r + h, pl.ds(1, lines, 2)] = value

    def expanded(x, f):
        place = (2 * (x // 2) + f) * 2
        return jnp.concatenate([e[place], e[place + 1]], axis=1)

    for x in range(6):
        for f in range(2):
            b1[x, f] = smooth_fine(expanded, x + 2, f)
    for x in range(2):
        for f in range(2):
            store(f, x, g_ref[x, f] + smooth_fine(lambda i, g: b1[i, g], x + 2, f))


def own_kernel(w_ref, g_ref, out_ref, e, b1):
    def store(part, x, value):
        out_ref[part, x] = value

    correct(w_ref, g_ref, e, b1, store)


def output_kernel(own_ref, w_ref, g_ref, out_ref, e, b1):
    core = lax.rem(lax.axis_index("grid"), 2)
    out_ref[core] = own_ref[...]

    def store(part, x, value):
        out_ref[1 - core, part, x] = value

    correct(w_ref, g_ref, e, b1, store)


def pair_phases(pair_table, k_fraction):
    kcount = k_fraction.shape[0]
    picks = pair_table[:, :, None] == jnp.arange(kcount, dtype=jnp.int32)[None, None, :]
    chosen = jnp.sum(jnp.where(picks, k_fraction[None, None, :], 0.0), axis=2)
    angle = 6.283185307179586 * (chosen[:, 0] - chosen[:, 1])
    return jnp.concatenate([jnp.cos(angle), jnp.sin(angle)])


def gather_blocks(value, blocks, block, permute_block):
    stride = 1
    while True:
        radix = min(4, blocks // stride)
        digit = block // stride % radix
        pieces = [value] + [
            permute_block(value, lambda b, k=k: b ^ k * stride) for k in range(1, radix)
        ]
        stride *= radix
        if stride == blocks:
            return pieces
        stacked = jnp.stack(pieces)[jnp.arange(radix) ^ digit]
        value = stacked.reshape(-1, *value.shape[1:])


def vmem(count):
    return [pl.BlockSpec(memory_space=pltpu.VMEM)] * count


smem = [pl.BlockSpec(memory_space=pltpu.SMEM)]


def call(kernel, out_shape, in_specs, scratch, flops):
    single = not isinstance(out_shape, (list, tuple))
    return pl.pallas_call(
        kernel,
        out_shape=out_shape,
        in_specs=in_specs,
        out_specs=vmem(1)[0] if single else vmem(len(out_shape)),
        scratch_shapes=[pltpu.VMEM(shape, jnp.float32) for shape in scratch],
        compiler_params=pltpu.CompilerParams(vmem_limit_bytes=48 * 2**20),
        cost_estimate=pl.CostEstimate(flops=flops, bytes_accessed=2**20, transcendentals=0),
    )


def shaped(*shape):
    return jax.ShapeDtypeStruct(shape, jnp.float32)


def per_device(
    pair_density, moments, shapes, slot_atom, slot_tile, slot_row, pair_table, k_fraction
):
    tile_count = lax.axis_size("grid")
    chips, blocks = tile_count // 2, tile_count // 4
    position = lax.axis_index("grid")
    core, block = position % 2, position // 4
    _, _, thick, lines, depth = pair_density.shape
    planes = 2 * thick
    slot_count = shapes.shape[0]
    capacity = max(2, 2 * slot_count // tile_count)
    devices = range(tile_count)

    def permute(value, target):
        return lax.ppermute(value, "grid", [(i, target(i)) for i in devices])

    def permute_block(value, target):
        return permute(value, lambda i: target(i // 4) * 4 + i % 4)

    def partner(i):
        return i ^ 1

    def even_side(i):
        return i ^ 2

    def odd_side(i):
        return (i // 2 + (1 if i // 2 % 2 else -1)) % chips * 2 + i % 2

    def next_block(i):
        return (i + (4 if i // 2 % 2 else -4)) % tile_count

    cs = pair_phases(pair_table, k_fraction)

    other = permute(lax.dynamic_index_in_dim(pair_density, 1 - core, 0, False), partner)
    tile_row, line_row = slot_tile.reshape(1, -1), slot_row.reshape(1, -1)
    row = 2 * depth
    kept, sent = call(
        rows_kernel,
        [shaped(slot_count, row), shaped(slot_count + 8, row)],
        vmem(5),
        [(2, slot_count, row)],
        10**7,
    )(moments, shapes, slot_atom.reshape(1, -1), tile_row, line_row)
    got = permute(sent, partner)
    apart = chips <= 8
    height = 16 * capacity + 8
    packed = call(
        pack_kernel,
        [shaped(height, 128)] * chips if apart else [shaped(chips, height, 128)],
        vmem(4),
        [],
        10**8,
    )(kept, got, tile_row, line_row)
    if apart:
        received = {0: packed[0]}
        for k in sorted(range(1, chips), reverse=True):
            received[k] = permute(packed[k], lambda i, k=k: i ^ (2 * k))
        received = [received[k] for k in range(chips)]
    else:
        groups = [[2 * k + c for k in range(chips)] for c in range(2)]
        received = [
            lax.all_to_all(
                packed[0], "grid", split_axis=0, concat_axis=0, axis_index_groups=groups, tiled=True
            )
        ]

    full = (2, lines, depth)
    small = (2, lines // 2, depth // 2)
    f, straight, across = call(
        density_kernel,
        [shaped(planes, *full), shaped(10, lines, 128), shaped(2, *full)],
        vmem(2 + len(received)),
        [(planes + 4, *full), (8, lines, 128)],
        10**8,
    )(pair_density, other, *received)
    even = permute(f, even_side)
    odd = permute(f, odd_side)
    straight = permute(straight, next_block)
    across = permute(across, lambda i: (i + (-4 if i // 2 % 2 else 4)) % tile_count)
    source = call(
        source_kernel,
        shaped(planes, *small),
        vmem(4) + smem,
        [(4 * planes, *full), (2 * planes + 4, *full), (4 * planes, lines, 128)],
        10**7,
    )(even, odd, straight, f, cs)
    pieces = gather_blocks(source, blocks, block, permute_block)
    own, send = call(
        fine_kernel,
        [shaped(thick, *full)] * 2,
        vmem(5) + smem,
        [(3 * planes + 4, *full), (planes + 8, *full), (planes + 4, *full), (planes, *full)],
        10**7,
    )(even, odd, straight, across, f, cs)
    got = permute(send, partner)

    n1, n2, n3 = tile_count, tile_count // 2, tile_count // 4
    tile = (8, 128)
    w_own, w_send = call(
        cycle_kernel,
        [shaped(5, *small)] * 2,
        vmem(len(pieces)) + smem,
        [
            (n1, *small),
            (n1 + 2, *small),
            (n1 + 2, *small),
            (n1, *small),
            (n2, *tile),
            (n2 + 2, *tile),
            (n2 + 2, *tile),
            (n2, 16, 128),
            (n3, *tile),
            (n3 + 2, *tile),
            (n3 + 2, *tile),
        ],
        10**8,
    )(*pieces, cs)
    w_got = permute(w_send, partner)
    scratch = [(20, lines, 128), (6, *full)]
    result = call(own_kernel, shaped(2, thick, lines, depth), vmem(2), scratch, 10**7)(w_own, own)
    return call(output_kernel, shaped(*pair_density.shape), vmem(3), scratch, 10**7)(
        result, w_got, got
    )


def solution(mesh):
    return jax.shard_map(
        per_device,
        mesh=mesh,
        in_specs=(
            P("rep", None, "grid", None, None),
            P(("rep", "grid"), None, None, None),
            P(("rep", "grid"), None, None),
            P(("rep", "grid")),
            P(("rep", "grid"), None),
            P(("rep", "grid")),
            P(),
            P(),
        ),
        out_specs=P("rep", None, "grid", None, None),
        check_vma=False,
    )
```

```python
import jax
import jax.numpy as jnp
from jax import lax
from jax.experimental import pallas as pl
from jax.experimental.pallas import tpu as pltpu
from jax.sharding import PartitionSpec as P

omega = 0.8
screen = 0.05
highest = lax.Precision.HIGHEST

fine_diagonal = 7.5 + screen
fine_scale = omega / fine_diagonal
fine_near = fine_scale * 4.0 / 3.0
fine_far = fine_scale / 12.0
keep = 1.0 - omega


def level_numbers(depth):
    quarter = 1.0 / 4**depth
    diagonal = 6.0 * quarter + screen
    return omega / diagonal, omega / diagonal * quarter


def each(count, body, most=16):
    if count <= most:
        for i in range(count):
            body(i)
    else:
        pl.loop(0, count, unroll=4)(body)


def dot(a, b):
    return jnp.dot(a, b, precision=highest, preferred_element_type=jnp.float32)


def pair_matrix(rows, columns, value):
    i = lax.broadcasted_iota(jnp.int32, (rows, columns), 0)
    j = lax.broadcasted_iota(jnp.int32, (rows, columns), 1)
    return jnp.where(i // 2 == j, value, 0.0)


def spread_matrix(rows, columns):
    i = lax.broadcasted_iota(jnp.int32, (rows, columns), 0)
    j = lax.broadcasted_iota(jnp.int32, (rows, columns), 1)
    return jnp.where(i == j // 2, 1.0, 0.0)


def roll(v, shift, axis):
    return pltpu.roll(v, shift % v.shape[axis], axis)


def smooth_fine(at, x, f):
    total = None
    for step, weight in ((1, fine_near), (2, -fine_far)):
        sides = [p for p in (at(x - step, f), at(x + step, f)) if p is not None]
        v = at(x, f)
        if v is not None:
            for axis in (0, 1):
                sides.append(roll(v, step, axis) + roll(v, -step, axis))
            if step == 1:
                total = keep * v
        if sides:
            part = weight * sum(sides[1:], sides[0])
            total = part if total is None else total + part
    return total


def rotated(real, imag, cosine, sine):
    return cosine * real - sine * imag, sine * real + cosine * imag


def place_planes(target, base, source, cosine, sine):
    for x in range(source.shape[0]):
        real, imag = rotated(source[x, 0], source[x, 1], cosine, sine)
        target[base + x, 0] = real
        target[base + x, 1] = imag


def place_halo(ext, middle, even_ref, odd_ref, cs_ref):
    position = lax.axis_index("grid")
    chips = lax.axis_size("grid") // 2
    core, chip = lax.rem(position, 2), lax.div(position, 2)
    cosine, sine = cs_ref[core], cs_ref[2 + core]
    first, last = chip == 0, chip == chips - 1
    low = (jnp.where(first, cosine, 1.0), jnp.where(first, -sine, 0.0))
    high = (jnp.where(last, cosine, 1.0), jnp.where(last, sine, 0.0))
    planes = even_ref.shape[0]
    parity = lax.rem(chip, 2)

    @pl.when(parity == 0)
    def _():
        place_planes(ext, middle - planes, odd_ref, *low)
        place_planes(ext, middle + planes, even_ref, *high)

    @pl.when(parity == 1)
    def _():
        place_planes(ext, middle - planes, even_ref, *low)
        place_planes(ext, middle + planes, odd_ref, *high)


def as_column(row):
    n = row.shape[1]
    i = lax.broadcasted_iota(jnp.int32, (n, n), 0)
    j = lax.broadcasted_iota(jnp.int32, (n, n), 1)
    return jnp.sum(jnp.where(i == j, row, 0.0), axis=1, keepdims=True)


def rows_kernel(moments_ref, shapes_ref, atom_ref, tile_ref, line_ref, keep_ref, send_ref, rows):
    core = lax.rem(lax.axis_index("grid"), 2)
    channels, slots, depth = shapes_ref.shape
    atoms = moments_ref.shape[0]
    atom = as_column(atom_ref[...].astype(jnp.float32))
    picks = [jnp.where(atom == float(a), 1.0, 0.0) for a in range(atoms)]
    chosen = []
    for f in range(4):
        total = None
        for a in range(atoms):
            value = picks[a] * moments_ref[a, f // 2, f % 2 : f % 2 + 1]
            total = value if total is None else total + value
        chosen.append(total)
    for i in range(slots // 8):
        near = slice(8 * i, 8 * i + 8)
        totals = [None] * 4
        for channel in range(channels):
            shape = shapes_ref[channel, near]
            for f in range(4):
                value = chosen[f][near, channel : channel + 1] * shape
                totals[f] = value if totals[f] is None else totals[f] + value
        for f in range(4):
            rows[f // 2, near, f % 2 * depth : (f % 2 + 1) * depth] = totals[f]
    keep_ref[...] = rows[core]
    send_ref[0:slots] = rows[1 - core]
    send_ref[slots:] = jnp.zeros((8, 2 * depth), jnp.float32)
    number = (tile_ref[...] * 64 + line_ref[...]).astype(jnp.float32)
    send_ref[slots : slots + 1, 0:slots] = number


def pack_kernel(own_ref, got_ref, tile_ref, line_ref, _, *out_refs):
    slots = own_ref.shape[0]
    apart = len(out_refs) > 1
    height = out_refs[0].shape[-2]
    ranks = (height - 8) // 4
    capacity = ranks // 4
    chips = lax.axis_size("grid") // 2
    chip = lax.div(lax.axis_index("grid"), 2)
    number = (tile_ref[...] * 64 + line_ref[...]).astype(jnp.float32)
    number = jnp.concatenate([number, got_ref[slots : slots + 1, 0:slots]], axis=1).astype(jnp.int32)
    tile, line = number // 64, number % 128 + 1
    column = as_column(tile.astype(jnp.float32)).astype(jnp.int32)
    i = lax.broadcasted_iota(jnp.int32, (2 * slots, 2 * slots), 0)
    j = lax.broadcasted_iota(jnp.int32, (2 * slots, 2 * slots), 1)
    ahead = jnp.where((column == tile) & (i < j) & (i // slots == j // slots), 1.0, 0.0)
    rank = jnp.sum(ahead, axis=0, keepdims=True).astype(jnp.int32)
    device = lax.broadcasted_iota(jnp.int32, (1, 2 * slots), 1) // slots
    place = tile // 2 * ranks + (2 * device + tile % 2) * capacity + rank
    r = lax.broadcasted_iota(jnp.int32, (ranks, 2 * slots), 0)
    targets = [lax.bitwise_xor(chip, k) if apart else k for k in range(chips)]
    pick = jnp.concatenate([jnp.where(place == r + target * ranks, 1.0, 0.0) for target in targets])
    rows = jnp.concatenate([own_ref[...], got_ref[0:slots]], axis=0)
    packed = dot(pick, rows)
    lines = jnp.sum(pick * line.astype(jnp.float32), axis=1, keepdims=True)
    bucket = lax.broadcasted_iota(jnp.int32, (chips * ranks, 128), 0)
    lane = lax.broadcasted_iota(jnp.int32, (chips * ranks, 128), 1)
    spot = bucket // ranks if apart else chip
    spots = jnp.where(lane == spot % (128 // ranks) * ranks + bucket % ranks, lines, 0.0)
    i = lax.broadcasted_iota(jnp.int32, (chips, chips * ranks), 0)
    j = lax.broadcasted_iota(jnp.int32, (chips, chips * ranks), 1)
    numbers = dot(jnp.where(i == j // ranks, 1.0, 0.0), spots)
    for k in range(chips):
        out = out_refs[k] if apart else out_refs[0].at[k]
        for q in range(4):
            out[q * ranks : (q + 1) * ranks] = packed[
                k * ranks : (k + 1) * ranks, q * 128 : (q + 1) * 128
            ]
        out[4 * ranks :] = jnp.broadcast_to(numbers[k : k + 1], (8, 128))


def message_order(chips):
    half = chips // 2
    return [0, 1, *range(half + 2, chips), half, half + 1, *range(2, half)]


def density_kernel(*refs):
    pd_ref, other_ref = refs[:2]
    f_ref, straight_ref, across_ref, b1, half = refs[-5:]
    pieces = refs[2:-5]
    position = lax.axis_index("grid")
    core, side = lax.rem(position, 2), lax.rem(lax.div(position, 2), 2)
    planes, _, lines, depth = f_ref.shape
    sources = lax.axis_size("grid") // 2
    height = pieces[0].shape[-2]
    ranks = (height - 8) // 4
    group = 128 // ranks

    def received(source, start, stop):
        if len(pieces) > 1:
            return pieces[message_order(sources).index(source)][start:stop]
        return pieces[0][source, start:stop]

    added = [None, None]
    for first in range(0, sources, group):
        members = range(first, min(first + group, sources))
        numbers = sum(received(k, 4 * ranks, 4 * ranks + 1) for k in members)
        line = lax.broadcasted_iota(jnp.int32, (planes * lines, 128), 0)
        spread = jnp.where(line == numbers.astype(jnp.int32) - 1, 1.0, 0.0)
        for part in range(2):
            values = jnp.concatenate(
                [
                    jnp.concatenate(
                        [received(k, q * ranks, (q + 1) * ranks) for k in members], axis=0
                    )
                    for q in (2 * part, 2 * part + 1)
                ],
                axis=1,
            )
            value = dot(spread[:, : len(members) * ranks], values)
            added[part] = value if added[part] is None else added[part] + value
    for x in range(planes):
        for part in range(2):
            f_ref[x, part] = added[part][x * lines : (x + 1) * lines]
    thick = planes // 2
    for x in range(thick):
        for part in range(2):
            f_ref[core * thick + x, part] += pd_ref[core, part, x]
            f_ref[(1 - core) * thick + x, part] += other_ref[part, x]

    def density(x, part):
        return f_ref[x, part] if 0 <= x < planes else None

    def once(x, part):
        return b1[x + 2, part] if -2 <= x < planes + 2 else None

    def outer(base, first_plane, one):
        for x in range(one, one + 4):
            for part in range(2):
                b1[x + 2, part] = smooth_fine(density, x, part)
        for i in range(2):
            for part in range(2):
                x = base + 2 * i
                total = smooth_fine(once, x, part) + smooth_fine(once, x + 1, part)
                for h in range(2):
                    half[(2 * i + part) * 2 + h] = total[:, h * 128 : (h + 1) * 128]
        for r, value in enumerate(lowered(half, 4, lines, depth)):
            straight_ref[8 + r // 2, r % 2 * 16 : r % 2 * 16 + 16] = value
        for x in range(2):
            for part in range(2):
                for h in range(2):
                    straight_ref[(2 * x + part) * 2 + h] = f_ref[
                        first_plane + x, part, :, h * 128 : (h + 1) * 128
                    ]
        other = planes - 2 - first_plane
        for x in range(2):
            across_ref[x] = f_ref[other + x]

    @pl.when(side == 0)
    def _():
        outer(-4, 0, -2)

    @pl.when(side == 1)
    def _():
        outer(planes, planes - 2, planes - 2)


def lowered(half, rows, lines, depth):
    matrix = pair_matrix(depth, depth // 2, 0.125)
    total = None
    for h in range(2):
        stacked = jnp.concatenate(
            [
                half[2 * r + h, pl.ds(0, lines // 2, 2)] + half[2 * r + h, pl.ds(1, lines // 2, 2)]
                for r in range(rows)
            ],
            axis=0,
        )
        value = dot(stacked, matrix[h * 128 : (h + 1) * 128])
        total = value if total is None else total + value
    return [total[r * lines // 2 : (r + 1) * lines // 2] for r in range(rows)]


def source_kernel(even_ref, odd_ref, straight_ref, f_ref, cs_ref, s_ref, ext, b1, half):
    position = lax.axis_index("grid")
    blocks = lax.axis_size("grid") // 4
    core, side, block = lax.rem(position, 2), lax.rem(lax.div(position, 2), 2), lax.div(position, 4)
    cosine, sine = cs_ref[core], cs_ref[2 + core]
    planes = f_ref.shape[0]
    lines, depth = f_ref.shape[2:]
    first, last = block == 0, block == blocks - 1
    low = (jnp.where(first, cosine, 1.0), jnp.where(first, -sine, 0.0))
    high = (jnp.where(last, cosine, 1.0), jnp.where(last, sine, 0.0))

    @pl.when(side == 0)
    def _():
        place_planes(ext, 0, odd_ref, *low)
        ext[planes : 2 * planes] = f_ref[...]
        ext[2 * planes : 3 * planes] = even_ref[...]
        ext[3 * planes :] = jnp.zeros((planes, 2, lines, depth), jnp.float32)

    @pl.when(side == 1)
    def _():
        ext[:planes] = jnp.zeros((planes, 2, lines, depth), jnp.float32)
        ext[planes : 2 * planes] = even_ref[...]
        ext[2 * planes : 3 * planes] = f_ref[...]
        place_planes(ext, 3 * planes, odd_ref, *high)

    for x in range(2 * planes + 4):
        for part in range(2):
            b1[x, part] = smooth_fine(lambda i, p: ext[i, p], x + planes - 2, part)
    for i in range(planes):
        for part in range(2):
            total = smooth_fine(lambda i, p: b1[i, p], 2 * i + 2, part) + smooth_fine(
                lambda i, p: b1[i, p], 2 * i + 3, part
            )
            for h in range(2):
                half[(2 * i + part) * 2 + h] = total[:, h * 128 : (h + 1) * 128]
    for r, value in enumerate(lowered(half, 2 * planes, lines, depth)):
        s_ref[r // 2, r % 2] = value

    def add(base, c, t):
        for x in range(2):
            real, imag = rotated(straight_ref[8 + x, 0:16], straight_ref[8 + x, 16:32], c, t)
            s_ref[base + x, 0] += real
            s_ref[base + x, 1] += imag

    @pl.when(side == 0)
    def _():
        add(2, *high)

    @pl.when(side == 1)
    def _():
        add(0, *low)


def fine_kernel(
    even_ref, odd_ref, straight_ref, across_ref, f_ref, cs_ref, own_ref, send_ref, ext, b1, b2, g
):
    position = lax.axis_index("grid")
    chips = lax.axis_size("grid") // 2
    core, chip = lax.rem(position, 2), lax.div(position, 2)
    cosine, sine = cs_ref[core], cs_ref[2 + core]
    planes = f_ref.shape[0]
    place_halo(ext, planes + 2, even_ref, odd_ref, cs_ref)
    ext[planes + 2 : 2 * planes + 2] = f_ref[...]
    first, last = chip < 2, chip >= chips - 2
    low = (jnp.where(first, cosine, 1.0), jnp.where(first, -sine, 0.0))
    high = (jnp.where(last, cosine, 1.0), jnp.where(last, sine, 0.0))

    def place_straight(base, c, t):
        for x in range(2):
            real, imag = [
                jnp.concatenate([straight_ref[4 * x + 2 * p], straight_ref[4 * x + 2 * p + 1]], axis=1)
                for p in range(2)
            ]
            ext[base + x, 0], ext[base + x, 1] = rotated(real, imag, c, t)

    @pl.when(lax.rem(chip, 2) == 0)
    def _():
        place_planes(ext, 0, across_ref, *low)
        place_straight(3 * planes + 2, *high)

    @pl.when(lax.rem(chip, 2) == 1)
    def _():
        place_straight(0, *low)
        place_planes(ext, 3 * planes + 2, across_ref, *high)

    for x in range(planes + 8):
        for part in range(2):
            b1[x, part] = smooth_fine(lambda i, p: ext[i, p], x + 2, part)
    for x in range(planes + 4):
        for part in range(2):
            b2[x, part] = smooth_fine(lambda i, p: b1[i, p], x + 2, part)
    for x in range(planes):
        for part in range(2):
            b3 = smooth_fine(lambda i, p: b2[i, p], x + 2, part)
            g[x, part] = fine_scale * (f_ref[x, part] + b1[x + 4, part] + b2[x + 2, part] + b3)
    half = planes // 2
    for x in range(half):
        own_ref[x] = g[core * half + x]
        send_ref[x] = g[(1 - core) * half + x]


def shift_z(v, step):
    width = v.shape[-1] // 2
    lane = lax.broadcasted_iota(jnp.int32, v.shape, len(v.shape) - 1)
    edge = 0 if step > 0 else width - 1
    inner = roll(v, step, 1)
    outer = roll(v, step + (width if step > 0 else -width), 1)
    return jnp.where(lane % width == edge, outer, inner)


def packed_sweep(values, count, depth, source, target, cosine, sine, residual=False):
    rate, near_rate = level_numbers(depth)
    values[0] = cosine * values[count] - sine * roll(values[count], 64, 1)
    values[count + 1] = cosine * values[1] + sine * roll(values[1], 64, 1)

    def body(x):
        v = values[x + 1]
        near = values[x] + values[x + 2]
        near = near + (roll(v, 1, 0) + roll(v, -1, 0))
        near = near + (shift_z(v, 1) + shift_z(v, -1))
        if residual:
            target[x] = source[x] - omega / rate * v + near_rate / rate * near
        else:
            target[x + 1] = rate * source[x] + keep * v + near_rate * near

    each(count, body)


def first_sweep(values, count, depth, source):
    rate, _ = level_numbers(depth)

    def body(x):
        values[x + 1] = rate * source[x]

    each(count, body)


def cycle_kernel(*refs):
    radix = len(refs) - 14
    pieces, refs = refs[:radix], refs[radix:]
    cs_ref, own_ref, send_ref, s, u, v, r1, s2, u2, v2, r2, s3, u3, v3 = refs
    position = lax.axis_index("grid")
    core, block = lax.rem(position, 2), lax.div(position, 4)
    count = s.shape[0]
    rate, near_rate = level_numbers(1)
    cosine, sine = cs_ref[core], cs_ref[2 + core]
    lane = lax.broadcasted_iota(jnp.int32, (8, 128), 1)
    lane_sine = jnp.where(lane < 64, -sine, sine)

    length = count // radix
    digit = lax.div(block, length // 4)
    for k, piece in enumerate(pieces):
        s[pl.ds(lax.bitwise_xor(lax.rem(digit, radix), k) * length, length)] = piece[...]

    def sweep(values, target, residual=False):
        values[0, 0], values[0, 1] = rotated(values[count, 0], values[count, 1], cosine, -sine)
        values[count + 1, 0], values[count + 1, 1] = rotated(
            values[1, 0], values[1, 1], cosine, sine
        )

        def body(x):
            for f in range(2):
                a = values[x + 1, f]
                near = values[x, f] + values[x + 2, f]
                near = near + (roll(a, 1, 0) + roll(a, -1, 0))
                near = near + (roll(a, 1, 1) + roll(a, -1, 1))
                if residual:
                    target[x, f] = s[x, f] - omega / rate * a + near_rate / rate * near
                else:
                    target[x + 1, f] = rate * s[x, f] + keep * a + near_rate * near

        each(count, body)

    def start(x):
        for f in range(2):
            u[x + 1, f] = rate * s[x, f]

    each(count, start)
    sweep(u, v)
    sweep(v, r1, residual=True)

    count2 = count // 2
    i = lax.broadcasted_iota(jnp.int32, (128, 128), 0)
    j = lax.broadcasted_iota(jnp.int32, (128, 128), 1)
    rows = []
    for f in range(2):

        def lower(x):
            r1[2 * x, f] = r1[2 * x, f] + r1[2 * x + 1, f]
            r2[x, 8 * f : 8 * f + 8] = r1[2 * x, f, pl.ds(0, 8, 2)] + r1[2 * x, f, pl.ds(1, 8, 2)]

        each(count2, lower)
        rows.append(r2[:, 8 * f : 8 * f + 8].reshape(count2 * 8, 128))
    lowered = sum(
        dot(rows[f], jnp.where(i // 2 + 64 * f == j, 0.125, 0.0)) for f in range(2)
    )
    s2[...] = lowered.reshape(count2, 8, 128)
    first_sweep(u2, count2, 2, s2)
    packed_sweep(u2, count2, 2, s2, v2, cosine, lane_sine)
    packed_sweep(v2, count2, 2, s2, u2, cosine, lane_sine, residual=True)

    count3 = count2 // 2

    def lower3(x):
        total = u2[2 * x] + u2[2 * x + 1]
        r2[x, 0:8] = total
        r2[x, 8:16] = total
        s3[x] = r2[x, pl.ds(0, 8, 2)] + r2[x, pl.ds(1, 8, 2)]

    each(count3, lower3)
    same = i // 64 == j // 64
    lowered = dot(
        s3[...].reshape(count3 * 8, 128), jnp.where(same & (i % 64 // 2 == j % 32), 0.125, 0.0)
    )
    s3[...] = lowered.reshape(count3, 8, 128)
    first_sweep(u3, count3, 3, s3)
    a, b = u3, v3
    for _ in range(5):
        packed_sweep(a, count3, 3, s3, b, cosine, lane_sine)
        a, b = b, a

    raised = dot(
        a[1 : count3 + 1].reshape(count3 * 8, 128),
        jnp.where(same & (i % 64 == j % 64 // 2), 1.0, 0.0),
    )
    s3[...] = raised.reshape(count3, 8, 128)

    def raise3(x):
        r2[x, pl.ds(0, 8, 2)] = s3[x]
        r2[x, pl.ds(1, 8, 2)] = s3[x]
        for k in range(2):
            v2[2 * x + k + 1] = v2[2 * x + k + 1] + r2[x, 0:8]

    each(count3, raise3)
    packed_sweep(v2, count2, 2, s2, u2, cosine, lane_sine)
    packed_sweep(u2, count2, 2, s2, v2, cosine, lane_sine)

    rows = v2[1 : count2 + 1].reshape(count2 * 8, 128)
    for f in range(2):
        raised = dot(rows, jnp.where(i == j // 2 + 64 * f, 1.0, 0.0))
        s2[...] = raised.reshape(count2, 8, 128)

        def raise2(x):
            r1[x, f, pl.ds(0, 8, 2)] = s2[x]
            r1[x, f, pl.ds(1, 8, 2)] = s2[x]
            for k in range(2):
                v[2 * x + k + 1, f] = v[2 * x + k + 1, f] + r1[x, f]

        each(count2, raise2)
    sweep(v, u)
    sweep(u, v)

    for target, tile in ((own_ref, position), (send_ref, position + 1 - 2 * core)):
        for k in range(5):
            q = tile + k - 2
            low, high = q < 0, q >= count
            q = jnp.where(low, q + count, jnp.where(high, q - count, q))
            c = jnp.where(low | high, cosine, 1.0)
            t = jnp.where(low, -sine, jnp.where(high, sine, 0.0))
            target[k, 0], target[k, 1] = rotated(v[q + 1, 0], v[q + 1, 1], c, t)


def correct(w_ref, g_ref, e, b1, store):
    lines = w_ref.shape[2]
    wide = dot(w_ref[...].reshape(10 * lines, 128), spread_matrix(128, 256))
    for r in range(10):
        for h in range(2):
            value = wide[r * lines : (r + 1) * lines, 128 * h : 128 * (h + 1)]
            e[2 * r + h, pl.ds(0, lines, 2)] = value
            e[2 * r + h, pl.ds(1, lines, 2)] = value

    def expanded(x, f):
        place = (2 * (x // 2) + f) * 2
        return jnp.concatenate([e[place], e[place + 1]], axis=1)

    for x in range(6):
        for f in range(2):
            b1[x, f] = smooth_fine(expanded, x + 2, f)
    for x in range(2):
        for f in range(2):
            store(f, x, g_ref[x, f] + smooth_fine(lambda i, g: b1[i, g], x + 2, f))


def own_kernel(w_ref, g_ref, out_ref, e, b1):
    def store(part, x, value):
        out_ref[part, x] = value

    correct(w_ref, g_ref, e, b1, store)


def output_kernel(own_ref, w_ref, g_ref, out_ref, e, b1):
    core = lax.rem(lax.axis_index("grid"), 2)
    out_ref[core] = own_ref[...]

    def store(part, x, value):
        out_ref[1 - core, part, x] = value

    correct(w_ref, g_ref, e, b1, store)


def pair_phases(pair_table, k_fraction):
    kcount = k_fraction.shape[0]
    picks = pair_table[:, :, None] == jnp.arange(kcount, dtype=jnp.int32)[None, None, :]
    chosen = jnp.sum(jnp.where(picks, k_fraction[None, None, :], 0.0), axis=2)
    angle = 6.283185307179586 * (chosen[:, 0] - chosen[:, 1])
    return jnp.concatenate([jnp.cos(angle), jnp.sin(angle)])


def gather_blocks(value, blocks, block, permute_block):
    stride = 1
    while True:
        radix = min(4, blocks // stride)
        digit = block // stride % radix
        pieces = [value] + [
            permute_block(value, lambda b, k=k: b ^ k * stride) for k in range(1, radix)
        ]
        stride *= radix
        if stride == blocks:
            return pieces
        stacked = jnp.stack(pieces)[jnp.arange(radix) ^ digit]
        value = stacked.reshape(-1, *value.shape[1:])


def vmem(count):
    return [pl.BlockSpec(memory_space=pltpu.VMEM)] * count


smem = [pl.BlockSpec(memory_space=pltpu.SMEM)]


def call(kernel, out_shape, in_specs, scratch, flops):
    single = not isinstance(out_shape, (list, tuple))
    return pl.pallas_call(
        kernel,
        out_shape=out_shape,
        in_specs=in_specs,
        out_specs=vmem(1)[0] if single else vmem(len(out_shape)),
        scratch_shapes=[pltpu.VMEM(shape, jnp.float32) for shape in scratch],
        compiler_params=pltpu.CompilerParams(vmem_limit_bytes=48 * 2**20),
        cost_estimate=pl.CostEstimate(flops=flops, bytes_accessed=2**20, transcendentals=0),
    )


def shaped(*shape):
    return jax.ShapeDtypeStruct(shape, jnp.float32)


def per_device(
    pair_density, moments, shapes, slot_atom, slot_tile, slot_row, pair_table, k_fraction
):
    tile_count = lax.axis_size("grid")
    chips, blocks = tile_count // 2, tile_count // 4
    position = lax.axis_index("grid")
    core, block = position % 2, position // 4
    _, _, thick, lines, depth = pair_density.shape
    planes = 2 * thick
    slot_count = shapes.shape[0]
    capacity = max(2, 2 * slot_count // tile_count)
    devices = range(tile_count)

    def permute(value, target):
        return lax.ppermute(value, "grid", [(i, target(i)) for i in devices])

    def permute_block(value, target):
        return permute(value, lambda i: target(i // 4) * 4 + i % 4)

    def partner(i):
        return i ^ 1

    def even_side(i):
        return i ^ 2

    def odd_side(i):
        return (i // 2 + (1 if i // 2 % 2 else -1)) % chips * 2 + i % 2

    def next_block(i):
        return (i + (4 if i // 2 % 2 else -4)) % tile_count

    cs = pair_phases(pair_table, k_fraction)

    other = permute(lax.dynamic_index_in_dim(pair_density, 1 - core, 0, False), partner)
    tile_row, line_row = slot_tile.reshape(1, -1), slot_row.reshape(1, -1)
    row = 2 * depth
    kept, sent = call(
        rows_kernel,
        [shaped(slot_count, row), shaped(slot_count + 8, row)],
        vmem(5),
        [(2, slot_count, row)],
        10**7,
    )(moments, shapes.transpose(1, 0, 2), slot_atom.reshape(1, -1), tile_row, line_row)
    got = permute(sent, partner)
    apart = chips <= 8
    height = 16 * capacity + 8
    packed = call(
        pack_kernel,
        [shaped(height, 128)] * chips if apart else [shaped(chips, height, 128)],
        vmem(4) + [pl.BlockSpec(memory_space=pl.ANY)],
        [],
        10**8,
    )(kept, got, tile_row, line_row, other)
    if apart:
        received = [
            permute(packed[k], lambda i, k=k: i ^ (2 * k)) if k else packed[k]
            for k in message_order(chips)
        ]
    else:
        groups = [[2 * k + c for k in range(chips)] for c in range(2)]
        received = [
            lax.all_to_all(
                packed[0], "grid", split_axis=0, concat_axis=0, axis_index_groups=groups, tiled=True
            )
        ]

    full = (2, lines, depth)
    small = (2, lines // 2, depth // 2)
    f, straight, across = call(
        density_kernel,
        [shaped(planes, *full), shaped(10, lines, 128), shaped(2, *full)],
        vmem(2 + len(received)),
        [(planes + 4, *full), (8, lines, 128)],
        10**8,
    )(pair_density, other, *received)
    even = permute(f, even_side)
    odd = permute(f, odd_side)
    straight = permute(straight, next_block)
    across = permute(across, lambda i: (i + (-4 if i // 2 % 2 else 4)) % tile_count)
    source = call(
        source_kernel,
        shaped(planes, *small),
        vmem(4) + smem,
        [(4 * planes, *full), (2 * planes + 4, *full), (4 * planes, lines, 128)],
        10**7,
    )(even, odd, straight, f, cs)
    pieces = gather_blocks(source, blocks, block, permute_block)
    own, send = call(
        fine_kernel,
        [shaped(thick, *full)] * 2,
        vmem(5) + smem,
        [(3 * planes + 4, *full), (planes + 8, *full), (planes + 4, *full), (planes, *full)],
        10**7,
    )(even, odd, straight, across, f, cs)
    got = permute(send, partner)

    n1, n2, n3 = tile_count, tile_count // 2, tile_count // 4
    tile = (8, 128)
    w_own, w_send = call(
        cycle_kernel,
        [shaped(5, *small)] * 2,
        vmem(len(pieces)) + smem,
        [
            (n1, *small),
            (n1 + 2, *small),
            (n1 + 2, *small),
            (n1, *small),
            (n2, *tile),
            (n2 + 2, *tile),
            (n2 + 2, *tile),
            (n2, 16, 128),
            (n3, *tile),
            (n3 + 2, *tile),
            (n3 + 2, *tile),
        ],
        10**8,
    )(*pieces, cs)
    w_got = permute(w_send, partner)
    scratch = [(20, lines, 128), (6, *full)]
    result = call(own_kernel, shaped(2, thick, lines, depth), vmem(2), scratch, 10**7)(w_own, own)
    return call(output_kernel, shaped(*pair_density.shape), vmem(3), scratch, 10**7)(
        result, w_got, got
    )


def solution(mesh):
    return jax.shard_map(
        per_device,
        mesh=mesh,
        in_specs=(
            P("rep", None, "grid", None, None),
            P(("rep", "grid"), None, None, None),
            P(("rep", "grid"), None, None),
            P(("rep", "grid")),
            P(("rep", "grid"), None),
            P(("rep", "grid")),
            P(),
            P(),
        ),
        out_specs=P("rep", None, "grid", None, None),
        check_vma=False,
    )
```

```python
import jax
import jax.numpy as jnp
from jax import lax
from jax.experimental import pallas as pl
from jax.experimental.pallas import tpu as pltpu
from jax.sharding import PartitionSpec as P

omega = 0.8
screen = 0.05
highest = lax.Precision.HIGHEST

fine_diagonal = 7.5 + screen
fine_scale = omega / fine_diagonal
fine_near = fine_scale * 4.0 / 3.0
fine_far = fine_scale / 12.0
keep = 1.0 - omega


def level_numbers(depth):
    quarter = 1.0 / 4**depth
    diagonal = 6.0 * quarter + screen
    return omega / diagonal, omega / diagonal * quarter


def each(count, body, most=16):
    if count <= most:
        for i in range(count):
            body(i)
    else:
        pl.loop(0, count, unroll=4)(body)


def dot(a, b):
    return jnp.dot(a, b, precision=highest, preferred_element_type=jnp.float32)


def pair_matrix(rows, columns, value):
    i = lax.broadcasted_iota(jnp.int32, (rows, columns), 0)
    j = lax.broadcasted_iota(jnp.int32, (rows, columns), 1)
    return jnp.where(i // 2 == j, value, 0.0)


def spread_matrix(rows, columns):
    i = lax.broadcasted_iota(jnp.int32, (rows, columns), 0)
    j = lax.broadcasted_iota(jnp.int32, (rows, columns), 1)
    return jnp.where(i == j // 2, 1.0, 0.0)


def roll(v, shift, axis):
    return pltpu.roll(v, shift % v.shape[axis], axis)


def smooth_fine(at, x, f):
    total = None
    for step, weight in ((1, fine_near), (2, -fine_far)):
        sides = [p for p in (at(x - step, f), at(x + step, f)) if p is not None]
        v = at(x, f)
        if v is not None:
            for axis in (0, 1):
                sides.append(roll(v, step, axis) + roll(v, -step, axis))
            if step == 1:
                total = keep * v
        if sides:
            part = weight * sum(sides[1:], sides[0])
            total = part if total is None else total + part
    return total


def rotated(real, imag, cosine, sine):
    return cosine * real - sine * imag, sine * real + cosine * imag


def place_planes(target, base, source, cosine, sine):
    for x in range(source.shape[0]):
        real, imag = rotated(source[x, 0], source[x, 1], cosine, sine)
        target[base + x, 0] = real
        target[base + x, 1] = imag


def place_in_grid():
    position = lax.axis_index("grid")
    return lax.rem(lax.div(position, 2), 2), lax.rem(position, 2), lax.div(position, 4)


def place_halo(ext, middle, even_ref, odd_ref, cs_ref):
    blocks = lax.axis_size("grid") // 4
    pair, parity, block = place_in_grid()
    cosine, sine = cs_ref[pair], cs_ref[2 + pair]
    first, last = (block == 0) & (parity == 0), (block == blocks - 1) & (parity == 1)
    low = (jnp.where(first, cosine, 1.0), jnp.where(first, -sine, 0.0))
    high = (jnp.where(last, cosine, 1.0), jnp.where(last, sine, 0.0))
    planes = even_ref.shape[0]

    @pl.when(parity == 0)
    def _():
        place_planes(ext, middle - planes, odd_ref, *low)
        place_planes(ext, middle + planes, even_ref, *high)

    @pl.when(parity == 1)
    def _():
        place_planes(ext, middle - planes, even_ref, *low)
        place_planes(ext, middle + planes, odd_ref, *high)


def as_column(row):
    n = row.shape[1]
    i = lax.broadcasted_iota(jnp.int32, (n, n), 0)
    j = lax.broadcasted_iota(jnp.int32, (n, n), 1)
    return jnp.sum(jnp.where(i == j, row, 0.0), axis=1, keepdims=True)


def rows_kernel(moments_ref, shapes_ref, atom_ref, tile_ref, line_ref, out_ref, shapes, arrived):
    channels, slots, depth = shapes.shape
    steps = arrived.shape[0]
    cuts = [channels * k // steps for k in range(steps + 1)]
    copies = [
        pltpu.make_async_copy(
            shapes_ref.at[cuts[k] : cuts[k + 1]], shapes.at[cuts[k] : cuts[k + 1]], arrived.at[k]
        )
        for k in range(steps)
    ]
    for copy in copies:
        copy.start()
    out_ref[slots:] = jnp.zeros((8, 4 * depth), jnp.float32)
    number = (tile_ref[...] * 64 + line_ref[...]).astype(jnp.float32)
    out_ref[slots : slots + 1, 0:slots] = number
    atoms = moments_ref.shape[0]
    atom = as_column(atom_ref[...].astype(jnp.float32))
    picks = [jnp.where(atom == float(a), 1.0, 0.0) for a in range(atoms)]
    chosen = []
    for f in range(4):
        total = None
        for a in range(atoms):
            value = picks[a] * moments_ref[a, f // 2, f % 2 : f % 2 + 1]
            total = value if total is None else total + value
        chosen.append(total)
    for k in range(steps):
        copies[k].wait()
        for i in range(slots // 8):
            near = slice(8 * i, 8 * i + 8)
            totals = [out_ref[near, f * depth : (f + 1) * depth] if k else None for f in range(4)]
            for channel in range(cuts[k], cuts[k + 1]):
                shape = shapes[channel, near]
                for f in range(4):
                    value = chosen[f][near, channel : channel + 1] * shape
                    totals[f] = value if totals[f] is None else totals[f] + value
            for f in range(4):
                out_ref[near, f * depth : (f + 1) * depth] = totals[f]


def pack_kernel(own_ref, got_ref, *refs):
    out_refs, scratch = refs[:-1], refs[-1]
    slots = own_ref.shape[0] - 8
    apart = len(out_refs) > 1
    height = out_refs[0].shape[-2]
    ranks = (height - 8) // 4
    capacity = ranks // 4
    chips = lax.axis_size("grid") // 2
    blocks = chips // 2
    position = lax.axis_index("grid")
    side, chip = lax.rem(position, 2), lax.div(position, 2)
    number = jnp.concatenate(
        [ref[slots : slots + 1, 0:slots] for ref in (own_ref, got_ref)], axis=1
    ).astype(jnp.int32)
    tile, line = number // 64, number % 128 + 1
    column = as_column(tile.astype(jnp.float32)).astype(jnp.int32)
    i = lax.broadcasted_iota(jnp.int32, (2 * slots, 2 * slots), 0)
    j = lax.broadcasted_iota(jnp.int32, (2 * slots, 2 * slots), 1)
    ahead = jnp.where((column == tile) & (i < j) & (i // slots == j // slots), 1.0, 0.0)
    rank = jnp.sum(ahead, axis=0, keepdims=True).astype(jnp.int32)
    device = lax.broadcasted_iota(jnp.int32, (1, 2 * slots), 1) // slots
    place = tile // 4 * ranks + (2 * device + tile % 2) * capacity + rank
    place = jnp.where(tile % 4 // 2 == side, place, -1)
    buckets = blocks * ranks
    pick = jnp.where(place == lax.broadcasted_iota(jnp.int32, (buckets, 2 * slots), 0), 1.0, 0.0)
    rows = jnp.concatenate([own_ref[0:slots], got_ref[0:slots]], axis=0)
    packed = dot(pick, rows)
    for q in range(8):
        scratch[q] = packed[:, q * 128 : (q + 1) * 128]
    lines = jnp.sum(pick * line.astype(jnp.float32), axis=1, keepdims=True)
    bucket = lax.broadcasted_iota(jnp.int32, (buckets, 128), 0)
    lane = lax.broadcasted_iota(jnp.int32, (buckets, 128), 1)
    spots = jnp.where(lane % ranks == bucket % ranks, lines, 0.0)
    i = lax.broadcasted_iota(jnp.int32, (chips, buckets), 0)
    j = lax.broadcasted_iota(jnp.int32, (chips, buckets), 1)
    target = lax.bitwise_xor(i, jnp.full(i.shape, chip, jnp.int32)) if apart else i
    numbers = dot(jnp.where(target // 2 == j // ranks, 1.0, 0.0), spots)
    spot = lax.broadcasted_iota(jnp.int32, (chips, 128), 0) if apart else chip
    lane = lax.broadcasted_iota(jnp.int32, (chips, 128), 1)
    numbers = jnp.where(lane // ranks == spot % (128 // ranks), numbers, 0.0)
    for k in range(chips):
        out = out_refs[k] if apart else out_refs[0].at[k]
        target = lax.bitwise_xor(chip, k) if apart else k
        block, pair = (lax.div(target, 2), lax.rem(target, 2)) if apart else (k // 2, k % 2)
        for q in range(4):
            start = block * ranks
            start = pl.multiple_of(start, ranks) if apart else start
            out[q * ranks : (q + 1) * ranks] = scratch[4 * pair + q, pl.ds(start, ranks)]
        out[4 * ranks :] = jnp.broadcast_to(numbers[k : k + 1], (8, 128))


def message_order(chips):
    half = chips // 2
    return [0, 1, *range(half + 2, chips), half, half + 1, *range(2, half)]


def density_kernel(*refs):
    first_ref, second_ref = refs[:2]
    f_ref, straight_ref, across_ref, b1, half = refs[-5:]
    pieces = refs[2:-5]
    pair, side, _ = place_in_grid()
    planes, _, lines, depth = f_ref.shape
    sources = lax.axis_size("grid") // 2
    height = pieces[0].shape[-2]
    ranks = (height - 8) // 4
    group = 128 // ranks

    def received(source, start, stop):
        if len(pieces) > 1:
            return pieces[message_order(sources).index(source)][start:stop]
        return pieces[0][source, start:stop]

    added = [None, None]
    for first in range(0, sources, group):
        members = range(first, min(first + group, sources))
        numbers = sum(received(k, 4 * ranks, 4 * ranks + 1) for k in members)
        line = lax.broadcasted_iota(jnp.int32, (planes * lines, 128), 0)
        spread = jnp.where(line == numbers.astype(jnp.int32) - 1, 1.0, 0.0)
        for part in range(2):
            values = jnp.concatenate(
                [
                    jnp.concatenate(
                        [received(k, q * ranks, (q + 1) * ranks) for k in members], axis=0
                    )
                    for q in (2 * part, 2 * part + 1)
                ],
                axis=1,
            )
            value = dot(spread[:, : len(members) * ranks], values)
            added[part] = value if added[part] is None else added[part] + value
    for x in range(planes):
        for part in range(2):
            f_ref[x, part] = added[part][x * lines : (x + 1) * lines]
    thick = planes // 2
    for x in range(thick):
        for part in range(2):
            f_ref[pair * thick + x, part] += first_ref[part, x]
            f_ref[(1 - pair) * thick + x, part] += second_ref[part, x]

    def density(x, part):
        return f_ref[x, part] if 0 <= x < planes else None

    def once(x, part):
        return b1[x + 2, part] if -2 <= x < planes + 2 else None

    def outer(base, first_plane, one):
        for x in range(one, one + 4):
            for part in range(2):
                b1[x + 2, part] = smooth_fine(density, x, part)
        for i in range(2):
            for part in range(2):
                x = base + 2 * i
                total = smooth_fine(once, x, part) + smooth_fine(once, x + 1, part)
                for h in range(2):
                    half[(2 * i + part) * 2 + h] = total[:, h * 128 : (h + 1) * 128]
        for r, value in enumerate(lowered(half, 4, lines, depth)):
            straight_ref[8 + r // 2, r % 2 * 16 : r % 2 * 16 + 16] = value
        for x in range(2):
            for part in range(2):
                for h in range(2):
                    straight_ref[(2 * x + part) * 2 + h] = f_ref[
                        first_plane + x, part, :, h * 128 : (h + 1) * 128
                    ]
        other = planes - 2 - first_plane
        for x in range(2):
            across_ref[x] = f_ref[other + x]

    @pl.when(side == 0)
    def _():
        outer(-4, 0, -2)

    @pl.when(side == 1)
    def _():
        outer(planes, planes - 2, planes - 2)


def lowered(half, rows, lines, depth):
    matrix = pair_matrix(depth, depth // 2, 0.125)
    total = None
    for h in range(2):
        stacked = jnp.concatenate(
            [
                half[2 * r + h, pl.ds(0, lines // 2, 2)] + half[2 * r + h, pl.ds(1, lines // 2, 2)]
                for r in range(rows)
            ],
            axis=0,
        )
        value = dot(stacked, matrix[h * 128 : (h + 1) * 128])
        total = value if total is None else total + value
    return [total[r * lines // 2 : (r + 1) * lines // 2] for r in range(rows)]


def source_kernel(even_ref, odd_ref, straight_ref, f_ref, cs_ref, s_ref, ext, b1, half):
    blocks = lax.axis_size("grid") // 4
    pair, side, block = place_in_grid()
    cosine, sine = cs_ref[pair], cs_ref[2 + pair]
    planes = f_ref.shape[0]
    lines, depth = f_ref.shape[2:]
    first, last = block == 0, block == blocks - 1
    low = (jnp.where(first, cosine, 1.0), jnp.where(first, -sine, 0.0))
    high = (jnp.where(last, cosine, 1.0), jnp.where(last, sine, 0.0))

    @pl.when(side == 0)
    def _():
        place_planes(ext, 0, odd_ref, *low)
        ext[planes : 2 * planes] = f_ref[...]
        ext[2 * planes : 3 * planes] = even_ref[...]
        ext[3 * planes :] = jnp.zeros((planes, 2, lines, depth), jnp.float32)

    @pl.when(side == 1)
    def _():
        ext[:planes] = jnp.zeros((planes, 2, lines, depth), jnp.float32)
        ext[planes : 2 * planes] = even_ref[...]
        ext[2 * planes : 3 * planes] = f_ref[...]
        place_planes(ext, 3 * planes, odd_ref, *high)

    for x in range(2 * planes + 4):
        for part in range(2):
            b1[x, part] = smooth_fine(lambda i, p: ext[i, p], x + planes - 2, part)
    for i in range(planes):
        for part in range(2):
            total = smooth_fine(lambda i, p: b1[i, p], 2 * i + 2, part) + smooth_fine(
                lambda i, p: b1[i, p], 2 * i + 3, part
            )
            for h in range(2):
                half[(2 * i + part) * 2 + h] = total[:, h * 128 : (h + 1) * 128]
    for r, value in enumerate(lowered(half, 2 * planes, lines, depth)):
        s_ref[r // 2, r % 2] = value

    def add(base, c, t):
        for x in range(2):
            real, imag = rotated(straight_ref[8 + x, 0:16], straight_ref[8 + x, 16:32], c, t)
            s_ref[base + x, 0] += real
            s_ref[base + x, 1] += imag

    @pl.when(side == 0)
    def _():
        add(2, *high)

    @pl.when(side == 1)
    def _():
        add(0, *low)


def fine_kernel(
    even_ref, odd_ref, straight_ref, across_ref, f_ref, cs_ref, first_ref, second_ref, ext, b1, b2, g
):
    blocks = lax.axis_size("grid") // 4
    pair, side, block = place_in_grid()
    cosine, sine = cs_ref[pair], cs_ref[2 + pair]
    planes = f_ref.shape[0]
    place_halo(ext, planes + 2, even_ref, odd_ref, cs_ref)
    ext[planes + 2 : 2 * planes + 2] = f_ref[...]
    first, last = block == 0, block == blocks - 1
    low = (jnp.where(first, cosine, 1.0), jnp.where(first, -sine, 0.0))
    high = (jnp.where(last, cosine, 1.0), jnp.where(last, sine, 0.0))

    def place_straight(base, c, t):
        for x in range(2):
            real, imag = [
                jnp.concatenate([straight_ref[4 * x + 2 * p], straight_ref[4 * x + 2 * p + 1]], axis=1)
                for p in range(2)
            ]
            ext[base + x, 0], ext[base + x, 1] = rotated(real, imag, c, t)

    @pl.when(side == 0)
    def _():
        place_planes(ext, 0, across_ref, *low)
        place_straight(3 * planes + 2, *high)

    @pl.when(side == 1)
    def _():
        place_straight(0, *low)
        place_planes(ext, 3 * planes + 2, across_ref, *high)

    for x in range(planes + 8):
        for part in range(2):
            b1[x, part] = smooth_fine(lambda i, p: ext[i, p], x + 2, part)
    for x in range(planes + 4):
        for part in range(2):
            b2[x, part] = smooth_fine(lambda i, p: b1[i, p], x + 2, part)
    for x in range(planes):
        for part in range(2):
            b3 = smooth_fine(lambda i, p: b2[i, p], x + 2, part)
            g[x, part] = fine_scale * (f_ref[x, part] + b1[x + 4, part] + b2[x + 2, part] + b3)
    half = planes // 2
    for x in range(half):
        first_ref[x] = g[pair * half + x]
        second_ref[x] = g[(1 - pair) * half + x]


def shift_z(v, step):
    width = v.shape[-1] // 2
    lane = lax.broadcasted_iota(jnp.int32, v.shape, len(v.shape) - 1)
    edge = 0 if step > 0 else width - 1
    inner = roll(v, step, 1)
    outer = roll(v, step + (width if step > 0 else -width), 1)
    return jnp.where(lane % width == edge, outer, inner)


def packed_sweep(values, count, depth, source, target, cosine, sine, residual=False):
    rate, near_rate = level_numbers(depth)
    values[0] = cosine * values[count] - sine * roll(values[count], 64, 1)
    values[count + 1] = cosine * values[1] + sine * roll(values[1], 64, 1)

    def body(x):
        v = values[x + 1]
        near = values[x] + values[x + 2]
        near = near + (roll(v, 1, 0) + roll(v, -1, 0))
        near = near + (shift_z(v, 1) + shift_z(v, -1))
        if residual:
            target[x] = source[x] - omega / rate * v + near_rate / rate * near
        else:
            target[x + 1] = rate * source[x] + keep * v + near_rate * near

    each(count, body)


def first_sweep(values, count, depth, source):
    rate, _ = level_numbers(depth)

    def body(x):
        values[x + 1] = rate * source[x]

    each(count, body)


def cycle_kernel(*refs):
    radix = len(refs) - 14
    pieces, refs = refs[:radix], refs[radix:]
    cs_ref, own_ref, send_ref, s, u, v, r1, s2, u2, v2, r2, s3, u3, v3 = refs
    position = lax.axis_index("grid")
    pair, _, block = place_in_grid()
    count = s.shape[0]
    rate, near_rate = level_numbers(1)
    cosine, sine = cs_ref[pair], cs_ref[2 + pair]
    lane = lax.broadcasted_iota(jnp.int32, (8, 128), 1)
    lane_sine = jnp.where(lane < 64, -sine, sine)

    length = count // radix
    digit = lax.div(block, length // 4)
    for k, piece in enumerate(pieces):
        s[pl.ds(lax.bitwise_xor(lax.rem(digit, radix), k) * length, length)] = piece[...]

    def sweep(values, target, residual=False):
        values[0, 0], values[0, 1] = rotated(values[count, 0], values[count, 1], cosine, -sine)
        values[count + 1, 0], values[count + 1, 1] = rotated(
            values[1, 0], values[1, 1], cosine, sine
        )

        def body(x):
            for f in range(2):
                a = values[x + 1, f]
                near = values[x, f] + values[x + 2, f]
                near = near + (roll(a, 1, 0) + roll(a, -1, 0))
                near = near + (roll(a, 1, 1) + roll(a, -1, 1))
                if residual:
                    target[x, f] = s[x, f] - omega / rate * a + near_rate / rate * near
                else:
                    target[x + 1, f] = rate * s[x, f] + keep * a + near_rate * near

        each(count, body)

    def start(x):
        for f in range(2):
            u[x + 1, f] = rate * s[x, f]

    each(count, start)
    sweep(u, v)
    sweep(v, r1, residual=True)

    count2 = count // 2
    i = lax.broadcasted_iota(jnp.int32, (128, 128), 0)
    j = lax.broadcasted_iota(jnp.int32, (128, 128), 1)
    rows = []
    for f in range(2):

        def lower(x):
            r1[2 * x, f] = r1[2 * x, f] + r1[2 * x + 1, f]
            r2[x, 8 * f : 8 * f + 8] = r1[2 * x, f, pl.ds(0, 8, 2)] + r1[2 * x, f, pl.ds(1, 8, 2)]

        each(count2, lower)
        rows.append(r2[:, 8 * f : 8 * f + 8].reshape(count2 * 8, 128))
    lowered = sum(
        dot(rows[f], jnp.where(i // 2 + 64 * f == j, 0.125, 0.0)) for f in range(2)
    )
    s2[...] = lowered.reshape(count2, 8, 128)
    first_sweep(u2, count2, 2, s2)
    packed_sweep(u2, count2, 2, s2, v2, cosine, lane_sine)
    packed_sweep(v2, count2, 2, s2, u2, cosine, lane_sine, residual=True)

    count3 = count2 // 2

    def lower3(x):
        total = u2[2 * x] + u2[2 * x + 1]
        r2[x, 0:8] = total
        r2[x, 8:16] = total
        s3[x] = r2[x, pl.ds(0, 8, 2)] + r2[x, pl.ds(1, 8, 2)]

    each(count3, lower3)
    same = i // 64 == j // 64
    lowered = dot(
        s3[...].reshape(count3 * 8, 128), jnp.where(same & (i % 64 // 2 == j % 32), 0.125, 0.0)
    )
    s3[...] = lowered.reshape(count3, 8, 128)
    first_sweep(u3, count3, 3, s3)
    a, b = u3, v3
    for _ in range(5):
        packed_sweep(a, count3, 3, s3, b, cosine, lane_sine)
        a, b = b, a

    raised = dot(
        a[1 : count3 + 1].reshape(count3 * 8, 128),
        jnp.where(same & (i % 64 == j % 64 // 2), 1.0, 0.0),
    )
    s3[...] = raised.reshape(count3, 8, 128)

    def raise3(x):
        r2[x, pl.ds(0, 8, 2)] = s3[x]
        r2[x, pl.ds(1, 8, 2)] = s3[x]
        for k in range(2):
            v2[2 * x + k + 1] = v2[2 * x + k + 1] + r2[x, 0:8]

    each(count3, raise3)
    packed_sweep(v2, count2, 2, s2, u2, cosine, lane_sine)
    packed_sweep(u2, count2, 2, s2, v2, cosine, lane_sine)

    rows = v2[1 : count2 + 1].reshape(count2 * 8, 128)
    for f in range(2):
        raised = dot(rows, jnp.where(i == j // 2 + 64 * f, 1.0, 0.0))
        s2[...] = raised.reshape(count2, 8, 128)

        def raise2(x):
            r1[x, f, pl.ds(0, 8, 2)] = s2[x]
            r1[x, f, pl.ds(1, 8, 2)] = s2[x]
            for k in range(2):
                v[2 * x + k + 1, f] = v[2 * x + k + 1, f] + r1[x, f]

        each(count2, raise2)
    sweep(v, u)
    sweep(u, v)

    for target, tile in ((own_ref, position), (send_ref, position + 2 - 4 * pair)):
        for k in range(5):
            q = tile + k - 2
            low, high = q < 0, q >= count
            q = jnp.where(low, q + count, jnp.where(high, q - count, q))
            c = jnp.where(low | high, cosine, 1.0)
            t = jnp.where(low, -sine, jnp.where(high, sine, 0.0))
            target[k, 0], target[k, 1] = rotated(v[q + 1, 0], v[q + 1, 1], c, t)


def correct(w_ref, pair, first_ref, second_ref, e, b1, store):
    own = place_in_grid()[1] == pair
    lines = w_ref.shape[2]
    wide = dot(w_ref[...].reshape(10 * lines, 128), spread_matrix(128, 256))
    for r in range(10):
        for h in range(2):
            value = wide[r * lines : (r + 1) * lines, 128 * h : 128 * (h + 1)]
            e[2 * r + h, pl.ds(0, lines, 2)] = value
            e[2 * r + h, pl.ds(1, lines, 2)] = value

    def expanded(x, f):
        place = (2 * (x // 2) + f) * 2
        return jnp.concatenate([e[place], e[place + 1]], axis=1)

    for x in range(6):
        for f in range(2):
            b1[x, f] = smooth_fine(expanded, x + 2, f)
    for x in range(2):
        for f in range(2):
            g = jnp.where(own, first_ref[x, f], second_ref[x, f])
            store(f, x, g + smooth_fine(lambda i, g: b1[i, g], x + 2, f))


def own_kernel(w_ref, first_ref, second_ref, out_ref, e, b1):
    def store(part, x, value):
        out_ref[part, x] = value

    correct(w_ref, place_in_grid()[0], first_ref, second_ref, e, b1, store)


def output_kernel(own_ref, w_ref, first_ref, second_ref, out_ref, e, b1):
    pair = place_in_grid()[0]
    out_ref[pair] = own_ref[...]

    def store(part, x, value):
        out_ref[1 - pair, part, x] = value

    correct(w_ref, 1 - pair, first_ref, second_ref, e, b1, store)


def pair_phases(pair_table, k_fraction):
    kcount = k_fraction.shape[0]
    picks = pair_table[:, :, None] == jnp.arange(kcount, dtype=jnp.int32)[None, None, :]
    chosen = jnp.sum(jnp.where(picks, k_fraction[None, None, :], 0.0), axis=2)
    angle = 6.283185307179586 * (chosen[:, 0] - chosen[:, 1])
    return jnp.concatenate([jnp.cos(angle), jnp.sin(angle)])


def gather_blocks(value, blocks, block, permute_block):
    stride = 1
    while True:
        radix = min(4, blocks // stride)
        digit = block // stride % radix
        pieces = [value] + [
            permute_block(value, lambda b, k=k: b ^ k * stride) for k in range(1, radix)
        ]
        stride *= radix
        if stride == blocks:
            return pieces
        stacked = jnp.stack(pieces)[jnp.arange(radix) ^ digit]
        value = stacked.reshape(-1, *value.shape[1:])


def vmem(count):
    return [pl.BlockSpec(memory_space=pltpu.VMEM)] * count


smem = [pl.BlockSpec(memory_space=pltpu.SMEM)]


def call(kernel, out_shape, in_specs, scratch, flops):
    single = not isinstance(out_shape, (list, tuple))
    return pl.pallas_call(
        kernel,
        out_shape=out_shape,
        in_specs=in_specs,
        out_specs=vmem(1)[0] if single else vmem(len(out_shape)),
        scratch_shapes=[
            pltpu.VMEM(shape, jnp.float32) if isinstance(shape, tuple) else shape
            for shape in scratch
        ],
        compiler_params=pltpu.CompilerParams(vmem_limit_bytes=48 * 2**20),
        cost_estimate=pl.CostEstimate(flops=flops, bytes_accessed=2**20, transcendentals=0),
    )


def shaped(*shape):
    return jax.ShapeDtypeStruct(shape, jnp.float32)


def per_device(
    pair_density, moments, shapes, slot_atom, slot_tile, slot_row, pair_table, k_fraction
):
    tile_count = lax.axis_size("grid")
    chips, blocks = tile_count // 2, tile_count // 4
    position = lax.axis_index("grid")
    core, block = position % 2, position // 4
    _, _, thick, lines, depth = pair_density.shape
    planes = 2 * thick
    slot_count = shapes.shape[0]
    capacity = max(2, 2 * slot_count // tile_count)
    devices = range(tile_count)

    def permute(value, target):
        return lax.ppermute(value, "grid", [(i, target(i)) for i in devices])

    def permute_block(value, target):
        return permute(value, lambda i: target(i // 4) * 4 + i % 4)

    def within_block(move):
        return lambda i: i // 4 * 4 + 2 * move(i // 2 % 2, i % 2)[0] + move(i // 2 % 2, i % 2)[1]

    def other_half(i):
        return i ^ 1

    def next_half(i):
        return (i + (3 if i % 2 else -3)) % tile_count

    def next_block(i):
        return (i + (4 if i % 2 else -4)) % tile_count

    def block_behind(i):
        return (i + (-4 if i % 2 else 4)) % tile_count

    cs = pair_phases(pair_table, k_fraction)

    first = permute(
        lax.dynamic_index_in_dim(pair_density, core, 0, False), within_block(lambda h, c: (c, h))
    )
    second = permute(
        lax.dynamic_index_in_dim(pair_density, 1 - core, 0, False),
        within_block(lambda h, c: (1 - c, h)),
    )
    rows = call(
        rows_kernel,
        shaped(slot_count + 8, 4 * depth),
        vmem(1) + [pl.BlockSpec(memory_space=pltpu.HBM)] + vmem(3),
        [(shapes.shape[1], slot_count, depth), pltpu.SemaphoreType.DMA((5,))],
        10**7,
    )(
        moments,
        shapes.transpose(1, 0, 2),
        slot_atom.reshape(1, -1),
        slot_tile.reshape(1, -1),
        slot_row.reshape(1, -1),
    )
    got = permute(rows, other_half)
    apart = chips <= 8
    height = 16 * capacity + 8
    packed = call(
        pack_kernel,
        [shaped(height, 128)] * chips if apart else [shaped(chips, height, 128)],
        vmem(2),
        [(8, 4 * capacity * blocks, 128)],
        10**8,
    )(rows, got)
    if apart:
        received = [
            permute(packed[k], lambda i, k=k: i ^ (2 * k)) if k else packed[k]
            for k in message_order(chips)
        ]
    else:
        groups = [[2 * k + c for k in range(chips)] for c in range(2)]
        received = [
            lax.all_to_all(
                packed[0], "grid", split_axis=0, concat_axis=0, axis_index_groups=groups, tiled=True
            )
        ]

    full = (2, lines, depth)
    small = (2, lines // 2, depth // 2)
    f, straight, across = call(
        density_kernel,
        [shaped(planes, *full), shaped(10, lines, 128), shaped(2, *full)],
        vmem(2 + len(received)),
        [(planes + 4, *full), (8, lines, 128)],
        10**8,
    )(first, second, *received)
    even = permute(f, other_half)
    odd = permute(f, next_half)
    straight = permute(straight, next_block)
    across = permute(across, block_behind)
    source = call(
        source_kernel,
        shaped(planes, *small),
        vmem(4) + smem,
        [(4 * planes, *full), (2 * planes + 4, *full), (4 * planes, lines, 128)],
        10**7,
    )(even, odd, straight, f, cs)
    pieces = gather_blocks(source, blocks, block, permute_block)
    first, second = call(
        fine_kernel,
        [shaped(thick, *full)] * 2,
        vmem(5) + smem,
        [(3 * planes + 4, *full), (planes + 8, *full), (planes + 4, *full), (planes, *full)],
        10**7,
    )(even, odd, straight, across, f, cs)
    first = permute(first, within_block(lambda h, c: (c, h)))
    second = permute(second, within_block(lambda h, c: (c, 1 - h)))

    n1, n2, n3 = tile_count, tile_count // 2, tile_count // 4
    tile = (8, 128)
    w_own, w_send = call(
        cycle_kernel,
        [shaped(5, *small)] * 2,
        vmem(len(pieces)) + smem,
        [
            (n1, *small),
            (n1 + 2, *small),
            (n1 + 2, *small),
            (n1, *small),
            (n2, *tile),
            (n2 + 2, *tile),
            (n2 + 2, *tile),
            (n2, 16, 128),
            (n3, *tile),
            (n3 + 2, *tile),
            (n3 + 2, *tile),
        ],
        10**8,
    )(*pieces, cs)
    w_got = permute(w_send, lambda i: i ^ 2)
    scratch = [(20, lines, 128), (6, *full)]
    result = call(own_kernel, shaped(2, thick, lines, depth), vmem(3), scratch, 10**7)(
        w_own, first, second
    )
    return call(output_kernel, shaped(*pair_density.shape), vmem(4), scratch, 10**7)(
        result, w_got, first, second
    )


def solution(mesh):
    return jax.shard_map(
        per_device,
        mesh=mesh,
        in_specs=(
            P("rep", None, "grid", None, None),
            P(("rep", "grid"), None, None, None),
            P(("rep", "grid"), None, None),
            P(("rep", "grid")),
            P(("rep", "grid"), None),
            P(("rep", "grid")),
            P(),
            P(),
        ),
        out_specs=P("rep", None, "grid", None, None),
        check_vma=False,
    )
```

```python
import jax
import jax.numpy as jnp
from jax import lax
from jax.experimental import pallas as pl
from jax.experimental.pallas import tpu as pltpu
from jax.sharding import PartitionSpec as P

omega = 0.8
screen = 0.05
highest = lax.Precision.HIGHEST

fine_diagonal = 7.5 + screen
fine_scale = omega / fine_diagonal
fine_near = fine_scale * 4.0 / 3.0
fine_far = fine_scale / 12.0
keep = 1.0 - omega


def level_numbers(depth):
    quarter = 1.0 / 4**depth
    diagonal = 6.0 * quarter + screen
    return omega / diagonal, omega / diagonal * quarter


def each(count, body, most=16):
    if count <= most:
        for i in range(count):
            body(i)
    else:
        pl.loop(0, count, unroll=4)(body)


def dot(a, b):
    return jnp.dot(a, b, precision=highest, preferred_element_type=jnp.float32)


def pair_matrix(rows, columns, value):
    i = lax.broadcasted_iota(jnp.int32, (rows, columns), 0)
    j = lax.broadcasted_iota(jnp.int32, (rows, columns), 1)
    return jnp.where(i // 2 == j, value, 0.0)


def spread_matrix(rows, columns):
    i = lax.broadcasted_iota(jnp.int32, (rows, columns), 0)
    j = lax.broadcasted_iota(jnp.int32, (rows, columns), 1)
    return jnp.where(i == j // 2, 1.0, 0.0)


def roll(v, shift, axis):
    return pltpu.roll(v, shift % v.shape[axis], axis)


def smooth_fine(at, x, f):
    total = None
    for step, weight in ((1, fine_near), (2, -fine_far)):
        sides = [p for p in (at(x - step, f), at(x + step, f)) if p is not None]
        v = at(x, f)
        if v is not None:
            for axis in (0, 1):
                sides.append(roll(v, step, axis) + roll(v, -step, axis))
            if step == 1:
                total = keep * v
        if sides:
            part = weight * sum(sides[1:], sides[0])
            total = part if total is None else total + part
    return total


def rotated(real, imag, cosine, sine):
    return cosine * real - sine * imag, sine * real + cosine * imag


def place_planes(target, base, source, cosine, sine):
    for x in range(source.shape[0]):
        real, imag = rotated(source[x, 0], source[x, 1], cosine, sine)
        target[base + x, 0] = real
        target[base + x, 1] = imag


def place_halo(ext, middle, even_ref, odd_ref, cs_ref):
    position = lax.axis_index("grid")
    chips = lax.axis_size("grid") // 2
    core, chip = lax.rem(position, 2), lax.div(position, 2)
    cosine, sine = cs_ref[core], cs_ref[2 + core]
    first, last = chip == 0, chip == chips - 1
    low = (jnp.where(first, cosine, 1.0), jnp.where(first, -sine, 0.0))
    high = (jnp.where(last, cosine, 1.0), jnp.where(last, sine, 0.0))
    planes = even_ref.shape[0]
    parity = lax.rem(chip, 2)

    @pl.when(parity == 0)
    def _():
        place_planes(ext, middle - planes, odd_ref, *low)
        place_planes(ext, middle + planes, even_ref, *high)

    @pl.when(parity == 1)
    def _():
        place_planes(ext, middle - planes, even_ref, *low)
        place_planes(ext, middle + planes, odd_ref, *high)


def as_column(row):
    n = row.shape[1]
    i = lax.broadcasted_iota(jnp.int32, (n, n), 0)
    j = lax.broadcasted_iota(jnp.int32, (n, n), 1)
    return jnp.sum(jnp.where(i == j, row, 0.0), axis=1, keepdims=True)


def rows_kernel(moments_ref, shapes_ref, slots_ref, keep_ref, send_ref, rows):
    core = lax.rem(lax.axis_index("grid"), 2)
    channels, slots, depth = shapes_ref.shape
    atoms = moments_ref.shape[0]
    atom = as_column(slots_ref[0:1].astype(jnp.float32))
    picks = [jnp.where(atom == float(a), 1.0, 0.0) for a in range(atoms)]
    chosen = []
    for f in range(4):
        total = None
        for a in range(atoms):
            value = picks[a] * moments_ref[a, f // 2, f % 2 : f % 2 + 1]
            total = value if total is None else total + value
        chosen.append(total)
    for i in range(slots // 8):
        near = slice(8 * i, 8 * i + 8)
        totals = [None] * 4
        for channel in range(channels):
            shape = shapes_ref[channel, near]
            for f in range(4):
                value = chosen[f][near, channel : channel + 1] * shape
                totals[f] = value if totals[f] is None else totals[f] + value
        for f in range(4):
            rows[f // 2, near, f % 2 * depth : (f % 2 + 1) * depth] = totals[f]
    keep_ref[...] = rows[core]
    send_ref[0:slots] = rows[1 - core]
    send_ref[slots:] = jnp.zeros((8, 2 * depth), jnp.float32)
    number = (slots_ref[1:2] * 64 + slots_ref[2:3]).astype(jnp.float32)
    send_ref[slots : slots + 1, 0:slots] = number


def pack_kernel(own_ref, got_ref, slots_ref, _, *out_refs):
    slots = own_ref.shape[0]
    apart = len(out_refs) > 1
    height = out_refs[0].shape[-2]
    ranks = (height - 8) // 4
    capacity = ranks // 4
    chips = lax.axis_size("grid") // 2
    chip = lax.div(lax.axis_index("grid"), 2)
    number = (slots_ref[1:2] * 64 + slots_ref[2:3]).astype(jnp.float32)
    number = jnp.concatenate([number, got_ref[slots : slots + 1, 0:slots]], axis=1).astype(jnp.int32)
    tile, line = number // 64, number % 128 + 1
    column = as_column(tile.astype(jnp.float32)).astype(jnp.int32)
    i = lax.broadcasted_iota(jnp.int32, (2 * slots, 2 * slots), 0)
    j = lax.broadcasted_iota(jnp.int32, (2 * slots, 2 * slots), 1)
    ahead = jnp.where((column == tile) & (i < j) & (i // slots == j // slots), 1.0, 0.0)
    rank = jnp.sum(ahead, axis=0, keepdims=True).astype(jnp.int32)
    device = lax.broadcasted_iota(jnp.int32, (1, 2 * slots), 1) // slots
    place = tile // 2 * ranks + (2 * device + tile % 2) * capacity + rank
    r = lax.broadcasted_iota(jnp.int32, (ranks, 2 * slots), 0)
    targets = [lax.bitwise_xor(chip, k) if apart else k for k in range(chips)]
    pick = jnp.concatenate([jnp.where(place == r + target * ranks, 1.0, 0.0) for target in targets])
    rows = jnp.concatenate([own_ref[...], got_ref[0:slots]], axis=0)
    packed = dot(pick, rows)
    lines = jnp.sum(pick * line.astype(jnp.float32), axis=1, keepdims=True)
    bucket = lax.broadcasted_iota(jnp.int32, (chips * ranks, 128), 0)
    lane = lax.broadcasted_iota(jnp.int32, (chips * ranks, 128), 1)
    spot = bucket // ranks if apart else chip
    spots = jnp.where(lane == spot % (128 // ranks) * ranks + bucket % ranks, lines, 0.0)
    i = lax.broadcasted_iota(jnp.int32, (chips, chips * ranks), 0)
    j = lax.broadcasted_iota(jnp.int32, (chips, chips * ranks), 1)
    numbers = dot(jnp.where(i == j // ranks, 1.0, 0.0), spots)
    for k in range(chips):
        out = out_refs[k] if apart else out_refs[0].at[k]
        for q in range(4):
            out[q * ranks : (q + 1) * ranks] = packed[
                k * ranks : (k + 1) * ranks, q * 128 : (q + 1) * 128
            ]
        out[4 * ranks :] = jnp.broadcast_to(numbers[k : k + 1], (8, 128))


def message_order(chips):
    half = chips // 2
    return [0, 1, *range(half + 2, chips), half, half + 1, *range(2, half)]


def density_kernel(*refs):
    pd_ref, other_ref = refs[:2]
    f_ref, inner_ref, outer_ref, b1, half = refs[-5:]
    pieces = refs[2:-5]
    position = lax.axis_index("grid")
    core, side = lax.rem(position, 2), lax.rem(lax.div(position, 2), 2)
    planes, _, lines, depth = f_ref.shape
    sources = lax.axis_size("grid") // 2
    height = pieces[0].shape[-2]
    ranks = (height - 8) // 4
    group = 128 // ranks

    def received(source, start, stop):
        if len(pieces) > 1:
            return pieces[message_order(sources).index(source)][start:stop]
        return pieces[0][source, start:stop]

    added = [None, None]
    for first in range(0, sources, group):
        members = range(first, min(first + group, sources))
        numbers = sum(received(k, 4 * ranks, 4 * ranks + 1) for k in members)
        line = lax.broadcasted_iota(jnp.int32, (planes * lines, 128), 0)
        spread = jnp.where(line == numbers.astype(jnp.int32) - 1, 1.0, 0.0)
        for part in range(2):
            values = jnp.concatenate(
                [
                    jnp.concatenate(
                        [received(k, q * ranks, (q + 1) * ranks) for k in members], axis=0
                    )
                    for q in (2 * part, 2 * part + 1)
                ],
                axis=1,
            )
            value = dot(spread[:, : len(members) * ranks], values)
            added[part] = value if added[part] is None else added[part] + value
    for x in range(planes):
        for part in range(2):
            f_ref[x, part] = added[part][x * lines : (x + 1) * lines]
    thick = planes // 2
    for x in range(thick):
        for part in range(2):
            f_ref[core * thick + x, part] += pd_ref[core, part, x]
            f_ref[(1 - core) * thick + x, part] += other_ref[part, x]

    def density(x, part):
        return f_ref[x, part] if 0 <= x < planes else None

    def once(x, part):
        return b1[x + 2, part] if -2 <= x < planes + 2 else None

    for x in range(-2, planes + 2):
        for part in range(2):
            b1[x + 2, part] = smooth_fine(density, x, part)
    rows = (planes + 8) // 2 * 2
    for i in range(rows // 2):
        for part in range(2):
            total = smooth_fine(once, 2 * i - 4, part) + smooth_fine(once, 2 * i - 3, part)
            for h in range(2):
                half[(2 * i + part) * 2 + h] = total[:, h * 128 : (h + 1) * 128]
    coarse = lowered(half, rows, lines, depth)

    @pl.when(side == 0)
    def _():
        for r in range(8):
            inner_ref[r // 2, r % 2] = coarse[4 + r]
        for r in range(4):
            outer_ref[r // 2, r % 2] = coarse[r]

    @pl.when(side == 1)
    def _():
        for r in range(8):
            inner_ref[r // 2, r % 2] = coarse[r]
        for r in range(4):
            outer_ref[r // 2, r % 2] = coarse[8 + r]


def lowered(half, rows, lines, depth):
    matrix = pair_matrix(depth, depth // 2, 0.125)
    total = None
    for h in range(2):
        stacked = jnp.concatenate(
            [
                half[2 * r + h, pl.ds(0, lines // 2, 2)] + half[2 * r + h, pl.ds(1, lines // 2, 2)]
                for r in range(rows)
            ],
            axis=0,
        )
        value = dot(stacked, matrix[h * 128 : (h + 1) * 128])
        total = value if total is None else total + value
    return [total[r * lines // 2 : (r + 1) * lines // 2] for r in range(rows)]


def source_kernel(own_ref, partner_ref, straight_ref, across_ref, cs_ref, _, s_ref, __):
    position = lax.axis_index("grid")
    blocks = lax.axis_size("grid") // 4
    core, side, block = lax.rem(position, 2), lax.rem(lax.div(position, 2), 2), lax.div(position, 4)
    cosine, sine = cs_ref[core], cs_ref[2 + core]
    first, last = block == 0, block == blocks - 1
    low = (jnp.where(first, cosine, 1.0), jnp.where(first, -sine, 0.0))
    high = (jnp.where(last, cosine, 1.0), jnp.where(last, sine, 0.0))

    def total(low_ref, high_ref):
        for x in range(4):
            source, (c, s) = (low_ref, low) if x < 2 else (high_ref, high)
            real, imag = rotated(source[x % 2, 0], source[x % 2, 1], c, s)
            s_ref[x, 0] = own_ref[x, 0] + partner_ref[x, 0] + real
            s_ref[x, 1] = own_ref[x, 1] + partner_ref[x, 1] + imag

    @pl.when(side == 0)
    def _():
        total(across_ref, straight_ref)

    @pl.when(side == 1)
    def _():
        total(straight_ref, across_ref)


def fine_kernel(
    even_ref, odd_ref, after_ref, before_ref, f_ref, cs_ref, _, own_ref, send_ref, ext, b1, b2, g
):
    position = lax.axis_index("grid")
    chips = lax.axis_size("grid") // 2
    core, chip = lax.rem(position, 2), lax.div(position, 2)
    cosine, sine = cs_ref[core], cs_ref[2 + core]
    planes = f_ref.shape[0]
    place_halo(ext, planes + 2, even_ref, odd_ref, cs_ref)
    ext[planes + 2 : 2 * planes + 2] = f_ref[...]
    first, last = chip < 2, chip >= chips - 2
    place_planes(
        ext, 0, before_ref, jnp.where(first, cosine, 1.0), jnp.where(first, -sine, 0.0)
    )
    place_planes(
        ext,
        3 * planes + 2,
        after_ref,
        jnp.where(last, cosine, 1.0),
        jnp.where(last, sine, 0.0),
    )
    for x in range(planes + 8):
        for part in range(2):
            b1[x, part] = smooth_fine(lambda i, p: ext[i, p], x + 2, part)
    for x in range(planes + 4):
        for part in range(2):
            b2[x, part] = smooth_fine(lambda i, p: b1[i, p], x + 2, part)
    for x in range(planes):
        for part in range(2):
            b3 = smooth_fine(lambda i, p: b2[i, p], x + 2, part)
            g[x, part] = fine_scale * (f_ref[x, part] + b1[x + 4, part] + b2[x + 2, part] + b3)
    half = planes // 2
    for x in range(half):
        own_ref[x] = g[core * half + x]
        send_ref[x] = g[(1 - core) * half + x]


def gate_kernel(*_):
    pass


def shift_z(v, step):
    width = v.shape[-1] // 2
    lane = lax.broadcasted_iota(jnp.int32, v.shape, len(v.shape) - 1)
    edge = 0 if step > 0 else width - 1
    inner = roll(v, step, 1)
    outer = roll(v, step + (width if step > 0 else -width), 1)
    return jnp.where(lane % width == edge, outer, inner)


def packed_sweep(values, count, depth, source, target, cosine, sine, residual=False):
    rate, near_rate = level_numbers(depth)
    values[0] = cosine * values[count] - sine * roll(values[count], 64, 1)
    values[count + 1] = cosine * values[1] + sine * roll(values[1], 64, 1)

    def body(x):
        v = values[x + 1]
        near = values[x] + values[x + 2]
        near = near + (roll(v, 1, 0) + roll(v, -1, 0))
        near = near + (shift_z(v, 1) + shift_z(v, -1))
        if residual:
            target[x] = source[x] - omega / rate * v + near_rate / rate * near
        else:
            target[x + 1] = rate * source[x] + keep * v + near_rate * near

    each(count, body)


def first_sweep(values, count, depth, source):
    rate, _ = level_numbers(depth)

    def body(x):
        values[x + 1] = rate * source[x]

    each(count, body)


def cycle_kernel(*refs):
    radix = len(refs) - 14
    pieces, refs = refs[:radix], refs[radix:]
    cs_ref, own_ref, send_ref, s, u, v, r1, s2, u2, v2, r2, s3, u3, v3 = refs
    position = lax.axis_index("grid")
    core, block = lax.rem(position, 2), lax.div(position, 4)
    count = s.shape[0]
    rate, near_rate = level_numbers(1)
    cosine, sine = cs_ref[core], cs_ref[2 + core]
    lane = lax.broadcasted_iota(jnp.int32, (8, 128), 1)
    lane_sine = jnp.where(lane < 64, -sine, sine)

    length = count // radix
    digit = lax.div(block, length // 4)
    for k, piece in enumerate(pieces):
        s[pl.ds(lax.bitwise_xor(lax.rem(digit, radix), k) * length, length)] = piece[...]

    def sweep(values, target, residual=False):
        values[0, 0], values[0, 1] = rotated(values[count, 0], values[count, 1], cosine, -sine)
        values[count + 1, 0], values[count + 1, 1] = rotated(
            values[1, 0], values[1, 1], cosine, sine
        )

        def body(x):
            for f in range(2):
                a = values[x + 1, f]
                near = values[x, f] + values[x + 2, f]
                near = near + (roll(a, 1, 0) + roll(a, -1, 0))
                near = near + (roll(a, 1, 1) + roll(a, -1, 1))
                if residual:
                    target[x, f] = s[x, f] - omega / rate * a + near_rate / rate * near
                else:
                    target[x + 1, f] = rate * s[x, f] + keep * a + near_rate * near

        each(count, body)

    def start(x):
        for f in range(2):
            u[x + 1, f] = rate * s[x, f]

    each(count, start)
    sweep(u, v)
    sweep(v, r1, residual=True)

    count2 = count // 2
    i = lax.broadcasted_iota(jnp.int32, (128, 128), 0)
    j = lax.broadcasted_iota(jnp.int32, (128, 128), 1)
    rows = []
    for f in range(2):

        def lower(x):
            r1[2 * x, f] = r1[2 * x, f] + r1[2 * x + 1, f]
            r2[x, 8 * f : 8 * f + 8] = r1[2 * x, f, pl.ds(0, 8, 2)] + r1[2 * x, f, pl.ds(1, 8, 2)]

        each(count2, lower)
        rows.append(r2[:, 8 * f : 8 * f + 8].reshape(count2 * 8, 128))
    lowered = sum(
        dot(rows[f], jnp.where(i // 2 + 64 * f == j, 0.125, 0.0)) for f in range(2)
    )
    s2[...] = lowered.reshape(count2, 8, 128)
    first_sweep(u2, count2, 2, s2)
    packed_sweep(u2, count2, 2, s2, v2, cosine, lane_sine)
    packed_sweep(v2, count2, 2, s2, u2, cosine, lane_sine, residual=True)

    count3 = count2 // 2

    def lower3(x):
        total = u2[2 * x] + u2[2 * x + 1]
        r2[x, 0:8] = total
        r2[x, 8:16] = total
        s3[x] = r2[x, pl.ds(0, 8, 2)] + r2[x, pl.ds(1, 8, 2)]

    each(count3, lower3)
    same = i // 64 == j // 64
    lowered = dot(
        s3[...].reshape(count3 * 8, 128), jnp.where(same & (i % 64 // 2 == j % 32), 0.125, 0.0)
    )
    s3[...] = lowered.reshape(count3, 8, 128)
    first_sweep(u3, count3, 3, s3)
    a, b = u3, v3
    for _ in range(5):
        packed_sweep(a, count3, 3, s3, b, cosine, lane_sine)
        a, b = b, a

    raised = dot(
        a[1 : count3 + 1].reshape(count3 * 8, 128),
        jnp.where(same & (i % 64 == j % 64 // 2), 1.0, 0.0),
    )
    s3[...] = raised.reshape(count3, 8, 128)

    def raise3(x):
        r2[x, pl.ds(0, 8, 2)] = s3[x]
        r2[x, pl.ds(1, 8, 2)] = s3[x]
        for k in range(2):
            v2[2 * x + k + 1] = v2[2 * x + k + 1] + r2[x, 0:8]

    each(count3, raise3)
    packed_sweep(v2, count2, 2, s2, u2, cosine, lane_sine)
    packed_sweep(u2, count2, 2, s2, v2, cosine, lane_sine)

    rows = v2[1 : count2 + 1].reshape(count2 * 8, 128)
    for f in range(2):
        raised = dot(rows, jnp.where(i == j // 2 + 64 * f, 1.0, 0.0))
        s2[...] = raised.reshape(count2, 8, 128)

        def raise2(x):
            r1[x, f, pl.ds(0, 8, 2)] = s2[x]
            r1[x, f, pl.ds(1, 8, 2)] = s2[x]
            for k in range(2):
                v[2 * x + k + 1, f] = v[2 * x + k + 1, f] + r1[x, f]

        each(count2, raise2)
    sweep(v, u)
    sweep(u, v)

    for target, tile in ((own_ref, position), (send_ref, position + 1 - 2 * core)):
        for k in range(5):
            q = tile + k - 2
            low, high = q < 0, q >= count
            q = jnp.where(low, q + count, jnp.where(high, q - count, q))
            c = jnp.where(low | high, cosine, 1.0)
            t = jnp.where(low, -sine, jnp.where(high, sine, 0.0))
            target[k, 0], target[k, 1] = rotated(v[q + 1, 0], v[q + 1, 1], c, t)


def correct(w_ref, g_ref, e, b1, store):
    lines = w_ref.shape[2]
    wide = dot(w_ref[...].reshape(10 * lines, 128), spread_matrix(128, 256))
    for r in range(10):
        for h in range(2):
            value = wide[r * lines : (r + 1) * lines, 128 * h : 128 * (h + 1)]
            e[2 * r + h, pl.ds(0, lines, 2)] = value
            e[2 * r + h, pl.ds(1, lines, 2)] = value

    def expanded(x, f):
        place = (2 * (x // 2) + f) * 2
        return jnp.concatenate([e[place], e[place + 1]], axis=1)

    for x in range(6):
        for f in range(2):
            b1[x, f] = smooth_fine(expanded, x + 2, f)
    for x in range(2):
        for f in range(2):
            store(f, x, g_ref[x, f] + smooth_fine(lambda i, g: b1[i, g], x + 2, f))


def own_kernel(w_ref, g_ref, out_ref, e, b1):
    def store(part, x, value):
        out_ref[part, x] = value

    correct(w_ref, g_ref, e, b1, store)


def output_kernel(own_ref, w_ref, g_ref, out_ref, e, b1):
    core = lax.rem(lax.axis_index("grid"), 2)
    out_ref[core] = own_ref[...]

    def store(part, x, value):
        out_ref[1 - core, part, x] = value

    correct(w_ref, g_ref, e, b1, store)


def pair_phases(pair_table, k_fraction):
    kcount = k_fraction.shape[0]
    picks = pair_table[:, :, None] == jnp.arange(kcount, dtype=jnp.int32)[None, None, :]
    chosen = jnp.sum(jnp.where(picks, k_fraction[None, None, :], 0.0), axis=2)
    angle = 6.283185307179586 * (chosen[:, 0] - chosen[:, 1])
    return jnp.concatenate([jnp.cos(angle), jnp.sin(angle)])


def gather_blocks(value, blocks, block, permute_block):
    stride = 1
    while True:
        radix = min(4, blocks // stride)
        digit = block // stride % radix
        pieces = [value] + [
            permute_block(value, lambda b, k=k: b ^ k * stride) for k in range(1, radix)
        ]
        stride *= radix
        if stride == blocks:
            return pieces
        stacked = jnp.stack(pieces)[jnp.arange(radix) ^ digit]
        value = stacked.reshape(-1, *value.shape[1:])


def vmem(count):
    return [pl.BlockSpec(memory_space=pltpu.VMEM)] * count


smem = [pl.BlockSpec(memory_space=pltpu.SMEM)]


def call(kernel, out_shape, in_specs, scratch, flops, aliases={}):
    single = not isinstance(out_shape, (list, tuple))
    return pl.pallas_call(
        kernel,
        out_shape=out_shape,
        in_specs=in_specs,
        out_specs=vmem(1)[0]
        if single
        else [
            pl.BlockSpec(memory_space=pl.ANY if i in aliases.values() else pltpu.VMEM)
            for i in range(len(out_shape))
        ],
        input_output_aliases=aliases,
        scratch_shapes=[pltpu.VMEM(shape, jnp.float32) for shape in scratch],
        compiler_params=pltpu.CompilerParams(vmem_limit_bytes=48 * 2**20),
        cost_estimate=pl.CostEstimate(flops=flops, bytes_accessed=2**20, transcendentals=0),
    )


def shaped(*shape):
    return jax.ShapeDtypeStruct(shape, jnp.float32)


def per_device(
    pair_density, moments, shapes, slot_atom, slot_tile, slot_row, pair_table, k_fraction
):
    tile_count = lax.axis_size("grid")
    chips, blocks = tile_count // 2, tile_count // 4
    position = lax.axis_index("grid")
    core, block = position % 2, position // 4
    _, _, thick, lines, depth = pair_density.shape
    planes = 2 * thick
    slot_count = shapes.shape[0]
    capacity = max(2, 2 * slot_count // tile_count)
    devices = range(tile_count)

    def permute(value, target):
        return lax.ppermute(value, "grid", [(i, target(i)) for i in devices])

    def permute_block(value, target):
        return permute(value, lambda i: target(i // 4) * 4 + i % 4)

    def partner(i):
        return i ^ 1

    def even_side(i):
        return i ^ 2

    def odd_side(i):
        return (i // 2 + (1 if i // 2 % 2 else -1)) % chips * 2 + i % 2

    def next_block(i):
        return (i + (4 if i // 2 % 2 else -4)) % tile_count

    cs = pair_phases(pair_table, k_fraction)

    other = permute(lax.dynamic_index_in_dim(pair_density, 1 - core, 0, False), partner)
    slots = jnp.stack([slot_atom, slot_tile[:, 0], slot_row])
    row = 2 * depth
    kept, sent = call(
        rows_kernel,
        [shaped(slot_count, row), shaped(slot_count + 8, row)],
        vmem(3),
        [(2, slot_count, row)],
        10**7,
    )(moments, shapes.transpose(1, 0, 2), slots)
    got = permute(sent, partner)
    apart = chips <= 8
    height = 16 * capacity + 8
    packed = call(
        pack_kernel,
        [shaped(height, 128)] * chips if apart else [shaped(chips, height, 128)],
        vmem(3) + [pl.BlockSpec(memory_space=pl.ANY)],
        [],
        10**8,
    )(kept, got, slots, other)
    if apart:
        received = [
            permute(packed[k], lambda i, k=k: i ^ (2 * k)) if k else packed[k]
            for k in message_order(chips)
        ]
    else:
        groups = [[2 * k + c for k in range(chips)] for c in range(2)]
        received = [
            lax.all_to_all(
                packed[0], "grid", split_axis=0, concat_axis=0, axis_index_groups=groups, tiled=True
            )
        ]

    full = (2, lines, depth)
    small = (2, lines // 2, depth // 2)
    f, inner, outer = call(
        density_kernel,
        [shaped(planes, *full), shaped(4, *small), shaped(2, *small)],
        vmem(2 + len(received)),
        [(planes + 4, *full), (2 * (planes + 8), lines, 128)],
        10**8,
    )(pair_density, other, *received)
    source, f = call(
        source_kernel,
        [shaped(4, *small), shaped(planes, *full)],
        vmem(4) + smem + [pl.BlockSpec(memory_space=pl.ANY)],
        [],
        10**6,
        {5: 1},
    )(
        inner,
        permute(inner, even_side),
        permute(outer, next_block),
        permute(outer, odd_side),
        cs,
        f,
    )
    pieces = gather_blocks(source, blocks, block, permute_block)
    even = permute(f, even_side)
    odd = permute(f, odd_side)
    low, high = call(
        gate_kernel,
        [shaped(thick, *full)] * 2,
        [pl.BlockSpec(memory_space=pl.ANY)] * (len(pieces) + 1),
        [],
        10**4,
        {0: 0, 1: 1},
    )(f[:thick], f[thick:], *pieces[1:])
    after = permute(low, lambda i: (i - 4) % tile_count)
    before = permute(high, lambda i: (i + 4) % tile_count)
    n1, n2, n3 = tile_count, tile_count // 2, tile_count // 4
    tile = (8, 128)
    w_own, w_send = call(
        cycle_kernel,
        [shaped(5, *small)] * 2,
        vmem(len(pieces)) + smem,
        [
            (n1, *small),
            (n1 + 2, *small),
            (n1 + 2, *small),
            (n1, *small),
            (n2, *tile),
            (n2 + 2, *tile),
            (n2 + 2, *tile),
            (n2, 16, 128),
            (n3, *tile),
            (n3 + 2, *tile),
            (n3 + 2, *tile),
        ],
        10**8,
    )(*pieces, cs)
    own, send = call(
        fine_kernel,
        [shaped(thick, *full)] * 2,
        vmem(5) + smem + [pl.BlockSpec(memory_space=pl.ANY)],
        [(3 * planes + 4, *full), (planes + 8, *full), (planes + 4, *full), (planes, *full)],
        10**7,
    )(even, odd, after, before, f, cs, w_own)
    got = permute(send, partner)

    w_got = permute(w_send, partner)
    scratch = [(20, lines, 128), (6, *full)]
    result = call(own_kernel, shaped(2, thick, lines, depth), vmem(2), scratch, 10**7)(w_own, own)
    return call(output_kernel, shaped(*pair_density.shape), vmem(3), scratch, 10**7)(
        result, w_got, got
    )


def solution(mesh):
    return jax.shard_map(
        per_device,
        mesh=mesh,
        in_specs=(
            P("rep", None, "grid", None, None),
            P(("rep", "grid"), None, None, None),
            P(("rep", "grid"), None, None),
            P(("rep", "grid")),
            P(("rep", "grid"), None),
            P(("rep", "grid")),
            P(),
            P(),
        ),
        out_specs=P("rep", None, "grid", None, None),
        check_vma=False,
    )
```

```python
import jax
import jax.numpy as jnp
from jax import lax
from jax.experimental import pallas as pl
from jax.experimental.pallas import tpu as pltpu
from jax.sharding import PartitionSpec as P

omega = 0.8
screen = 0.05
highest = lax.Precision.HIGHEST

fine_diagonal = 7.5 + screen
fine_scale = omega / fine_diagonal
fine_near = fine_scale * 4.0 / 3.0
fine_far = fine_scale / 12.0
keep = 1.0 - omega


def level_numbers(depth):
    quarter = 1.0 / 4**depth
    diagonal = 6.0 * quarter + screen
    return omega / diagonal, omega / diagonal * quarter


def each(count, body, most=16):
    if count <= most:
        for i in range(count):
            body(i)
    else:
        pl.loop(0, count, unroll=4)(body)


def dot(a, b):
    return jnp.dot(a, b, precision=highest, preferred_element_type=jnp.float32)


def pair_matrix(rows, columns, value):
    i = lax.broadcasted_iota(jnp.int32, (rows, columns), 0)
    j = lax.broadcasted_iota(jnp.int32, (rows, columns), 1)
    return jnp.where(i // 2 == j, value, 0.0)


def spread_matrix(rows, columns):
    i = lax.broadcasted_iota(jnp.int32, (rows, columns), 0)
    j = lax.broadcasted_iota(jnp.int32, (rows, columns), 1)
    return jnp.where(i == j // 2, 1.0, 0.0)


def roll(v, shift, axis):
    return pltpu.roll(v, shift % v.shape[axis], axis)


def smooth_fine(at, x, f):
    total = None
    for step, weight in ((1, fine_near), (2, -fine_far)):
        sides = [p for p in (at(x - step, f), at(x + step, f)) if p is not None]
        v = at(x, f)
        if v is not None:
            for axis in (0, 1):
                sides.append(roll(v, step, axis) + roll(v, -step, axis))
            if step == 1:
                total = keep * v
        if sides:
            part = weight * sum(sides[1:], sides[0])
            total = part if total is None else total + part
    return total


def rotated(real, imag, cosine, sine):
    return cosine * real - sine * imag, sine * real + cosine * imag


def place_planes(target, base, count, at, cosine, sine):
    for x in range(count):
        real, imag = rotated(at(x, 0), at(x, 1), cosine, sine)
        target[base + x, 0] = real
        target[base + x, 1] = imag


def whole_planes(ref):
    return lambda x, part: ref[x, part]


def as_column(row):
    n = row.shape[1]
    i = lax.broadcasted_iota(jnp.int32, (n, n), 0)
    j = lax.broadcasted_iota(jnp.int32, (n, n), 1)
    return jnp.sum(jnp.where(i == j, row, 0.0), axis=1, keepdims=True)


def rows_kernel(moments_ref, shapes_ref, slots_ref, keep_ref, send_ref, rows):
    core = lax.rem(lax.axis_index("grid"), 2)
    channels, slots, depth = shapes_ref.shape
    atoms = moments_ref.shape[0]
    atom = as_column(slots_ref[0:1].astype(jnp.float32))
    picks = [jnp.where(atom == float(a), 1.0, 0.0) for a in range(atoms)]
    chosen = []
    for f in range(4):
        total = None
        for a in range(atoms):
            value = picks[a] * moments_ref[a, f // 2, f % 2 : f % 2 + 1]
            total = value if total is None else total + value
        chosen.append(total)
    for i in range(slots // 8):
        near = slice(8 * i, 8 * i + 8)
        totals = [None] * 4
        for channel in range(channels):
            shape = shapes_ref[channel, near]
            for f in range(4):
                value = chosen[f][near, channel : channel + 1] * shape
                totals[f] = value if totals[f] is None else totals[f] + value
        for f in range(4):
            rows[f // 2, near, f % 2 * depth : (f % 2 + 1) * depth] = totals[f]
    keep_ref[...] = rows[core]
    send_ref[0:slots] = rows[1 - core]
    send_ref[slots:] = jnp.zeros((8, 2 * depth), jnp.float32)
    number = (slots_ref[1:2] * 64 + slots_ref[2:3]).astype(jnp.float32)
    send_ref[slots : slots + 1, 0:slots] = number


def pack_kernel(own_ref, got_ref, slots_ref, _, *out_refs):
    slots = own_ref.shape[0]
    apart = len(out_refs) > 1
    height = out_refs[0].shape[-2]
    ranks = (height - 8) // 4
    capacity = ranks // 4
    chips = lax.axis_size("grid") // 2
    chip = lax.div(lax.axis_index("grid"), 2)
    number = (slots_ref[1:2] * 64 + slots_ref[2:3]).astype(jnp.float32)
    number = jnp.concatenate([number, got_ref[slots : slots + 1, 0:slots]], axis=1).astype(jnp.int32)
    tile, line = number // 64, number % 128 + 1
    column = as_column(tile.astype(jnp.float32)).astype(jnp.int32)
    i = lax.broadcasted_iota(jnp.int32, (2 * slots, 2 * slots), 0)
    j = lax.broadcasted_iota(jnp.int32, (2 * slots, 2 * slots), 1)
    ahead = jnp.where((column == tile) & (i < j) & (i // slots == j // slots), 1.0, 0.0)
    rank = jnp.sum(ahead, axis=0, keepdims=True).astype(jnp.int32)
    device = lax.broadcasted_iota(jnp.int32, (1, 2 * slots), 1) // slots
    place = tile // 2 * ranks + (2 * device + tile % 2) * capacity + rank
    r = lax.broadcasted_iota(jnp.int32, (ranks, 2 * slots), 0)
    targets = [lax.bitwise_xor(chip, k) if apart else k for k in range(chips)]
    pick = jnp.concatenate([jnp.where(place == r + target * ranks, 1.0, 0.0) for target in targets])
    rows = jnp.concatenate([own_ref[...], got_ref[0:slots]], axis=0)
    packed = dot(pick, rows)
    lines = jnp.sum(pick * line.astype(jnp.float32), axis=1, keepdims=True)
    bucket = lax.broadcasted_iota(jnp.int32, (chips * ranks, 128), 0)
    lane = lax.broadcasted_iota(jnp.int32, (chips * ranks, 128), 1)
    spot = bucket // ranks if apart else chip
    spots = jnp.where(lane == spot % (128 // ranks) * ranks + bucket % ranks, lines, 0.0)
    i = lax.broadcasted_iota(jnp.int32, (chips, chips * ranks), 0)
    j = lax.broadcasted_iota(jnp.int32, (chips, chips * ranks), 1)
    numbers = dot(jnp.where(i == j // ranks, 1.0, 0.0), spots)
    for k in range(chips):
        out = out_refs[k] if apart else out_refs[0].at[k]
        for q in range(4):
            out[q * ranks : (q + 1) * ranks] = packed[
                k * ranks : (k + 1) * ranks, q * 128 : (q + 1) * 128
            ]
        out[4 * ranks :] = jnp.broadcast_to(numbers[k : k + 1], (8, 128))


def message_order(chips):
    half = chips // 2
    return [0, 1, *range(half + 2, chips), half, half + 1, *range(2, half)]


def density_kernel(*refs):
    pd_ref, other_ref = refs[:2]
    f_ref, inner_ref, odd_ref, straight_ref, across_ref, b1, half = refs[-7:]
    pieces = refs[2:-7]
    position = lax.axis_index("grid")
    core, side = lax.rem(position, 2), lax.rem(lax.div(position, 2), 2)
    planes, _, lines, depth = f_ref.shape
    sources = lax.axis_size("grid") // 2
    height = pieces[0].shape[-2]
    ranks = (height - 8) // 4
    group = 128 // ranks

    def received(source, start, stop):
        if len(pieces) > 1:
            return pieces[message_order(sources).index(source)][start:stop]
        return pieces[0][source, start:stop]

    added = [None, None]
    for first in range(0, sources, group):
        members = range(first, min(first + group, sources))
        numbers = sum(received(k, 4 * ranks, 4 * ranks + 1) for k in members)
        line = lax.broadcasted_iota(jnp.int32, (planes * lines, 128), 0)
        spread = jnp.where(line == numbers.astype(jnp.int32) - 1, 1.0, 0.0)
        for part in range(2):
            values = jnp.concatenate(
                [
                    jnp.concatenate(
                        [received(k, q * ranks, (q + 1) * ranks) for k in members], axis=0
                    )
                    for q in (2 * part, 2 * part + 1)
                ],
                axis=1,
            )
            value = dot(spread[:, : len(members) * ranks], values)
            added[part] = value if added[part] is None else added[part] + value
    for x in range(planes):
        for part in range(2):
            f_ref[x, part] = added[part][x * lines : (x + 1) * lines]
    thick = planes // 2
    for x in range(thick):
        for part in range(2):
            f_ref[core * thick + x, part] += pd_ref[core, part, x]
            f_ref[(1 - core) * thick + x, part] += other_ref[part, x]

    def density(x, part):
        return f_ref[x, part] if 0 <= x < planes else None

    def once(x, part):
        return b1[x + 2, part] if -2 <= x < planes + 2 else None

    for x in range(-2, planes + 2):
        for part in range(2):
            b1[x + 2, part] = smooth_fine(density, x, part)
    rows = (planes + 8) // 2 * 2
    for i in range(rows // 2):
        for part in range(2):
            total = smooth_fine(once, 2 * i - 4, part) + smooth_fine(once, 2 * i - 3, part)
            for h in range(2):
                half[(2 * i + part) * 2 + h] = total[:, h * 128 : (h + 1) * 128]
    coarse = lowered(half, rows, lines, depth)

    def send(inner, outer, near):
        for r in range(8):
            inner_ref[r // 2, r % 2] = coarse[inner + r]
        for target in (odd_ref, straight_ref):
            first = 0 if target is odd_ref else near
            count = (target.shape[0] - 2) // 4
            for x in range(count):
                for part in range(2):
                    for h in range(2):
                        target[(2 * x + part) * 2 + h] = f_ref[
                            first + x, part, :, h * 128 : (h + 1) * 128
                        ]
            for r in range(4):
                target[4 * count + r // 2, r % 2 * 16 : r % 2 * 16 + 16] = coarse[outer + r]
        for x in range(2):
            across_ref[x] = f_ref[planes - 2 - near + x]

    @pl.when(side == 0)
    def _():
        send(4, 0, 0)

    @pl.when(side == 1)
    def _():
        send(0, 8, planes - 2)


def packed_planes(ref):
    def at(x, part):
        return jnp.concatenate([ref[(2 * x + part) * 2], ref[(2 * x + part) * 2 + 1]], axis=1)

    return at


def lowered(half, rows, lines, depth):
    matrix = pair_matrix(depth, depth // 2, 0.125)
    total = None
    for h in range(2):
        stacked = jnp.concatenate(
            [
                half[2 * r + h, pl.ds(0, lines // 2, 2)] + half[2 * r + h, pl.ds(1, lines // 2, 2)]
                for r in range(rows)
            ],
            axis=0,
        )
        value = dot(stacked, matrix[h * 128 : (h + 1) * 128])
        total = value if total is None else total + value
    return [total[r * lines // 2 : (r + 1) * lines // 2] for r in range(rows)]


def source_kernel(own_ref, partner_ref, straight_ref, odd_ref, cs_ref, _, s_ref, __):
    position = lax.axis_index("grid")
    blocks = lax.axis_size("grid") // 4
    core, side, block = lax.rem(position, 2), lax.rem(lax.div(position, 2), 2), lax.div(position, 4)
    cosine, sine = cs_ref[core], cs_ref[2 + core]
    first, last = block == 0, block == blocks - 1
    low = (jnp.where(first, cosine, 1.0), jnp.where(first, -sine, 0.0))
    high = (jnp.where(last, cosine, 1.0), jnp.where(last, sine, 0.0))

    def total(low_ref, high_ref):
        for x in range(4):
            source, (c, s) = (low_ref, low) if x < 2 else (high_ref, high)
            place = source.shape[0] - 2 + x % 2
            real, imag = rotated(source[place, 0:16], source[place, 16:32], c, s)
            s_ref[x, 0] = own_ref[x, 0] + partner_ref[x, 0] + real
            s_ref[x, 1] = own_ref[x, 1] + partner_ref[x, 1] + imag

    @pl.when(side == 0)
    def _():
        total(odd_ref, straight_ref)

    @pl.when(side == 1)
    def _():
        total(straight_ref, odd_ref)


def fine_kernel(
    even_ref, odd_ref, straight_ref, across_ref, f_ref, cs_ref, _, own_ref, send_ref, ext, b1, b2, g
):
    position = lax.axis_index("grid")
    blocks = lax.axis_size("grid") // 4
    core, side, block = lax.rem(position, 2), lax.rem(lax.div(position, 2), 2), lax.div(position, 4)
    cosine, sine = cs_ref[core], cs_ref[2 + core]
    planes = f_ref.shape[0]
    first, last = block == 0, block == blocks - 1
    low = (jnp.where(first, cosine, 1.0), jnp.where(first, -sine, 0.0))
    high = (jnp.where(last, cosine, 1.0), jnp.where(last, sine, 0.0))
    ext[planes + 2 : 2 * planes + 2] = f_ref[...]

    @pl.when(side == 0)
    def _():
        place_planes(ext, 0, 2, whole_planes(across_ref), *low)
        place_planes(ext, 2, planes, packed_planes(odd_ref), *low)
        ext[2 * planes + 2 : 3 * planes + 2] = even_ref[...]
        place_planes(ext, 3 * planes + 2, 2, packed_planes(straight_ref), *high)

    @pl.when(side == 1)
    def _():
        place_planes(ext, 0, 2, packed_planes(straight_ref), *low)
        ext[2 : planes + 2] = even_ref[...]
        place_planes(ext, 2 * planes + 2, planes, packed_planes(odd_ref), *high)
        place_planes(ext, 3 * planes + 2, 2, whole_planes(across_ref), *high)

    for x in range(planes + 8):
        for part in range(2):
            b1[x, part] = smooth_fine(lambda i, p: ext[i, p], x + 2, part)
    for x in range(planes + 4):
        for part in range(2):
            b2[x, part] = smooth_fine(lambda i, p: b1[i, p], x + 2, part)
    for x in range(planes):
        for part in range(2):
            b3 = smooth_fine(lambda i, p: b2[i, p], x + 2, part)
            g[x, part] = fine_scale * (f_ref[x, part] + b1[x + 4, part] + b2[x + 2, part] + b3)
    half = planes // 2
    for x in range(half):
        own_ref[x] = g[core * half + x]
        send_ref[x] = g[(1 - core) * half + x]


def shift_z(v, step):
    width = v.shape[-1] // 2
    lane = lax.broadcasted_iota(jnp.int32, v.shape, len(v.shape) - 1)
    edge = 0 if step > 0 else width - 1
    inner = roll(v, step, 1)
    outer = roll(v, step + (width if step > 0 else -width), 1)
    return jnp.where(lane % width == edge, outer, inner)


def packed_sweep(values, count, depth, source, target, cosine, sine, residual=False):
    rate, near_rate = level_numbers(depth)
    values[0] = cosine * values[count] - sine * roll(values[count], 64, 1)
    values[count + 1] = cosine * values[1] + sine * roll(values[1], 64, 1)

    def body(x):
        v = values[x + 1]
        near = values[x] + values[x + 2]
        near = near + (roll(v, 1, 0) + roll(v, -1, 0))
        near = near + (shift_z(v, 1) + shift_z(v, -1))
        if residual:
            target[x] = source[x] - omega / rate * v + near_rate / rate * near
        else:
            target[x + 1] = rate * source[x] + keep * v + near_rate * near

    each(count, body)


def first_sweep(values, count, depth, source):
    rate, _ = level_numbers(depth)

    def body(x):
        values[x + 1] = rate * source[x]

    each(count, body)


def cycle_kernel(*refs):
    radix = len(refs) - 14
    pieces, refs = refs[:radix], refs[radix:]
    cs_ref, own_ref, send_ref, s, u, v, r1, s2, u2, v2, r2, s3, u3, v3 = refs
    position = lax.axis_index("grid")
    core, block = lax.rem(position, 2), lax.div(position, 4)
    count = s.shape[0]
    rate, near_rate = level_numbers(1)
    cosine, sine = cs_ref[core], cs_ref[2 + core]
    lane = lax.broadcasted_iota(jnp.int32, (8, 128), 1)
    lane_sine = jnp.where(lane < 64, -sine, sine)

    length = count // radix
    digit = lax.div(block, length // 4)
    for k, piece in enumerate(pieces):
        s[pl.ds(lax.bitwise_xor(lax.rem(digit, radix), k) * length, length)] = piece[...]

    def sweep(values, target, residual=False):
        values[0, 0], values[0, 1] = rotated(values[count, 0], values[count, 1], cosine, -sine)
        values[count + 1, 0], values[count + 1, 1] = rotated(
            values[1, 0], values[1, 1], cosine, sine
        )

        def body(x):
            for f in range(2):
                a = values[x + 1, f]
                near = values[x, f] + values[x + 2, f]
                near = near + (roll(a, 1, 0) + roll(a, -1, 0))
                near = near + (roll(a, 1, 1) + roll(a, -1, 1))
                if residual:
                    target[x, f] = s[x, f] - omega / rate * a + near_rate / rate * near
                else:
                    target[x + 1, f] = rate * s[x, f] + keep * a + near_rate * near

        each(count, body)

    def start(x):
        for f in range(2):
            u[x + 1, f] = rate * s[x, f]

    each(count, start)
    sweep(u, v)
    sweep(v, r1, residual=True)

    count2 = count // 2
    i = lax.broadcasted_iota(jnp.int32, (128, 128), 0)
    j = lax.broadcasted_iota(jnp.int32, (128, 128), 1)
    rows = []
    for f in range(2):

        def lower(x):
            r1[2 * x, f] = r1[2 * x, f] + r1[2 * x + 1, f]
            r2[x, 8 * f : 8 * f + 8] = r1[2 * x, f, pl.ds(0, 8, 2)] + r1[2 * x, f, pl.ds(1, 8, 2)]

        each(count2, lower)
        rows.append(r2[:, 8 * f : 8 * f + 8].reshape(count2 * 8, 128))
    lowered = sum(
        dot(rows[f], jnp.where(i // 2 + 64 * f == j, 0.125, 0.0)) for f in range(2)
    )
    s2[...] = lowered.reshape(count2, 8, 128)
    first_sweep(u2, count2, 2, s2)
    packed_sweep(u2, count2, 2, s2, v2, cosine, lane_sine)
    packed_sweep(v2, count2, 2, s2, u2, cosine, lane_sine, residual=True)

    count3 = count2 // 2

    def lower3(x):
        total = u2[2 * x] + u2[2 * x + 1]
        r2[x, 0:8] = total
        r2[x, 8:16] = total
        s3[x] = r2[x, pl.ds(0, 8, 2)] + r2[x, pl.ds(1, 8, 2)]

    each(count3, lower3)
    same = i // 64 == j // 64
    lowered = dot(
        s3[...].reshape(count3 * 8, 128), jnp.where(same & (i % 64 // 2 == j % 32), 0.125, 0.0)
    )
    s3[...] = lowered.reshape(count3, 8, 128)
    first_sweep(u3, count3, 3, s3)
    a, b = u3, v3
    for _ in range(5):
        packed_sweep(a, count3, 3, s3, b, cosine, lane_sine)
        a, b = b, a

    raised = dot(
        a[1 : count3 + 1].reshape(count3 * 8, 128),
        jnp.where(same & (i % 64 == j % 64 // 2), 1.0, 0.0),
    )
    s3[...] = raised.reshape(count3, 8, 128)

    def raise3(x):
        r2[x, pl.ds(0, 8, 2)] = s3[x]
        r2[x, pl.ds(1, 8, 2)] = s3[x]
        for k in range(2):
            v2[2 * x + k + 1] = v2[2 * x + k + 1] + r2[x, 0:8]

    each(count3, raise3)
    packed_sweep(v2, count2, 2, s2, u2, cosine, lane_sine)
    packed_sweep(u2, count2, 2, s2, v2, cosine, lane_sine)

    rows = v2[1 : count2 + 1].reshape(count2 * 8, 128)
    for f in range(2):
        raised = dot(rows, jnp.where(i == j // 2 + 64 * f, 1.0, 0.0))
        s2[...] = raised.reshape(count2, 8, 128)

        def raise2(x):
            r1[x, f, pl.ds(0, 8, 2)] = s2[x]
            r1[x, f, pl.ds(1, 8, 2)] = s2[x]
            for k in range(2):
                v[2 * x + k + 1, f] = v[2 * x + k + 1, f] + r1[x, f]

        each(count2, raise2)
    sweep(v, u)
    sweep(u, v)

    for target, tile in ((own_ref, position), (send_ref, position + 1 - 2 * core)):
        for k in range(5):
            q = tile + k - 2
            low, high = q < 0, q >= count
            q = jnp.where(low, q + count, jnp.where(high, q - count, q))
            c = jnp.where(low | high, cosine, 1.0)
            t = jnp.where(low, -sine, jnp.where(high, sine, 0.0))
            target[k, 0], target[k, 1] = rotated(v[q + 1, 0], v[q + 1, 1], c, t)


def correct(w_ref, g_ref, e, b1, store):
    lines = w_ref.shape[2]
    wide = dot(w_ref[...].reshape(10 * lines, 128), spread_matrix(128, 256))
    for r in range(10):
        for h in range(2):
            value = wide[r * lines : (r + 1) * lines, 128 * h : 128 * (h + 1)]
            e[2 * r + h, pl.ds(0, lines, 2)] = value
            e[2 * r + h, pl.ds(1, lines, 2)] = value

    def expanded(x, f):
        place = (2 * (x // 2) + f) * 2
        return jnp.concatenate([e[place], e[place + 1]], axis=1)

    for x in range(6):
        for f in range(2):
            b1[x, f] = smooth_fine(expanded, x + 2, f)
    for x in range(2):
        for f in range(2):
            store(f, x, g_ref[x, f] + smooth_fine(lambda i, g: b1[i, g], x + 2, f))


def own_kernel(w_ref, g_ref, out_ref, e, b1):
    def store(part, x, value):
        out_ref[part, x] = value

    correct(w_ref, g_ref, e, b1, store)


def output_kernel(own_ref, w_ref, g_ref, out_ref, e, b1):
    core = lax.rem(lax.axis_index("grid"), 2)
    out_ref[core] = own_ref[...]

    def store(part, x, value):
        out_ref[1 - core, part, x] = value

    correct(w_ref, g_ref, e, b1, store)


def pair_phases(pair_table, k_fraction):
    kcount = k_fraction.shape[0]
    picks = pair_table[:, :, None] == jnp.arange(kcount, dtype=jnp.int32)[None, None, :]
    chosen = jnp.sum(jnp.where(picks, k_fraction[None, None, :], 0.0), axis=2)
    angle = 6.283185307179586 * (chosen[:, 0] - chosen[:, 1])
    return jnp.concatenate([jnp.cos(angle), jnp.sin(angle)])


def gather_blocks(value, blocks, block, permute_block):
    stride = 1
    while True:
        radix = min(4, blocks // stride)
        digit = block // stride % radix
        pieces = [value] + [
            permute_block(value, lambda b, k=k: b ^ k * stride) for k in range(1, radix)
        ]
        stride *= radix
        if stride == blocks:
            return pieces
        stacked = jnp.stack(pieces)[jnp.arange(radix) ^ digit]
        value = stacked.reshape(-1, *value.shape[1:])


def vmem(count):
    return [pl.BlockSpec(memory_space=pltpu.VMEM)] * count


smem = [pl.BlockSpec(memory_space=pltpu.SMEM)]


def call(kernel, out_shape, in_specs, scratch, flops, aliases={}):
    single = not isinstance(out_shape, (list, tuple))
    return pl.pallas_call(
        kernel,
        out_shape=out_shape,
        in_specs=in_specs,
        out_specs=vmem(1)[0]
        if single
        else [
            pl.BlockSpec(memory_space=pl.ANY if i in aliases.values() else pltpu.VMEM)
            for i in range(len(out_shape))
        ],
        input_output_aliases=aliases,
        scratch_shapes=[pltpu.VMEM(shape, jnp.float32) for shape in scratch],
        compiler_params=pltpu.CompilerParams(vmem_limit_bytes=48 * 2**20),
        cost_estimate=pl.CostEstimate(flops=flops, bytes_accessed=2**20, transcendentals=0),
    )


def shaped(*shape):
    return jax.ShapeDtypeStruct(shape, jnp.float32)


def per_device(
    pair_density, moments, shapes, slot_atom, slot_tile, slot_row, pair_table, k_fraction
):
    tile_count = lax.axis_size("grid")
    chips, blocks = tile_count // 2, tile_count // 4
    position = lax.axis_index("grid")
    core, block = position % 2, position // 4
    _, _, thick, lines, depth = pair_density.shape
    planes = 2 * thick
    slot_count = shapes.shape[0]
    capacity = max(2, 2 * slot_count // tile_count)
    devices = range(tile_count)

    def permute(value, target):
        return lax.ppermute(value, "grid", [(i, target(i)) for i in devices])

    def permute_block(value, target):
        return permute(value, lambda i: target(i // 4) * 4 + i % 4)

    def partner(i):
        return i ^ 1

    def even_side(i):
        return i ^ 2

    def odd_side(i):
        return (i // 2 + (1 if i // 2 % 2 else -1)) % chips * 2 + i % 2

    def next_block(i):
        return (i + (4 if i // 2 % 2 else -4)) % tile_count

    def block_behind(i):
        return (i + (-4 if i // 2 % 2 else 4)) % tile_count

    cs = pair_phases(pair_table, k_fraction)

    other = permute(lax.dynamic_index_in_dim(pair_density, 1 - core, 0, False), partner)
    slots = jnp.stack([slot_atom, slot_tile[:, 0], slot_row])
    row = 2 * depth
    kept, sent = call(
        rows_kernel,
        [shaped(slot_count, row), shaped(slot_count + 8, row)],
        vmem(3),
        [(2, slot_count, row)],
        10**7,
    )(moments, shapes.transpose(1, 0, 2), slots)
    got = permute(sent, partner)
    apart = chips <= 8
    height = 16 * capacity + 8
    packed = call(
        pack_kernel,
        [shaped(height, 128)] * chips if apart else [shaped(chips, height, 128)],
        vmem(3) + [pl.BlockSpec(memory_space=pl.ANY)],
        [],
        10**8,
    )(kept, got, slots, other)
    if apart:
        received = [
            permute(packed[k], lambda i, k=k: i ^ (2 * k)) if k else packed[k]
            for k in message_order(chips)
        ]
    else:
        groups = [[2 * k + c for k in range(chips)] for c in range(2)]
        received = [
            lax.all_to_all(
                packed[0], "grid", split_axis=0, concat_axis=0, axis_index_groups=groups, tiled=True
            )
        ]

    full = (2, lines, depth)
    small = (2, lines // 2, depth // 2)
    f, inner, odd, straight, across = call(
        density_kernel,
        [
            shaped(planes, *full),
            shaped(4, *small),
            shaped(4 * planes + 2, lines, 128),
            shaped(10, lines, 128),
            shaped(2, *full),
        ],
        vmem(2 + len(received)),
        [(planes + 4, *full), (2 * (planes + 8), lines, 128)],
        10**8,
    )(pair_density, other, *received)
    odd = permute(odd, odd_side)
    straight = permute(straight, next_block)
    across = permute(across, block_behind)
    source, f = call(
        source_kernel,
        [shaped(4, *small), shaped(planes, *full)],
        vmem(4) + smem + [pl.BlockSpec(memory_space=pl.ANY)],
        [],
        10**6,
        {5: 1},
    )(inner, permute(inner, even_side), straight, odd, cs, f)
    pieces = gather_blocks(source, blocks, block, permute_block)
    even = permute(f, even_side)

    n1, n2, n3 = tile_count, tile_count // 2, tile_count // 4
    tile = (8, 128)
    w_own, w_send = call(
        cycle_kernel,
        [shaped(5, *small)] * 2,
        vmem(len(pieces)) + smem,
        [
            (n1, *small),
            (n1 + 2, *small),
            (n1 + 2, *small),
            (n1, *small),
            (n2, *tile),
            (n2 + 2, *tile),
            (n2 + 2, *tile),
            (n2, 16, 128),
            (n3, *tile),
            (n3 + 2, *tile),
            (n3 + 2, *tile),
        ],
        10**8,
    )(*pieces, cs)
    own, send = call(
        fine_kernel,
        [shaped(thick, *full)] * 2,
        vmem(5) + smem + [pl.BlockSpec(memory_space=pl.ANY)],
        [(3 * planes + 4, *full), (planes + 8, *full), (planes + 4, *full), (planes, *full)],
        10**7,
    )(even, odd, straight, across, f, cs, w_own)
    got = permute(send, partner)

    w_got = permute(w_send, partner)
    scratch = [(20, lines, 128), (6, *full)]
    result = call(own_kernel, shaped(2, thick, lines, depth), vmem(2), scratch, 10**7)(w_own, own)
    return call(output_kernel, shaped(*pair_density.shape), vmem(3), scratch, 10**7)(
        result, w_got, got
    )


def solution(mesh):
    return jax.shard_map(
        per_device,
        mesh=mesh,
        in_specs=(
            P("rep", None, "grid", None, None),
            P(("rep", "grid"), None, None, None),
            P(("rep", "grid"), None, None),
            P(("rep", "grid")),
            P(("rep", "grid"), None),
            P(("rep", "grid")),
            P(),
            P(),
        ),
        out_specs=P("rep", None, "grid", None, None),
        check_vma=False,
    )
```

```python
import jax
import jax.numpy as jnp
from jax import lax
from jax.experimental import pallas as pl
from jax.experimental.pallas import tpu as pltpu
from jax.sharding import PartitionSpec as P

omega = 0.8
screen = 0.05
highest = lax.Precision.HIGHEST

fine_diagonal = 7.5 + screen
fine_scale = omega / fine_diagonal
fine_near = fine_scale * 4.0 / 3.0
fine_far = fine_scale / 12.0
keep = 1.0 - omega


def level_numbers(depth):
    quarter = 1.0 / 4**depth
    diagonal = 6.0 * quarter + screen
    return omega / diagonal, omega / diagonal * quarter


def each(count, body, most=16):
    if count <= most:
        for i in range(count):
            body(i)
    else:
        pl.loop(0, count, unroll=4)(body)


def dot(a, b):
    return jnp.dot(a, b, precision=highest, preferred_element_type=jnp.float32)


def pair_matrix(rows, columns, value):
    i = lax.broadcasted_iota(jnp.int32, (rows, columns), 0)
    j = lax.broadcasted_iota(jnp.int32, (rows, columns), 1)
    return jnp.where(i // 2 == j, value, 0.0)


def spread_matrix(rows, columns):
    i = lax.broadcasted_iota(jnp.int32, (rows, columns), 0)
    j = lax.broadcasted_iota(jnp.int32, (rows, columns), 1)
    return jnp.where(i == j // 2, 1.0, 0.0)


def roll(v, shift, axis):
    return pltpu.roll(v, shift % v.shape[axis], axis)


def smooth_fine(at, x, f):
    total = None
    for step, weight in ((1, fine_near), (2, -fine_far)):
        sides = [p for p in (at(x - step, f), at(x + step, f)) if p is not None]
        v = at(x, f)
        if v is not None:
            for axis in (0, 1):
                sides.append(roll(v, step, axis) + roll(v, -step, axis))
            if step == 1:
                total = keep * v
        if sides:
            part = weight * sum(sides[1:], sides[0])
            total = part if total is None else total + part
    return total


def rotated(real, imag, cosine, sine):
    return cosine * real - sine * imag, sine * real + cosine * imag


def place_planes(target, base, count, at, cosine, sine):
    for x in range(count):
        real, imag = rotated(at(x, 0), at(x, 1), cosine, sine)
        target[base + x, 0] = real
        target[base + x, 1] = imag


def whole_planes(ref):
    return lambda x, part: ref[x, part]


def as_column(row):
    n = row.shape[1]
    i = lax.broadcasted_iota(jnp.int32, (n, n), 0)
    j = lax.broadcasted_iota(jnp.int32, (n, n), 1)
    return jnp.sum(jnp.where(i == j, row, 0.0), axis=1, keepdims=True)


def rows_kernel(moments_ref, shapes_ref, slots_ref, keep_ref, send_ref, rows):
    core = lax.rem(lax.axis_index("grid"), 2)
    channels, slots, depth = shapes_ref.shape
    atoms = moments_ref.shape[0]
    atom = as_column(slots_ref[0:1].astype(jnp.float32))
    picks = [jnp.where(atom == float(a), 1.0, 0.0) for a in range(atoms)]
    chosen = []
    for f in range(4):
        total = None
        for a in range(atoms):
            value = picks[a] * moments_ref[a, f // 2, f % 2 : f % 2 + 1]
            total = value if total is None else total + value
        chosen.append(total)
    for i in range(slots // 8):
        near = slice(8 * i, 8 * i + 8)
        totals = [None] * 4
        for channel in range(channels):
            shape = shapes_ref[channel, near]
            for f in range(4):
                value = chosen[f][near, channel : channel + 1] * shape
                totals[f] = value if totals[f] is None else totals[f] + value
        for f in range(4):
            rows[f // 2, near, f % 2 * depth : (f % 2 + 1) * depth] = totals[f]
    keep_ref[...] = rows[core]
    send_ref[0:slots] = rows[1 - core]
    send_ref[slots:] = jnp.zeros((8, 2 * depth), jnp.float32)
    number = (slots_ref[1:2] * 64 + slots_ref[2:3]).astype(jnp.float32)
    send_ref[slots : slots + 1, 0:slots] = number


def pack_kernel(own_ref, got_ref, slots_ref, _, *out_refs):
    slots = own_ref.shape[0]
    apart = len(out_refs) > 1
    height = out_refs[0].shape[-2]
    ranks = (height - 8) // 4
    capacity = ranks // 4
    chips = lax.axis_size("grid") // 2
    chip = lax.div(lax.axis_index("grid"), 2)
    number = (slots_ref[1:2] * 64 + slots_ref[2:3]).astype(jnp.float32)
    number = jnp.concatenate([number, got_ref[slots : slots + 1, 0:slots]], axis=1).astype(jnp.int32)
    tile, line = number // 64, number % 128 + 1
    column = as_column(tile.astype(jnp.float32)).astype(jnp.int32)
    i = lax.broadcasted_iota(jnp.int32, (2 * slots, 2 * slots), 0)
    j = lax.broadcasted_iota(jnp.int32, (2 * slots, 2 * slots), 1)
    ahead = jnp.where((column == tile) & (i < j) & (i // slots == j // slots), 1.0, 0.0)
    rank = jnp.sum(ahead, axis=0, keepdims=True).astype(jnp.int32)
    device = lax.broadcasted_iota(jnp.int32, (1, 2 * slots), 1) // slots
    place = tile // 2 * ranks + (2 * device + tile % 2) * capacity + rank
    r = lax.broadcasted_iota(jnp.int32, (ranks, 2 * slots), 0)
    targets = [lax.bitwise_xor(chip, k) if apart else k for k in range(chips)]
    pick = jnp.concatenate([jnp.where(place == r + target * ranks, 1.0, 0.0) for target in targets])
    rows = jnp.concatenate([own_ref[...], got_ref[0:slots]], axis=0)
    packed = dot(pick, rows)
    lines = jnp.sum(pick * line.astype(jnp.float32), axis=1, keepdims=True)
    bucket = lax.broadcasted_iota(jnp.int32, (chips * ranks, 128), 0)
    lane = lax.broadcasted_iota(jnp.int32, (chips * ranks, 128), 1)
    spot = bucket // ranks if apart else chip
    spots = jnp.where(lane == spot % (128 // ranks) * ranks + bucket % ranks, lines, 0.0)
    i = lax.broadcasted_iota(jnp.int32, (chips, chips * ranks), 0)
    j = lax.broadcasted_iota(jnp.int32, (chips, chips * ranks), 1)
    numbers = dot(jnp.where(i == j // ranks, 1.0, 0.0), spots)
    for k in range(chips):
        out = out_refs[k] if apart else out_refs[0].at[k]
        for q in range(4):
            out[q * ranks : (q + 1) * ranks] = packed[
                k * ranks : (k + 1) * ranks, q * 128 : (q + 1) * 128
            ]
        out[4 * ranks :] = jnp.broadcast_to(numbers[k : k + 1], (8, 128))


def message_order(chips):
    half = chips // 2
    return [0, 1, *range(half + 2, chips), half, half + 1, *range(2, half)]


def density_kernel(*refs):
    pd_ref, other_ref = refs[:2]
    f_ref, inner_ref, odd_ref, straight_ref, across_ref, b1, half = refs[-7:]
    pieces = refs[2:-7]
    position = lax.axis_index("grid")
    core, side = lax.rem(position, 2), lax.rem(lax.div(position, 2), 2)
    planes, _, lines, depth = f_ref.shape
    sources = lax.axis_size("grid") // 2
    height = pieces[0].shape[-2]
    ranks = (height - 8) // 4
    group = 128 // ranks

    def received(source, start, stop):
        if len(pieces) > 1:
            return pieces[message_order(sources).index(source)][start:stop]
        return pieces[0][source, start:stop]

    added = [None, None]
    for first in range(0, sources, group):
        members = range(first, min(first + group, sources))
        numbers = sum(received(k, 4 * ranks, 4 * ranks + 1) for k in members)
        line = lax.broadcasted_iota(jnp.int32, (planes * lines, 128), 0)
        spread = jnp.where(line == numbers.astype(jnp.int32) - 1, 1.0, 0.0)
        for part in range(2):
            values = jnp.concatenate(
                [
                    jnp.concatenate(
                        [received(k, q * ranks, (q + 1) * ranks) for k in members], axis=0
                    )
                    for q in (2 * part, 2 * part + 1)
                ],
                axis=1,
            )
            value = dot(spread[:, : len(members) * ranks], values)
            added[part] = value if added[part] is None else added[part] + value
    for x in range(planes):
        for part in range(2):
            f_ref[x, part] = added[part][x * lines : (x + 1) * lines]
    thick = planes // 2
    for x in range(thick):
        for part in range(2):
            f_ref[core * thick + x, part] += pd_ref[core, part, x]
            f_ref[(1 - core) * thick + x, part] += other_ref[part, x]

    def density(x, part):
        return f_ref[x, part] if 0 <= x < planes else None

    def once(x, part):
        return b1[x + 2, part] if -2 <= x < planes + 2 else None

    for x in range(-2, planes + 2):
        for part in range(2):
            b1[x + 2, part] = smooth_fine(density, x, part)
    rows = (planes + 8) // 2 * 2
    for i in range(rows // 2):
        for part in range(2):
            total = smooth_fine(once, 2 * i - 4, part) + smooth_fine(once, 2 * i - 3, part)
            for h in range(2):
                half[(2 * i + part) * 2 + h] = total[:, h * 128 : (h + 1) * 128]
    coarse = lowered(half, rows, lines, depth)

    def send(inner, outer, near):
        for r in range(8):
            inner_ref[r // 2, r % 2] = coarse[inner + r]
        for target in (odd_ref, straight_ref):
            first = 0 if target is odd_ref else near
            count = (target.shape[0] - 2) // 4
            for x in range(count):
                for part in range(2):
                    for h in range(2):
                        target[(2 * x + part) * 2 + h] = f_ref[
                            first + x, part, :, h * 128 : (h + 1) * 128
                        ]
            for r in range(4):
                target[4 * count + r // 2, r % 2 * 16 : r % 2 * 16 + 16] = coarse[outer + r]
        for x in range(2):
            across_ref[x] = f_ref[planes - 2 - near + x]

    @pl.when(side == 0)
    def _():
        send(4, 0, 0)

    @pl.when(side == 1)
    def _():
        send(0, 8, planes - 2)


def packed_planes(ref):
    def at(x, part):
        return jnp.concatenate([ref[(2 * x + part) * 2], ref[(2 * x + part) * 2 + 1]], axis=1)

    return at


def lowered(half, rows, lines, depth):
    matrix = pair_matrix(depth, depth // 2, 0.125)
    total = None
    for h in range(2):
        stacked = jnp.concatenate(
            [
                half[2 * r + h, pl.ds(0, lines // 2, 2)] + half[2 * r + h, pl.ds(1, lines // 2, 2)]
                for r in range(rows)
            ],
            axis=0,
        )
        value = dot(stacked, matrix[h * 128 : (h + 1) * 128])
        total = value if total is None else total + value
    return [total[r * lines // 2 : (r + 1) * lines // 2] for r in range(rows)]


def source_kernel(own_ref, partner_ref, straight_ref, odd_ref, cs_ref, _, s_ref):
    position = lax.axis_index("grid")
    blocks = lax.axis_size("grid") // 4
    core, side, block = lax.rem(position, 2), lax.rem(lax.div(position, 2), 2), lax.div(position, 4)
    cosine, sine = cs_ref[core], cs_ref[2 + core]
    first, last = block == 0, block == blocks - 1
    low = (jnp.where(first, cosine, 1.0), jnp.where(first, -sine, 0.0))
    high = (jnp.where(last, cosine, 1.0), jnp.where(last, sine, 0.0))

    def total(low_ref, high_ref):
        for x in range(4):
            source, (c, s) = (low_ref, low) if x < 2 else (high_ref, high)
            place = source.shape[0] - 2 + x % 2
            real, imag = rotated(source[place, 0:16], source[place, 16:32], c, s)
            s_ref[x, 0] = own_ref[x, 0] + partner_ref[x, 0] + real
            s_ref[x, 1] = own_ref[x, 1] + partner_ref[x, 1] + imag

    @pl.when(side == 0)
    def _():
        total(odd_ref, straight_ref)

    @pl.when(side == 1)
    def _():
        total(straight_ref, odd_ref)


def fine_kernel(
    even_ref, odd_ref, straight_ref, across_ref, f_ref, cs_ref, own_ref, send_ref, ext, b1, b2, g
):
    position = lax.axis_index("grid")
    blocks = lax.axis_size("grid") // 4
    core, side, block = lax.rem(position, 2), lax.rem(lax.div(position, 2), 2), lax.div(position, 4)
    cosine, sine = cs_ref[core], cs_ref[2 + core]
    planes = f_ref.shape[0]
    first, last = block == 0, block == blocks - 1
    low = (jnp.where(first, cosine, 1.0), jnp.where(first, -sine, 0.0))
    high = (jnp.where(last, cosine, 1.0), jnp.where(last, sine, 0.0))
    ext[planes + 2 : 2 * planes + 2] = f_ref[...]

    @pl.when(side == 0)
    def _():
        place_planes(ext, 0, 2, whole_planes(across_ref), *low)
        place_planes(ext, 2, planes, packed_planes(odd_ref), *low)
        ext[2 * planes + 2 : 3 * planes + 2] = even_ref[...]
        place_planes(ext, 3 * planes + 2, 2, packed_planes(straight_ref), *high)

    @pl.when(side == 1)
    def _():
        place_planes(ext, 0, 2, packed_planes(straight_ref), *low)
        ext[2 : planes + 2] = even_ref[...]
        place_planes(ext, 2 * planes + 2, planes, packed_planes(odd_ref), *high)
        place_planes(ext, 3 * planes + 2, 2, whole_planes(across_ref), *high)

    for x in range(planes + 8):
        for part in range(2):
            b1[x, part] = smooth_fine(lambda i, p: ext[i, p], x + 2, part)
    for x in range(planes + 4):
        for part in range(2):
            b2[x, part] = smooth_fine(lambda i, p: b1[i, p], x + 2, part)
    for x in range(planes):
        for part in range(2):
            b3 = smooth_fine(lambda i, p: b2[i, p], x + 2, part)
            g[x, part] = fine_scale * (f_ref[x, part] + b1[x + 4, part] + b2[x + 2, part] + b3)
    half = planes // 2
    for x in range(half):
        own_ref[x] = g[core * half + x]
        send_ref[x] = g[(1 - core) * half + x]


def shift_z(v, step):
    width = v.shape[-1] // 2
    lane = lax.broadcasted_iota(jnp.int32, v.shape, len(v.shape) - 1)
    edge = 0 if step > 0 else width - 1
    inner = roll(v, step, 1)
    outer = roll(v, step + (width if step > 0 else -width), 1)
    return jnp.where(lane % width == edge, outer, inner)


def packed_sweep(values, count, depth, source, target, cosine, sine, residual=False):
    rate, near_rate = level_numbers(depth)
    values[0] = cosine * values[count] - sine * roll(values[count], 64, 1)
    values[count + 1] = cosine * values[1] + sine * roll(values[1], 64, 1)

    def body(x):
        v = values[x + 1]
        near = values[x] + values[x + 2]
        near = near + (roll(v, 1, 0) + roll(v, -1, 0))
        near = near + (shift_z(v, 1) + shift_z(v, -1))
        if residual:
            target[x] = source[x] - omega / rate * v + near_rate / rate * near
        else:
            target[x + 1] = rate * source[x] + keep * v + near_rate * near

    each(count, body)


def first_sweep(values, count, depth, source):
    rate, _ = level_numbers(depth)

    def body(x):
        values[x + 1] = rate * source[x]

    each(count, body)


def cycle_kernel(*refs):
    radix = len(refs) - 14
    pieces, refs = refs[:radix], refs[radix:]
    cs_ref, own_ref, send_ref, s, u, v, r1, s2, u2, v2, r2, s3, u3, v3 = refs
    position = lax.axis_index("grid")
    core, block = lax.rem(position, 2), lax.div(position, 4)
    count = s.shape[0]
    rate, near_rate = level_numbers(1)
    cosine, sine = cs_ref[core], cs_ref[2 + core]
    lane = lax.broadcasted_iota(jnp.int32, (8, 128), 1)
    lane_sine = jnp.where(lane < 64, -sine, sine)

    length = count // radix
    digit = lax.div(block, length // 4)
    for k, piece in enumerate(pieces):
        s[pl.ds(lax.bitwise_xor(lax.rem(digit, radix), k) * length, length)] = piece[...]

    def sweep(values, target, residual=False):
        values[0, 0], values[0, 1] = rotated(values[count, 0], values[count, 1], cosine, -sine)
        values[count + 1, 0], values[count + 1, 1] = rotated(
            values[1, 0], values[1, 1], cosine, sine
        )

        def body(x):
            for f in range(2):
                a = values[x + 1, f]
                near = values[x, f] + values[x + 2, f]
                near = near + (roll(a, 1, 0) + roll(a, -1, 0))
                near = near + (roll(a, 1, 1) + roll(a, -1, 1))
                if residual:
                    target[x, f] = s[x, f] - omega / rate * a + near_rate / rate * near
                else:
                    target[x + 1, f] = rate * s[x, f] + keep * a + near_rate * near

        each(count, body)

    def start(x):
        for f in range(2):
            u[x + 1, f] = rate * s[x, f]

    each(count, start)
    sweep(u, v)
    sweep(v, r1, residual=True)

    count2 = count // 2
    i = lax.broadcasted_iota(jnp.int32, (128, 128), 0)
    j = lax.broadcasted_iota(jnp.int32, (128, 128), 1)
    rows = []
    for f in range(2):

        def lower(x):
            r1[2 * x, f] = r1[2 * x, f] + r1[2 * x + 1, f]
            r2[x, 8 * f : 8 * f + 8] = r1[2 * x, f, pl.ds(0, 8, 2)] + r1[2 * x, f, pl.ds(1, 8, 2)]

        each(count2, lower)
        rows.append(r2[:, 8 * f : 8 * f + 8].reshape(count2 * 8, 128))
    lowered = sum(
        dot(rows[f], jnp.where(i // 2 + 64 * f == j, 0.125, 0.0)) for f in range(2)
    )
    s2[...] = lowered.reshape(count2, 8, 128)
    first_sweep(u2, count2, 2, s2)
    packed_sweep(u2, count2, 2, s2, v2, cosine, lane_sine)
    packed_sweep(v2, count2, 2, s2, u2, cosine, lane_sine, residual=True)

    count3 = count2 // 2

    def lower3(x):
        total = u2[2 * x] + u2[2 * x + 1]
        r2[x, 0:8] = total
        r2[x, 8:16] = total
        s3[x] = r2[x, pl.ds(0, 8, 2)] + r2[x, pl.ds(1, 8, 2)]

    each(count3, lower3)
    same = i // 64 == j // 64
    lowered = dot(
        s3[...].reshape(count3 * 8, 128), jnp.where(same & (i % 64 // 2 == j % 32), 0.125, 0.0)
    )
    s3[...] = lowered.reshape(count3, 8, 128)
    first_sweep(u3, count3, 3, s3)
    a, b = u3, v3
    for _ in range(5):
        packed_sweep(a, count3, 3, s3, b, cosine, lane_sine)
        a, b = b, a

    raised = dot(
        a[1 : count3 + 1].reshape(count3 * 8, 128),
        jnp.where(same & (i % 64 == j % 64 // 2), 1.0, 0.0),
    )
    s3[...] = raised.reshape(count3, 8, 128)

    def raise3(x):
        r2[x, pl.ds(0, 8, 2)] = s3[x]
        r2[x, pl.ds(1, 8, 2)] = s3[x]
        for k in range(2):
            v2[2 * x + k + 1] = v2[2 * x + k + 1] + r2[x, 0:8]

    each(count3, raise3)
    packed_sweep(v2, count2, 2, s2, u2, cosine, lane_sine)
    packed_sweep(u2, count2, 2, s2, v2, cosine, lane_sine)

    rows = v2[1 : count2 + 1].reshape(count2 * 8, 128)
    for f in range(2):
        raised = dot(rows, jnp.where(i == j // 2 + 64 * f, 1.0, 0.0))
        s2[...] = raised.reshape(count2, 8, 128)

        def raise2(x):
            r1[x, f, pl.ds(0, 8, 2)] = s2[x]
            r1[x, f, pl.ds(1, 8, 2)] = s2[x]
            for k in range(2):
                v[2 * x + k + 1, f] = v[2 * x + k + 1, f] + r1[x, f]

        each(count2, raise2)
    sweep(v, u)
    sweep(u, v)

    for target, tile in ((own_ref, position), (send_ref, position + 1 - 2 * core)):
        for k in range(5):
            q = tile + k - 2
            low, high = q < 0, q >= count
            q = jnp.where(low, q + count, jnp.where(high, q - count, q))
            c = jnp.where(low | high, cosine, 1.0)
            t = jnp.where(low, -sine, jnp.where(high, sine, 0.0))
            target[k, 0], target[k, 1] = rotated(v[q + 1, 0], v[q + 1, 1], c, t)


def correct(w_ref, g_ref, e, b1, store):
    lines = w_ref.shape[2]
    wide = dot(w_ref[...].reshape(10 * lines, 128), spread_matrix(128, 256))
    for r in range(10):
        for h in range(2):
            value = wide[r * lines : (r + 1) * lines, 128 * h : 128 * (h + 1)]
            e[2 * r + h, pl.ds(0, lines, 2)] = value
            e[2 * r + h, pl.ds(1, lines, 2)] = value

    def expanded(x, f):
        place = (2 * (x // 2) + f) * 2
        return jnp.concatenate([e[place], e[place + 1]], axis=1)

    for x in range(6):
        for f in range(2):
            b1[x, f] = smooth_fine(expanded, x + 2, f)
    for x in range(2):
        for f in range(2):
            store(f, x, g_ref[x, f] + smooth_fine(lambda i, g: b1[i, g], x + 2, f))


def own_kernel(w_ref, g_ref, out_ref, e, b1):
    def store(part, x, value):
        out_ref[part, x] = value

    correct(w_ref, g_ref, e, b1, store)


def output_kernel(own_ref, w_ref, g_ref, out_ref, e, b1):
    core = lax.rem(lax.axis_index("grid"), 2)
    out_ref[core] = own_ref[...]

    def store(part, x, value):
        out_ref[1 - core, part, x] = value

    correct(w_ref, g_ref, e, b1, store)


def pair_phases(pair_table, k_fraction):
    kcount = k_fraction.shape[0]
    picks = pair_table[:, :, None] == jnp.arange(kcount, dtype=jnp.int32)[None, None, :]
    chosen = jnp.sum(jnp.where(picks, k_fraction[None, None, :], 0.0), axis=2)
    angle = 6.283185307179586 * (chosen[:, 0] - chosen[:, 1])
    return jnp.concatenate([jnp.cos(angle), jnp.sin(angle)])


def gather_blocks(value, blocks, block, permute_block):
    stride = 1
    while True:
        radix = min(4, blocks // stride)
        digit = block // stride % radix
        pieces = [value] + [
            permute_block(value, lambda b, k=k: b ^ k * stride) for k in range(1, radix)
        ]
        stride *= radix
        if stride == blocks:
            return pieces
        stacked = jnp.stack(pieces)[jnp.arange(radix) ^ digit]
        value = stacked.reshape(-1, *value.shape[1:])


def vmem(count):
    return [pl.BlockSpec(memory_space=pltpu.VMEM)] * count


smem = [pl.BlockSpec(memory_space=pltpu.SMEM)]


def call(kernel, out_shape, in_specs, scratch, flops):
    single = not isinstance(out_shape, (list, tuple))
    return pl.pallas_call(
        kernel,
        out_shape=out_shape,
        in_specs=in_specs,
        out_specs=vmem(1)[0]
        if single
        else vmem(len(out_shape)),
        scratch_shapes=[pltpu.VMEM(shape, jnp.float32) for shape in scratch],
        compiler_params=pltpu.CompilerParams(vmem_limit_bytes=48 * 2**20),
        cost_estimate=pl.CostEstimate(flops=flops, bytes_accessed=2**20, transcendentals=0),
    )


def gate_kernel(*_):
    pass


def gate(value, other):
    return pl.pallas_call(
        gate_kernel,
        out_shape=jax.ShapeDtypeStruct(value.shape, value.dtype),
        in_specs=[pl.BlockSpec(memory_space=pl.ANY)] * 2,
        out_specs=pl.BlockSpec(memory_space=pl.ANY),
        input_output_aliases={0: 0},
        cost_estimate=pl.CostEstimate(flops=0, bytes_accessed=0, transcendentals=0),
    )(value, other)


def shaped(*shape):
    return jax.ShapeDtypeStruct(shape, jnp.float32)


def per_device(
    pair_density, moments, shapes, slot_atom, slot_tile, slot_row, pair_table, k_fraction
):
    tile_count = lax.axis_size("grid")
    chips, blocks = tile_count // 2, tile_count // 4
    position = lax.axis_index("grid")
    core, block = position % 2, position // 4
    _, _, thick, lines, depth = pair_density.shape
    planes = 2 * thick
    slot_count = shapes.shape[0]
    capacity = max(2, 2 * slot_count // tile_count)
    devices = range(tile_count)

    def permute(value, target):
        return lax.ppermute(value, "grid", [(i, target(i)) for i in devices])

    def permute_block(value, target):
        return permute(value, lambda i: target(i // 4) * 4 + i % 4)

    def partner(i):
        return i ^ 1

    def even_side(i):
        return i ^ 2

    def odd_side(i):
        return (i // 2 + (1 if i // 2 % 2 else -1)) % chips * 2 + i % 2

    def next_block(i):
        return (i + (4 if i // 2 % 2 else -4)) % tile_count

    def block_behind(i):
        return (i + (-4 if i // 2 % 2 else 4)) % tile_count

    cs = pair_phases(pair_table, k_fraction)

    other = permute(lax.dynamic_index_in_dim(pair_density, 1 - core, 0, False), partner)
    slots = jnp.stack([slot_atom, slot_tile[:, 0], slot_row])
    row = 2 * depth
    kept, sent = call(
        rows_kernel,
        [shaped(slot_count, row), shaped(slot_count + 8, row)],
        vmem(3),
        [(2, slot_count, row)],
        10**7,
    )(moments, shapes.transpose(1, 0, 2), slots)
    got = permute(sent, partner)
    apart = chips <= 8
    height = 16 * capacity + 8
    packed = call(
        pack_kernel,
        [shaped(height, 128)] * chips if apart else [shaped(chips, height, 128)],
        vmem(3) + [pl.BlockSpec(memory_space=pl.ANY)],
        [],
        10**8,
    )(kept, got, slots, other)
    if apart:
        received = [
            permute(packed[k], lambda i, k=k: i ^ (2 * k)) if k else packed[k]
            for k in message_order(chips)
        ]
    else:
        groups = [[2 * k + c for k in range(chips)] for c in range(2)]
        received = [
            lax.all_to_all(
                packed[0], "grid", split_axis=0, concat_axis=0, axis_index_groups=groups, tiled=True
            )
        ]

    full = (2, lines, depth)
    small = (2, lines // 2, depth // 2)
    f, inner, odd, straight, across = call(
        density_kernel,
        [
            shaped(planes, *full),
            shaped(4, *small),
            shaped(4 * planes + 2, lines, 128),
            shaped(10, lines, 128),
            shaped(2, *full),
        ],
        vmem(2 + len(received)),
        [(planes + 4, *full), (2 * (planes + 8), lines, 128)],
        10**8,
    )(pair_density, other, *received)
    odd = permute(odd, odd_side)
    straight = permute(straight, next_block)
    across = permute(across, block_behind)
    theirs = permute(inner, even_side)
    f = gate(f, theirs)
    even = permute(f, even_side)
    source = call(
        source_kernel,
        shaped(4, *small),
        vmem(4) + smem + [pl.BlockSpec(memory_space=pl.ANY)],
        [],
        10**6,
    )(inner, theirs, straight, odd, cs, across)
    pieces = gather_blocks(source, blocks, block, permute_block)

    own, send = call(
        fine_kernel,
        [shaped(thick, *full)] * 2,
        vmem(5) + smem,
        [(3 * planes + 4, *full), (planes + 8, *full), (planes + 4, *full), (planes, *full)],
        10**7,
    )(even, odd, straight, across, f, cs)
    got = permute(send, partner)

    n1, n2, n3 = tile_count, tile_count // 2, tile_count // 4
    tile = (8, 128)
    w_own, w_send = call(
        cycle_kernel,
        [shaped(5, *small)] * 2,
        vmem(len(pieces)) + smem,
        [
            (n1, *small),
            (n1 + 2, *small),
            (n1 + 2, *small),
            (n1, *small),
            (n2, *tile),
            (n2 + 2, *tile),
            (n2 + 2, *tile),
            (n2, 16, 128),
            (n3, *tile),
            (n3 + 2, *tile),
            (n3 + 2, *tile),
        ],
        10**8,
    )(*pieces, cs)
    w_got = permute(w_send, partner)
    scratch = [(20, lines, 128), (6, *full)]
    result = call(own_kernel, shaped(2, thick, lines, depth), vmem(2), scratch, 10**7)(w_own, own)
    return call(output_kernel, shaped(*pair_density.shape), vmem(3), scratch, 10**7)(
        result, w_got, got
    )


def solution(mesh):
    return jax.shard_map(
        per_device,
        mesh=mesh,
        in_specs=(
            P("rep", None, "grid", None, None),
            P(("rep", "grid"), None, None, None),
            P(("rep", "grid"), None, None),
            P(("rep", "grid")),
            P(("rep", "grid"), None),
            P(("rep", "grid")),
            P(),
            P(),
        ),
        out_specs=P("rep", None, "grid", None, None),
        check_vma=False,
    )
```

```python
import jax
import jax.numpy as jnp
from jax import lax
from jax.experimental import pallas as pl
from jax.experimental.pallas import tpu as pltpu
from jax.sharding import PartitionSpec as P

omega = 0.8
screen = 0.05
highest = lax.Precision.HIGHEST

fine_diagonal = 7.5 + screen
fine_scale = omega / fine_diagonal
fine_near = fine_scale * 4.0 / 3.0
fine_far = fine_scale / 12.0
keep = 1.0 - omega


def level_numbers(depth):
    quarter = 1.0 / 4**depth
    diagonal = 6.0 * quarter + screen
    return omega / diagonal, omega / diagonal * quarter


def each(count, body, most=16):
    if count <= most:
        for i in range(count):
            body(i)
    else:
        pl.loop(0, count, unroll=4)(body)


def dot(a, b):
    return jnp.dot(a, b, precision=highest, preferred_element_type=jnp.float32)


def pair_matrix(rows, columns, value):
    i = lax.broadcasted_iota(jnp.int32, (rows, columns), 0)
    j = lax.broadcasted_iota(jnp.int32, (rows, columns), 1)
    return jnp.where(i // 2 == j, value, 0.0)


def spread_matrix(rows, columns):
    i = lax.broadcasted_iota(jnp.int32, (rows, columns), 0)
    j = lax.broadcasted_iota(jnp.int32, (rows, columns), 1)
    return jnp.where(i == j // 2, 1.0, 0.0)


def roll(v, shift, axis):
    return pltpu.roll(v, shift % v.shape[axis], axis)


def smooth_fine(at, x, f):
    total = None
    for step, weight in ((1, fine_near), (2, -fine_far)):
        sides = [p for p in (at(x - step, f), at(x + step, f)) if p is not None]
        v = at(x, f)
        if v is not None:
            for axis in (0, 1):
                sides.append(roll(v, step, axis) + roll(v, -step, axis))
            if step == 1:
                total = keep * v
        if sides:
            part = weight * sum(sides[1:], sides[0])
            total = part if total is None else total + part
    return total


def rotated(real, imag, cosine, sine):
    return cosine * real - sine * imag, sine * real + cosine * imag


def place_planes(target, base, source, cosine, sine):
    for x in range(source.shape[0]):
        real, imag = rotated(source[x, 0], source[x, 1], cosine, sine)
        target[base + x, 0] = real
        target[base + x, 1] = imag


def place_halo(ext, middle, even_ref, odd_ref, cs_ref):
    position = lax.axis_index("grid")
    chips = lax.axis_size("grid") // 2
    core, chip = lax.rem(position, 2), lax.div(position, 2)
    cosine, sine = cs_ref[core], cs_ref[2 + core]
    first, last = chip == 0, chip == chips - 1
    low = (jnp.where(first, cosine, 1.0), jnp.where(first, -sine, 0.0))
    high = (jnp.where(last, cosine, 1.0), jnp.where(last, sine, 0.0))
    planes = even_ref.shape[0]
    parity = lax.rem(chip, 2)

    @pl.when(parity == 0)
    def _():
        place_planes(ext, middle - planes, odd_ref, *low)
        place_planes(ext, middle + planes, even_ref, *high)

    @pl.when(parity == 1)
    def _():
        place_planes(ext, middle - planes, even_ref, *low)
        place_planes(ext, middle + planes, odd_ref, *high)


def as_column(row):
    n = row.shape[1]
    i = lax.broadcasted_iota(jnp.int32, (n, n), 0)
    j = lax.broadcasted_iota(jnp.int32, (n, n), 1)
    return jnp.sum(jnp.where(i == j, row, 0.0), axis=1, keepdims=True)


def rows_kernel(moments_ref, shapes_ref, slots_ref, keep_ref, send_ref, rows):
    core = lax.rem(lax.axis_index("grid"), 2)
    channels, slots, depth = shapes_ref.shape
    atoms = moments_ref.shape[1]
    atom = as_column(slots_ref[0:1].astype(jnp.float32))
    picks = [jnp.where(atom == float(a), 1.0, 0.0) for a in range(atoms)]
    chosen = []
    for f in range(4):
        total = None
        for a in range(atoms):
            value = picks[a] * moments_ref[f, a : a + 1]
            total = value if total is None else total + value
        chosen.append(total)
    for i in range(slots // 8):
        near = slice(8 * i, 8 * i + 8)
        totals = [None] * 4
        for channel in range(channels):
            shape = shapes_ref[channel, near]
            for f in range(4):
                value = chosen[f][near, channel : channel + 1] * shape
                totals[f] = value if totals[f] is None else totals[f] + value
        for f in range(4):
            rows[f // 2, near, f % 2 * depth : (f % 2 + 1) * depth] = totals[f]
    keep_ref[...] = rows[core]
    send_ref[0:slots] = rows[1 - core]
    send_ref[slots:] = jnp.zeros((8, 2 * depth), jnp.float32)
    number = (slots_ref[1:2] * 64 + slots_ref[2:3]).astype(jnp.float32)
    send_ref[slots : slots + 1, 0:slots] = number


def pack_kernel(own_ref, got_ref, slots_ref, _, *out_refs):
    slots = own_ref.shape[0]
    apart = len(out_refs) > 1
    height = out_refs[0].shape[-2]
    ranks = (height - 8) // 4
    capacity = ranks // 4
    chips = lax.axis_size("grid") // 2
    chip = lax.div(lax.axis_index("grid"), 2)
    number = (slots_ref[1:2] * 64 + slots_ref[2:3]).astype(jnp.float32)
    number = jnp.concatenate([number, got_ref[slots : slots + 1, 0:slots]], axis=1).astype(jnp.int32)
    tile, line = number // 64, number % 128 + 1
    column = as_column(tile.astype(jnp.float32)).astype(jnp.int32)
    i = lax.broadcasted_iota(jnp.int32, (2 * slots, 2 * slots), 0)
    j = lax.broadcasted_iota(jnp.int32, (2 * slots, 2 * slots), 1)
    ahead = jnp.where((column == tile) & (i < j) & (i // slots == j // slots), 1.0, 0.0)
    rank = jnp.sum(ahead, axis=0, keepdims=True).astype(jnp.int32)
    device = lax.broadcasted_iota(jnp.int32, (1, 2 * slots), 1) // slots
    place = tile // 2 * ranks + (2 * device + tile % 2) * capacity + rank
    r = lax.broadcasted_iota(jnp.int32, (ranks, 2 * slots), 0)
    targets = [lax.bitwise_xor(chip, k) if apart else k for k in range(chips)]
    pick = jnp.concatenate([jnp.where(place == r + target * ranks, 1.0, 0.0) for target in targets])
    rows = jnp.concatenate([own_ref[...], got_ref[0:slots]], axis=0)
    packed = dot(pick, rows)
    lines = jnp.sum(pick * line.astype(jnp.float32), axis=1, keepdims=True)
    bucket = lax.broadcasted_iota(jnp.int32, (chips * ranks, 128), 0)
    lane = lax.broadcasted_iota(jnp.int32, (chips * ranks, 128), 1)
    spot = bucket // ranks if apart else chip
    spots = jnp.where(lane == spot % (128 // ranks) * ranks + bucket % ranks, lines, 0.0)
    i = lax.broadcasted_iota(jnp.int32, (chips, chips * ranks), 0)
    j = lax.broadcasted_iota(jnp.int32, (chips, chips * ranks), 1)
    numbers = dot(jnp.where(i == j // ranks, 1.0, 0.0), spots)
    for k in range(chips):
        out = out_refs[k] if apart else out_refs[0].at[k]
        for q in range(4):
            out[q * ranks : (q + 1) * ranks] = packed[
                k * ranks : (k + 1) * ranks, q * 128 : (q + 1) * 128
            ]
        out[4 * ranks :] = jnp.broadcast_to(numbers[k : k + 1], (8, 128))


def message_order(chips):
    half = chips // 2
    return [0, 1, *range(half + 2, chips), half, half + 1, *range(2, half)]


def density_kernel(*refs):
    pd_ref, other_ref = refs[:2]
    f_ref, straight_ref, across_ref, b1, half = refs[-5:]
    pieces = refs[2:-5]
    position = lax.axis_index("grid")
    core, side = lax.rem(position, 2), lax.rem(lax.div(position, 2), 2)
    planes, _, lines, depth = f_ref.shape
    sources = lax.axis_size("grid") // 2
    height = pieces[0].shape[-2]
    ranks = (height - 8) // 4
    group = 128 // ranks

    def received(source, start, stop):
        if len(pieces) > 1:
            return pieces[message_order(sources).index(source)][start:stop]
        return pieces[0][source, start:stop]

    added = [None, None]
    for first in range(0, sources, group):
        members = range(first, min(first + group, sources))
        numbers = sum(received(k, 4 * ranks, 4 * ranks + 1) for k in members)
        line = lax.broadcasted_iota(jnp.int32, (planes * lines, 128), 0)
        spread = jnp.where(line == numbers.astype(jnp.int32) - 1, 1.0, 0.0)
        for part in range(2):
            values = jnp.concatenate(
                [
                    jnp.concatenate(
                        [received(k, q * ranks, (q + 1) * ranks) for k in members], axis=0
                    )
                    for q in (2 * part, 2 * part + 1)
                ],
                axis=1,
            )
            value = dot(spread[:, : len(members) * ranks], values)
            added[part] = value if added[part] is None else added[part] + value
    for x in range(planes):
        for part in range(2):
            f_ref[x, part] = added[part][x * lines : (x + 1) * lines]
    thick = planes // 2
    for x in range(thick):
        for part in range(2):
            f_ref[core * thick + x, part] += pd_ref[core, part, x]
            f_ref[(1 - core) * thick + x, part] += other_ref[part, x]

    def density(x, part):
        return f_ref[x, part] if 0 <= x < planes else None

    def once(x, part):
        return b1[x + 2, part] if -2 <= x < planes + 2 else None

    def outer(base, first_plane, one):
        for x in range(one, one + 4):
            for part in range(2):
                b1[x + 2, part] = smooth_fine(density, x, part)
        for i in range(2):
            for part in range(2):
                x = base + 2 * i
                total = smooth_fine(once, x, part) + smooth_fine(once, x + 1, part)
                for h in range(2):
                    half[(2 * i + part) * 2 + h] = total[:, h * 128 : (h + 1) * 128]
        for r, value in enumerate(lowered(half, 4, lines, depth)):
            straight_ref[8 + r // 2, r % 2 * 16 : r % 2 * 16 + 16] = value
        for x in range(2):
            for part in range(2):
                for h in range(2):
                    straight_ref[(2 * x + part) * 2 + h] = f_ref[
                        first_plane + x, part, :, h * 128 : (h + 1) * 128
                    ]
        other = planes - 2 - first_plane
        for x in range(2):
            across_ref[x] = f_ref[other + x]

    @pl.when(side == 0)
    def _():
        outer(-4, 0, -2)

    @pl.when(side == 1)
    def _():
        outer(planes, planes - 2, planes - 2)


def lowered(half, rows, lines, depth):
    matrix = pair_matrix(depth, depth // 2, 0.125)
    total = None
    for h in range(2):
        stacked = jnp.concatenate(
            [
                half[2 * r + h, pl.ds(0, lines // 2, 2)] + half[2 * r + h, pl.ds(1, lines // 2, 2)]
                for r in range(rows)
            ],
            axis=0,
        )
        value = dot(stacked, matrix[h * 128 : (h + 1) * 128])
        total = value if total is None else total + value
    return [total[r * lines // 2 : (r + 1) * lines // 2] for r in range(rows)]


def source_kernel(even_ref, odd_ref, straight_ref, f_ref, cs_ref, s_ref, ext, b1, half):
    position = lax.axis_index("grid")
    blocks = lax.axis_size("grid") // 4
    core, side, block = lax.rem(position, 2), lax.rem(lax.div(position, 2), 2), lax.div(position, 4)
    cosine, sine = cs_ref[core], cs_ref[2 + core]
    planes = f_ref.shape[0]
    lines, depth = f_ref.shape[2:]
    first, last = block == 0, block == blocks - 1
    low = (jnp.where(first, cosine, 1.0), jnp.where(first, -sine, 0.0))
    high = (jnp.where(last, cosine, 1.0), jnp.where(last, sine, 0.0))

    @pl.when(side == 0)
    def _():
        place_planes(ext, 0, odd_ref, *low)
        ext[planes : 2 * planes] = f_ref[...]
        ext[2 * planes : 3 * planes] = even_ref[...]
        ext[3 * planes :] = jnp.zeros((planes, 2, lines, depth), jnp.float32)

    @pl.when(side == 1)
    def _():
        ext[:planes] = jnp.zeros((planes, 2, lines, depth), jnp.float32)
        ext[planes : 2 * planes] = even_ref[...]
        ext[2 * planes : 3 * planes] = f_ref[...]
        place_planes(ext, 3 * planes, odd_ref, *high)

    for x in range(2 * planes + 4):
        for part in range(2):
            b1[x, part] = smooth_fine(lambda i, p: ext[i, p], x + planes - 2, part)
    for i in range(planes):
        for part in range(2):
            total = smooth_fine(lambda i, p: b1[i, p], 2 * i + 2, part) + smooth_fine(
                lambda i, p: b1[i, p], 2 * i + 3, part
            )
            for h in range(2):
                half[(2 * i + part) * 2 + h] = total[:, h * 128 : (h + 1) * 128]
    for r, value in enumerate(lowered(half, 2 * planes, lines, depth)):
        s_ref[r // 2, r % 2] = value

    def add(base, c, t):
        for x in range(2):
            real, imag = rotated(straight_ref[8 + x, 0:16], straight_ref[8 + x, 16:32], c, t)
            s_ref[base + x, 0] += real
            s_ref[base + x, 1] += imag

    @pl.when(side == 0)
    def _():
        add(2, *high)

    @pl.when(side == 1)
    def _():
        add(0, *low)


def fine_kernel(
    even_ref, odd_ref, straight_ref, across_ref, f_ref, cs_ref, own_ref, send_ref, ext, b1, b2, g
):
    position = lax.axis_index("grid")
    chips = lax.axis_size("grid") // 2
    core, chip = lax.rem(position, 2), lax.div(position, 2)
    cosine, sine = cs_ref[core], cs_ref[2 + core]
    planes = f_ref.shape[0]
    place_halo(ext, planes + 2, even_ref, odd_ref, cs_ref)
    ext[planes + 2 : 2 * planes + 2] = f_ref[...]
    first, last = chip < 2, chip >= chips - 2
    low = (jnp.where(first, cosine, 1.0), jnp.where(first, -sine, 0.0))
    high = (jnp.where(last, cosine, 1.0), jnp.where(last, sine, 0.0))

    def place_straight(base, c, t):
        for x in range(2):
            real, imag = [
                jnp.concatenate([straight_ref[4 * x + 2 * p], straight_ref[4 * x + 2 * p + 1]], axis=1)
                for p in range(2)
            ]
            ext[base + x, 0], ext[base + x, 1] = rotated(real, imag, c, t)

    @pl.when(lax.rem(chip, 2) == 0)
    def _():
        place_planes(ext, 0, across_ref, *low)
        place_straight(3 * planes + 2, *high)

    @pl.when(lax.rem(chip, 2) == 1)
    def _():
        place_straight(0, *low)
        place_planes(ext, 3 * planes + 2, across_ref, *high)

    for x in range(planes + 8):
        for part in range(2):
            b1[x, part] = smooth_fine(lambda i, p: ext[i, p], x + 2, part)
    for x in range(planes + 4):
        for part in range(2):
            b2[x, part] = smooth_fine(lambda i, p: b1[i, p], x + 2, part)
    for x in range(planes):
        for part in range(2):
            b3 = smooth_fine(lambda i, p: b2[i, p], x + 2, part)
            g[x, part] = fine_scale * (f_ref[x, part] + b1[x + 4, part] + b2[x + 2, part] + b3)
    half = planes // 2
    for x in range(half):
        own_ref[x] = g[core * half + x]
        send_ref[x] = g[(1 - core) * half + x]


def shift_z(v, step):
    width = v.shape[-1] // 2
    lane = lax.broadcasted_iota(jnp.int32, v.shape, len(v.shape) - 1)
    edge = 0 if step > 0 else width - 1
    inner = roll(v, step, 1)
    outer = roll(v, step + (width if step > 0 else -width), 1)
    return jnp.where(lane % width == edge, outer, inner)


def packed_sweep(values, count, depth, source, target, cosine, sine, residual=False):
    rate, near_rate = level_numbers(depth)
    values[0] = cosine * values[count] - sine * roll(values[count], 64, 1)
    values[count + 1] = cosine * values[1] + sine * roll(values[1], 64, 1)

    def body(x):
        v = values[x + 1]
        near = values[x] + values[x + 2]
        near = near + (roll(v, 1, 0) + roll(v, -1, 0))
        near = near + (shift_z(v, 1) + shift_z(v, -1))
        if residual:
            target[x] = source[x] - omega / rate * v + near_rate / rate * near
        else:
            target[x + 1] = rate * source[x] + keep * v + near_rate * near

    each(count, body)


def first_sweep(values, count, depth, source):
    rate, _ = level_numbers(depth)

    def body(x):
        values[x + 1] = rate * source[x]

    each(count, body)


def cycle_kernel(*refs):
    radix = len(refs) - 14
    pieces, refs = refs[:radix], refs[radix:]
    cs_ref, own_ref, send_ref, s, u, v, r1, s2, u2, v2, r2, s3, u3, v3 = refs
    position = lax.axis_index("grid")
    core, block = lax.rem(position, 2), lax.div(position, 4)
    count = s.shape[0]
    rate, near_rate = level_numbers(1)
    cosine, sine = cs_ref[core], cs_ref[2 + core]
    lane = lax.broadcasted_iota(jnp.int32, (8, 128), 1)
    lane_sine = jnp.where(lane < 64, -sine, sine)

    length = count // radix
    digit = lax.div(block, length // 4)
    for k, piece in enumerate(pieces):
        s[pl.ds(lax.bitwise_xor(lax.rem(digit, radix), k) * length, length)] = piece[...]

    def sweep(values, target, residual=False):
        values[0, 0], values[0, 1] = rotated(values[count, 0], values[count, 1], cosine, -sine)
        values[count + 1, 0], values[count + 1, 1] = rotated(
            values[1, 0], values[1, 1], cosine, sine
        )

        def body(x):
            for f in range(2):
                a = values[x + 1, f]
                near = values[x, f] + values[x + 2, f]
                near = near + (roll(a, 1, 0) + roll(a, -1, 0))
                near = near + (roll(a, 1, 1) + roll(a, -1, 1))
                if residual:
                    target[x, f] = s[x, f] - omega / rate * a + near_rate / rate * near
                else:
                    target[x + 1, f] = rate * s[x, f] + keep * a + near_rate * near

        each(count, body)

    def start(x):
        for f in range(2):
            u[x + 1, f] = rate * s[x, f]

    each(count, start)
    sweep(u, v)
    sweep(v, r1, residual=True)

    count2 = count // 2
    i = lax.broadcasted_iota(jnp.int32, (128, 128), 0)
    j = lax.broadcasted_iota(jnp.int32, (128, 128), 1)
    rows = []
    for f in range(2):

        def lower(x):
            r1[2 * x, f] = r1[2 * x, f] + r1[2 * x + 1, f]
            r2[x, 8 * f : 8 * f + 8] = r1[2 * x, f, pl.ds(0, 8, 2)] + r1[2 * x, f, pl.ds(1, 8, 2)]

        each(count2, lower)
        rows.append(r2[:, 8 * f : 8 * f + 8].reshape(count2 * 8, 128))
    lowered = sum(
        dot(rows[f], jnp.where(i // 2 + 64 * f == j, 0.125, 0.0)) for f in range(2)
    )
    s2[...] = lowered.reshape(count2, 8, 128)
    first_sweep(u2, count2, 2, s2)
    packed_sweep(u2, count2, 2, s2, v2, cosine, lane_sine)
    packed_sweep(v2, count2, 2, s2, u2, cosine, lane_sine, residual=True)

    count3 = count2 // 2

    def lower3(x):
        total = u2[2 * x] + u2[2 * x + 1]
        r2[x, 0:8] = total
        r2[x, 8:16] = total
        s3[x] = r2[x, pl.ds(0, 8, 2)] + r2[x, pl.ds(1, 8, 2)]

    each(count3, lower3)
    same = i // 64 == j // 64
    lowered = dot(
        s3[...].reshape(count3 * 8, 128), jnp.where(same & (i % 64 // 2 == j % 32), 0.125, 0.0)
    )
    s3[...] = lowered.reshape(count3, 8, 128)
    first_sweep(u3, count3, 3, s3)
    a, b = u3, v3
    for _ in range(5):
        packed_sweep(a, count3, 3, s3, b, cosine, lane_sine)
        a, b = b, a

    raised = dot(
        a[1 : count3 + 1].reshape(count3 * 8, 128),
        jnp.where(same & (i % 64 == j % 64 // 2), 1.0, 0.0),
    )
    s3[...] = raised.reshape(count3, 8, 128)

    def raise3(x):
        r2[x, pl.ds(0, 8, 2)] = s3[x]
        r2[x, pl.ds(1, 8, 2)] = s3[x]
        for k in range(2):
            v2[2 * x + k + 1] = v2[2 * x + k + 1] + r2[x, 0:8]

    each(count3, raise3)
    packed_sweep(v2, count2, 2, s2, u2, cosine, lane_sine)
    packed_sweep(u2, count2, 2, s2, v2, cosine, lane_sine)

    rows = v2[1 : count2 + 1].reshape(count2 * 8, 128)
    for f in range(2):
        raised = dot(rows, jnp.where(i == j // 2 + 64 * f, 1.0, 0.0))
        s2[...] = raised.reshape(count2, 8, 128)

        def raise2(x):
            r1[x, f, pl.ds(0, 8, 2)] = s2[x]
            r1[x, f, pl.ds(1, 8, 2)] = s2[x]
            for k in range(2):
                v[2 * x + k + 1, f] = v[2 * x + k + 1, f] + r1[x, f]

        each(count2, raise2)
    sweep(v, u)
    sweep(u, v)

    for target, tile in ((own_ref, position), (send_ref, position + 1 - 2 * core)):
        for k in range(5):
            q = tile + k - 2
            low, high = q < 0, q >= count
            q = jnp.where(low, q + count, jnp.where(high, q - count, q))
            c = jnp.where(low | high, cosine, 1.0)
            t = jnp.where(low, -sine, jnp.where(high, sine, 0.0))
            target[k, 0], target[k, 1] = rotated(v[q + 1, 0], v[q + 1, 1], c, t)


def correct(w_ref, g_ref, e, b1, store):
    lines = w_ref.shape[2]
    wide = dot(w_ref[...].reshape(10 * lines, 128), spread_matrix(128, 256))
    for r in range(10):
        for h in range(2):
            value = wide[r * lines : (r + 1) * lines, 128 * h : 128 * (h + 1)]
            e[2 * r + h, pl.ds(0, lines, 2)] = value
            e[2 * r + h, pl.ds(1, lines, 2)] = value

    def expanded(x, f):
        place = (2 * (x // 2) + f) * 2
        return jnp.concatenate([e[place], e[place + 1]], axis=1)

    for x in range(6):
        for f in range(2):
            b1[x, f] = smooth_fine(expanded, x + 2, f)
    for x in range(2):
        for f in range(2):
            store(f, x, g_ref[x, f] + smooth_fine(lambda i, g: b1[i, g], x + 2, f))


def own_kernel(w_ref, g_ref, out_ref, e, b1):
    def store(part, x, value):
        out_ref[part, x] = value

    correct(w_ref, g_ref, e, b1, store)


def output_kernel(own_ref, w_ref, g_ref, out_ref, e, b1):
    core = lax.rem(lax.axis_index("grid"), 2)
    out_ref[core] = own_ref[...]

    def store(part, x, value):
        out_ref[1 - core, part, x] = value

    correct(w_ref, g_ref, e, b1, store)


def pair_phases(pair_table, k_fraction):
    kcount = k_fraction.shape[0]
    picks = pair_table[:, :, None] == jnp.arange(kcount, dtype=jnp.int32)[None, None, :]
    chosen = jnp.sum(jnp.where(picks, k_fraction[None, None, :], 0.0), axis=2)
    angle = 6.283185307179586 * (chosen[:, 0] - chosen[:, 1])
    return jnp.concatenate([jnp.cos(angle), jnp.sin(angle)])


def gather_blocks(value, blocks, block, permute_block):
    stride = 1
    while True:
        radix = min(4, blocks // stride)
        digit = block // stride % radix
        pieces = [value] + [
            permute_block(value, lambda b, k=k: b ^ k * stride) for k in range(1, radix)
        ]
        stride *= radix
        if stride == blocks:
            return pieces
        stacked = jnp.stack(pieces)[jnp.arange(radix) ^ digit]
        value = stacked.reshape(-1, *value.shape[1:])


def vmem(count):
    return [pl.BlockSpec(memory_space=pltpu.VMEM)] * count


smem = [pl.BlockSpec(memory_space=pltpu.SMEM)]


def call(kernel, out_shape, in_specs, scratch, flops):
    single = not isinstance(out_shape, (list, tuple))
    return pl.pallas_call(
        kernel,
        out_shape=out_shape,
        in_specs=in_specs,
        out_specs=vmem(1)[0] if single else vmem(len(out_shape)),
        scratch_shapes=[pltpu.VMEM(shape, jnp.float32) for shape in scratch],
        compiler_params=pltpu.CompilerParams(vmem_limit_bytes=48 * 2**20),
        cost_estimate=pl.CostEstimate(flops=flops, bytes_accessed=2**20, transcendentals=0),
    )


def shaped(*shape):
    return jax.ShapeDtypeStruct(shape, jnp.float32)


def per_device(
    pair_density, moments, shapes, slot_atom, slot_tile, slot_row, pair_table, k_fraction
):
    tile_count = lax.axis_size("grid")
    chips, blocks = tile_count // 2, tile_count // 4
    position = lax.axis_index("grid")
    core, block = position % 2, position // 4
    _, _, thick, lines, depth = pair_density.shape
    planes = 2 * thick
    slot_count = shapes.shape[0]
    capacity = max(2, 2 * slot_count // tile_count)
    devices = range(tile_count)

    def permute(value, target):
        return lax.ppermute(value, "grid", [(i, target(i)) for i in devices])

    def permute_block(value, target):
        return permute(value, lambda i: target(i // 4) * 4 + i % 4)

    def partner(i):
        return i ^ 1

    def even_side(i):
        return i ^ 2

    def odd_side(i):
        return (i // 2 + (1 if i // 2 % 2 else -1)) % chips * 2 + i % 2

    def next_block(i):
        return (i + (4 if i // 2 % 2 else -4)) % tile_count

    cs = pair_phases(pair_table, k_fraction)

    other = permute(lax.dynamic_index_in_dim(pair_density, 1 - core, 0, False), partner)
    slots = jnp.stack([slot_atom, slot_tile[:, 0], slot_row])
    fields = moments.reshape(moments.shape[0], 4, -1).transpose(1, 0, 2)
    row = 2 * depth
    kept, sent = call(
        rows_kernel,
        [shaped(slot_count, row), shaped(slot_count + 8, row)],
        vmem(3),
        [(2, slot_count, row)],
        10**7,
    )(fields, shapes.transpose(1, 0, 2), slots)
    got = permute(sent, partner)
    apart = chips <= 8
    height = 16 * capacity + 8
    packed = call(
        pack_kernel,
        [shaped(height, 128)] * chips if apart else [shaped(chips, height, 128)],
        vmem(3) + [pl.BlockSpec(memory_space=pl.ANY)],
        [],
        10**8,
    )(kept, got, slots, other)
    if apart:
        received = [
            permute(packed[k], lambda i, k=k: i ^ (2 * k)) if k else packed[k]
            for k in message_order(chips)
        ]
    else:
        groups = [[2 * k + c for k in range(chips)] for c in range(2)]
        received = [
            lax.all_to_all(
                packed[0], "grid", split_axis=0, concat_axis=0, axis_index_groups=groups, tiled=True
            )
        ]

    full = (2, lines, depth)
    small = (2, lines // 2, depth // 2)
    f, straight, across = call(
        density_kernel,
        [shaped(planes, *full), shaped(10, lines, 128), shaped(2, *full)],
        vmem(2 + len(received)),
        [(planes + 4, *full), (8, lines, 128)],
        10**8,
    )(pair_density, other, *received)
    even = permute(f, even_side)
    odd = permute(f, odd_side)
    straight = permute(straight, next_block)
    across = permute(across, lambda i: (i + (-4 if i // 2 % 2 else 4)) % tile_count)
    source = call(
        source_kernel,
        shaped(planes, *small),
        vmem(4) + smem,
        [(4 * planes, *full), (2 * planes + 4, *full), (4 * planes, lines, 128)],
        10**7,
    )(even, odd, straight, f, cs)
    pieces = gather_blocks(source, blocks, block, permute_block)
    own, send = call(
        fine_kernel,
        [shaped(thick, *full)] * 2,
        vmem(5) + smem,
        [(3 * planes + 4, *full), (planes + 8, *full), (planes + 4, *full), (planes, *full)],
        10**7,
    )(even, odd, straight, across, f, cs)
    got = permute(send, partner)

    n1, n2, n3 = tile_count, tile_count // 2, tile_count // 4
    tile = (8, 128)
    w_own, w_send = call(
        cycle_kernel,
        [shaped(5, *small)] * 2,
        vmem(len(pieces)) + smem,
        [
            (n1, *small),
            (n1 + 2, *small),
            (n1 + 2, *small),
            (n1, *small),
            (n2, *tile),
            (n2 + 2, *tile),
            (n2 + 2, *tile),
            (n2, 16, 128),
            (n3, *tile),
            (n3 + 2, *tile),
            (n3 + 2, *tile),
        ],
        10**8,
    )(*pieces, cs)
    w_got = permute(w_send, partner)
    scratch = [(20, lines, 128), (6, *full)]
    result = call(own_kernel, shaped(2, thick, lines, depth), vmem(2), scratch, 10**7)(w_own, own)
    return call(output_kernel, shaped(*pair_density.shape), vmem(3), scratch, 10**7)(
        result, w_got, got
    )


def solution(mesh):
    return jax.shard_map(
        per_device,
        mesh=mesh,
        in_specs=(
            P("rep", None, "grid", None, None),
            P(("rep", "grid"), None, None, None),
            P(("rep", "grid"), None, None),
            P(("rep", "grid")),
            P(("rep", "grid"), None),
            P(("rep", "grid")),
            P(),
            P(),
        ),
        out_specs=P("rep", None, "grid", None, None),
        check_vma=False,
    )
```

```python
import jax
import jax.numpy as jnp
from jax import lax
from jax.experimental import pallas as pl
from jax.experimental.pallas import tpu as pltpu
from jax.sharding import PartitionSpec as P

omega = 0.8
screen = 0.05

fine_diagonal = 7.5 + screen
fine_scale = omega / fine_diagonal
fine_near = fine_scale * 4.0 / 3.0
fine_far = fine_scale / 12.0
keep = 1.0 - omega


def level_numbers(depth):
    quarter = 1.0 / 4**depth
    diagonal = 6.0 * quarter + screen
    return omega / diagonal, omega / diagonal * quarter


def each(count, body, most=16):
    if count <= most:
        for i in range(count):
            body(i)
    else:
        pl.loop(0, count, unroll=4)(body)


def parts_of(values):
    parts = []
    for _ in range(3):
        parts.append(values.astype(jnp.bfloat16))
        values = values - parts[-1].astype(jnp.float32)
    return parts


def dot(values, exact):
    exact = exact.astype(jnp.bfloat16)
    products = [jnp.dot(p, exact, preferred_element_type=jnp.float32) for p in parts_of(values)]
    return products[0] + (products[1] + products[2])


def pick_dot(exact, values):
    exact = exact.astype(jnp.bfloat16)
    products = [jnp.dot(exact, p, preferred_element_type=jnp.float32) for p in parts_of(values)]
    return products[0] + (products[1] + products[2])


def pair_matrix(rows, columns, value):
    i = lax.broadcasted_iota(jnp.int32, (rows, columns), 0)
    j = lax.broadcasted_iota(jnp.int32, (rows, columns), 1)
    return jnp.where(i // 2 == j, value, 0.0)


def spread_matrix(rows, columns):
    i = lax.broadcasted_iota(jnp.int32, (rows, columns), 0)
    j = lax.broadcasted_iota(jnp.int32, (rows, columns), 1)
    return jnp.where(i == j // 2, 1.0, 0.0)


def roll(v, shift, axis):
    return pltpu.roll(v, shift % v.shape[axis], axis)


def smooth_fine(at, x, f):
    total = None
    for step, weight in ((1, fine_near), (2, -fine_far)):
        sides = [p for p in (at(x - step, f), at(x + step, f)) if p is not None]
        v = at(x, f)
        if v is not None:
            for axis in (0, 1):
                sides.append(roll(v, step, axis) + roll(v, -step, axis))
            if step == 1:
                total = keep * v
        if sides:
            part = weight * sum(sides[1:], sides[0])
            total = part if total is None else total + part
    return total


def rotated(real, imag, cosine, sine):
    return cosine * real - sine * imag, sine * real + cosine * imag


def place_planes(target, base, source, cosine, sine):
    for x in range(source.shape[0]):
        real, imag = rotated(source[x, 0], source[x, 1], cosine, sine)
        target[base + x, 0] = real
        target[base + x, 1] = imag


def place_halo(ext, middle, even_ref, odd_ref, cs_ref):
    position = lax.axis_index("grid")
    chips = lax.axis_size("grid") // 2
    core, chip = lax.rem(position, 2), lax.div(position, 2)
    cosine, sine = cs_ref[core], cs_ref[2 + core]
    first, last = chip == 0, chip == chips - 1
    low = (jnp.where(first, cosine, 1.0), jnp.where(first, -sine, 0.0))
    high = (jnp.where(last, cosine, 1.0), jnp.where(last, sine, 0.0))
    planes = even_ref.shape[0]
    parity = lax.rem(chip, 2)

    @pl.when(parity == 0)
    def _():
        place_planes(ext, middle - planes, odd_ref, *low)
        place_planes(ext, middle + planes, even_ref, *high)

    @pl.when(parity == 1)
    def _():
        place_planes(ext, middle - planes, even_ref, *low)
        place_planes(ext, middle + planes, odd_ref, *high)


def as_column(row):
    n = row.shape[1]
    i = lax.broadcasted_iota(jnp.int32, (n, n), 0)
    j = lax.broadcasted_iota(jnp.int32, (n, n), 1)
    return jnp.sum(jnp.where(i == j, row, 0.0), axis=1, keepdims=True)


def rows_kernel(moments_ref, shapes_ref, slots_ref, keep_ref, send_ref, rows):
    core = lax.rem(lax.axis_index("grid"), 2)
    channels, slots, depth = shapes_ref.shape
    atoms = moments_ref.shape[1]
    atom = as_column(slots_ref[0:1].astype(jnp.float32))
    picks = [jnp.where(atom == float(a), 1.0, 0.0) for a in range(atoms)]
    chosen = []
    for f in range(4):
        total = None
        for a in range(atoms):
            value = picks[a] * moments_ref[f, a : a + 1]
            total = value if total is None else total + value
        chosen.append(total)
    for i in range(slots // 8):
        near = slice(8 * i, 8 * i + 8)
        totals = [None] * 4
        for channel in range(channels):
            shape = shapes_ref[channel, near]
            for f in range(4):
                value = chosen[f][near, channel : channel + 1] * shape
                totals[f] = value if totals[f] is None else totals[f] + value
        for f in range(4):
            rows[f // 2, near, f % 2 * depth : (f % 2 + 1) * depth] = totals[f]
    keep_ref[...] = rows[core]
    send_ref[0:slots] = rows[1 - core]
    send_ref[slots:] = jnp.zeros((8, 2 * depth), jnp.float32)
    number = (slots_ref[1:2] * 64 + slots_ref[2:3]).astype(jnp.float32)
    send_ref[slots : slots + 1, 0:slots] = number


def pack_kernel(own_ref, got_ref, slots_ref, *out_refs):
    slots = own_ref.shape[0]
    apart = len(out_refs) > 1
    height = out_refs[0].shape[-2]
    ranks = (height - 8) // 4
    capacity = ranks // 4
    chips = lax.axis_size("grid") // 2
    chip = lax.div(lax.axis_index("grid"), 2)
    number = (slots_ref[1:2] * 64 + slots_ref[2:3]).astype(jnp.float32)
    number = jnp.concatenate([number, got_ref[slots : slots + 1, 0:slots]], axis=1).astype(jnp.int32)
    tile, line = number // 64, number % 128 + 1
    column = as_column(tile.astype(jnp.float32)).astype(jnp.int32)
    i = lax.broadcasted_iota(jnp.int32, (2 * slots, 2 * slots), 0)
    j = lax.broadcasted_iota(jnp.int32, (2 * slots, 2 * slots), 1)
    ahead = jnp.where((column == tile) & (i < j) & (i // slots == j // slots), 1.0, 0.0)
    rank = jnp.sum(ahead, axis=0, keepdims=True).astype(jnp.int32)
    device = lax.broadcasted_iota(jnp.int32, (1, 2 * slots), 1) // slots
    place = tile // 2 * ranks + (2 * device + tile % 2) * capacity + rank
    r = lax.broadcasted_iota(jnp.int32, (ranks, 2 * slots), 0)
    targets = [lax.bitwise_xor(chip, k) if apart else k for k in range(chips)]
    pick = jnp.concatenate([jnp.where(place == r + target * ranks, 1.0, 0.0) for target in targets])
    rows = jnp.concatenate([own_ref[...], got_ref[0:slots]], axis=0)
    packed = pick_dot(pick, rows)
    lines = jnp.sum(pick * line.astype(jnp.float32), axis=1, keepdims=True)
    bucket = lax.broadcasted_iota(jnp.int32, (chips * ranks, 128), 0)
    lane = lax.broadcasted_iota(jnp.int32, (chips * ranks, 128), 1)
    spot = bucket // ranks if apart else chip
    spots = jnp.where(lane == spot % (128 // ranks) * ranks + bucket % ranks, lines, 0.0)
    i = lax.broadcasted_iota(jnp.int32, (chips, chips * ranks), 0)
    j = lax.broadcasted_iota(jnp.int32, (chips, chips * ranks), 1)
    numbers = pick_dot(jnp.where(i == j // ranks, 1.0, 0.0), spots)
    for k in range(chips):
        out = out_refs[k] if apart else out_refs[0].at[k]
        for q in range(4):
            out[q * ranks : (q + 1) * ranks] = packed[
                k * ranks : (k + 1) * ranks, q * 128 : (q + 1) * 128
            ]
        out[4 * ranks :] = jnp.broadcast_to(numbers[k : k + 1], (8, 128))


def message_order(chips):
    half = chips // 2
    return [0, 1, *range(half + 2, chips), half, half + 1, *range(2, half)]


def density_kernel(*refs):
    pd_ref, other_ref = refs[:2]
    f_ref, straight_ref, across_ref, b1, half = refs[-5:]
    pieces = refs[2:-5]
    position = lax.axis_index("grid")
    core, side = lax.rem(position, 2), lax.rem(lax.div(position, 2), 2)
    planes, _, lines, depth = f_ref.shape
    sources = lax.axis_size("grid") // 2
    height = pieces[0].shape[-2]
    ranks = (height - 8) // 4
    group = 128 // ranks

    def received(source, start, stop):
        if len(pieces) > 1:
            return pieces[message_order(sources).index(source)][start:stop]
        return pieces[0][source, start:stop]

    added = [None, None]
    for first in range(0, sources, group):
        members = range(first, min(first + group, sources))
        numbers = sum(received(k, 4 * ranks, 4 * ranks + 1) for k in members)
        line = lax.broadcasted_iota(jnp.int32, (planes * lines, 128), 0)
        spread = jnp.where(line == numbers.astype(jnp.int32) - 1, 1.0, 0.0)
        for part in range(2):
            values = jnp.concatenate(
                [
                    jnp.concatenate(
                        [received(k, q * ranks, (q + 1) * ranks) for k in members], axis=0
                    )
                    for q in (2 * part, 2 * part + 1)
                ],
                axis=1,
            )
            value = pick_dot(spread[:, : len(members) * ranks], values)
            added[part] = value if added[part] is None else added[part] + value
    for x in range(planes):
        for part in range(2):
            f_ref[x, part] = added[part][x * lines : (x + 1) * lines]
    thick = planes // 2
    for x in range(thick):
        for part in range(2):
            f_ref[core * thick + x, part] += pd_ref[core, part, x]
            f_ref[(1 - core) * thick + x, part] += other_ref[part, x]

    def density(x, part):
        return f_ref[x, part] if 0 <= x < planes else None

    def once(x, part):
        return b1[x + 2, part] if -2 <= x < planes + 2 else None

    def outer(base, first_plane, one):
        for x in range(one, one + 4):
            for part in range(2):
                b1[x + 2, part] = smooth_fine(density, x, part)
        for i in range(2):
            for part in range(2):
                x = base + 2 * i
                total = smooth_fine(once, x, part) + smooth_fine(once, x + 1, part)
                for h in range(2):
                    half[(2 * i + part) * 2 + h] = total[:, h * 128 : (h + 1) * 128]
        for r, value in enumerate(lowered(half, 4, lines, depth)):
            straight_ref[8 + r // 2, r % 2 * 16 : r % 2 * 16 + 16] = value
        for x in range(2):
            for part in range(2):
                for h in range(2):
                    straight_ref[(2 * x + part) * 2 + h] = f_ref[
                        first_plane + x, part, :, h * 128 : (h + 1) * 128
                    ]
        other = planes - 2 - first_plane
        for x in range(2):
            across_ref[x] = f_ref[other + x]

    @pl.when(side == 0)
    def _():
        outer(-4, 0, -2)

    @pl.when(side == 1)
    def _():
        outer(planes, planes - 2, planes - 2)


def lowered(half, rows, lines, depth):
    matrix = pair_matrix(depth, depth // 2, 0.125)
    total = None
    for h in range(2):
        stacked = jnp.concatenate(
            [
                half[2 * r + h, pl.ds(0, lines // 2, 2)] + half[2 * r + h, pl.ds(1, lines // 2, 2)]
                for r in range(rows)
            ],
            axis=0,
        )
        value = dot(stacked, matrix[h * 128 : (h + 1) * 128])
        total = value if total is None else total + value
    return [total[r * lines // 2 : (r + 1) * lines // 2] for r in range(rows)]


def source_kernel(even_ref, odd_ref, straight_ref, f_ref, cs_ref, s_ref, ext, b1, half):
    position = lax.axis_index("grid")
    blocks = lax.axis_size("grid") // 4
    core, side, block = lax.rem(position, 2), lax.rem(lax.div(position, 2), 2), lax.div(position, 4)
    cosine, sine = cs_ref[core], cs_ref[2 + core]
    planes = f_ref.shape[0]
    lines, depth = f_ref.shape[2:]
    first, last = block == 0, block == blocks - 1
    low = (jnp.where(first, cosine, 1.0), jnp.where(first, -sine, 0.0))
    high = (jnp.where(last, cosine, 1.0), jnp.where(last, sine, 0.0))

    @pl.when(side == 0)
    def _():
        place_planes(ext, 0, odd_ref, *low)
        ext[planes : 2 * planes] = f_ref[...]
        ext[2 * planes : 3 * planes] = even_ref[...]
        ext[3 * planes :] = jnp.zeros((planes, 2, lines, depth), jnp.float32)

    @pl.when(side == 1)
    def _():
        ext[:planes] = jnp.zeros((planes, 2, lines, depth), jnp.float32)
        ext[planes : 2 * planes] = even_ref[...]
        ext[2 * planes : 3 * planes] = f_ref[...]
        place_planes(ext, 3 * planes, odd_ref, *high)

    for x in range(2 * planes + 4):
        for part in range(2):
            b1[x, part] = smooth_fine(lambda i, p: ext[i, p], x + planes - 2, part)
    for i in range(planes):
        for part in range(2):
            total = smooth_fine(lambda i, p: b1[i, p], 2 * i + 2, part) + smooth_fine(
                lambda i, p: b1[i, p], 2 * i + 3, part
            )
            for h in range(2):
                half[(2 * i + part) * 2 + h] = total[:, h * 128 : (h + 1) * 128]
    for r, value in enumerate(lowered(half, 2 * planes, lines, depth)):
        s_ref[r // 2, r % 2] = value

    def add(base, c, t):
        for x in range(2):
            real, imag = rotated(straight_ref[8 + x, 0:16], straight_ref[8 + x, 16:32], c, t)
            s_ref[base + x, 0] += real
            s_ref[base + x, 1] += imag

    @pl.when(side == 0)
    def _():
        add(2, *high)

    @pl.when(side == 1)
    def _():
        add(0, *low)


def fine_kernel(
    even_ref, odd_ref, straight_ref, across_ref, f_ref, cs_ref, own_ref, send_ref, ext, b1, b2, g
):
    position = lax.axis_index("grid")
    chips = lax.axis_size("grid") // 2
    core, chip = lax.rem(position, 2), lax.div(position, 2)
    cosine, sine = cs_ref[core], cs_ref[2 + core]
    planes = f_ref.shape[0]
    place_halo(ext, planes + 2, even_ref, odd_ref, cs_ref)
    ext[planes + 2 : 2 * planes + 2] = f_ref[...]
    first, last = chip < 2, chip >= chips - 2
    low = (jnp.where(first, cosine, 1.0), jnp.where(first, -sine, 0.0))
    high = (jnp.where(last, cosine, 1.0), jnp.where(last, sine, 0.0))

    def place_straight(base, c, t):
        for x in range(2):
            real, imag = [
                jnp.concatenate([straight_ref[4 * x + 2 * p], straight_ref[4 * x + 2 * p + 1]], axis=1)
                for p in range(2)
            ]
            ext[base + x, 0], ext[base + x, 1] = rotated(real, imag, c, t)

    @pl.when(lax.rem(chip, 2) == 0)
    def _():
        place_planes(ext, 0, across_ref, *low)
        place_straight(3 * planes + 2, *high)

    @pl.when(lax.rem(chip, 2) == 1)
    def _():
        place_straight(0, *low)
        place_planes(ext, 3 * planes + 2, across_ref, *high)

    for x in range(planes + 8):
        for part in range(2):
            b1[x, part] = smooth_fine(lambda i, p: ext[i, p], x + 2, part)
    for x in range(planes + 4):
        for part in range(2):
            b2[x, part] = smooth_fine(lambda i, p: b1[i, p], x + 2, part)
    for x in range(planes):
        for part in range(2):
            b3 = smooth_fine(lambda i, p: b2[i, p], x + 2, part)
            g[x, part] = fine_scale * (f_ref[x, part] + b1[x + 4, part] + b2[x + 2, part] + b3)
    half = planes // 2
    for x in range(half):
        own_ref[x] = g[core * half + x]
        send_ref[x] = g[(1 - core) * half + x]


def shift_z(v, step):
    width = v.shape[-1] // 2
    lane = lax.broadcasted_iota(jnp.int32, v.shape, len(v.shape) - 1)
    edge = 0 if step > 0 else width - 1
    inner = roll(v, step, 1)
    outer = roll(v, step + (width if step > 0 else -width), 1)
    return jnp.where(lane % width == edge, outer, inner)


def packed_sweep(values, count, depth, source, target, cosine, sine, residual=False):
    rate, near_rate = level_numbers(depth)
    values[0] = cosine * values[count] - sine * roll(values[count], 64, 1)
    values[count + 1] = cosine * values[1] + sine * roll(values[1], 64, 1)

    def body(x):
        v = values[x + 1]
        near = values[x] + values[x + 2]
        near = near + (roll(v, 1, 0) + roll(v, -1, 0))
        near = near + (shift_z(v, 1) + shift_z(v, -1))
        if residual:
            target[x] = source[x] - omega / rate * v + near_rate / rate * near
        else:
            target[x + 1] = rate * source[x] + keep * v + near_rate * near

    each(count, body)


def first_sweep(values, count, depth, source):
    rate, _ = level_numbers(depth)

    def body(x):
        values[x + 1] = rate * source[x]

    each(count, body)


def cycle_kernel(*refs):
    radix = len(refs) - 14
    pieces, refs = refs[:radix], refs[radix:]
    cs_ref, own_ref, send_ref, s, u, v, r1, s2, u2, v2, r2, s3, u3, v3 = refs
    position = lax.axis_index("grid")
    core, block = lax.rem(position, 2), lax.div(position, 4)
    count = s.shape[0]
    rate, near_rate = level_numbers(1)
    cosine, sine = cs_ref[core], cs_ref[2 + core]
    lane = lax.broadcasted_iota(jnp.int32, (8, 128), 1)
    lane_sine = jnp.where(lane < 64, -sine, sine)

    length = count // radix
    digit = lax.div(block, length // 4)
    for k, piece in enumerate(pieces):
        s[pl.ds(lax.bitwise_xor(lax.rem(digit, radix), k) * length, length)] = piece[...]

    def sweep(values, target, residual=False):
        values[0, 0], values[0, 1] = rotated(values[count, 0], values[count, 1], cosine, -sine)
        values[count + 1, 0], values[count + 1, 1] = rotated(
            values[1, 0], values[1, 1], cosine, sine
        )

        def body(x):
            for f in range(2):
                a = values[x + 1, f]
                near = values[x, f] + values[x + 2, f]
                near = near + (roll(a, 1, 0) + roll(a, -1, 0))
                near = near + (roll(a, 1, 1) + roll(a, -1, 1))
                if residual:
                    target[x, f] = s[x, f] - omega / rate * a + near_rate / rate * near
                else:
                    target[x + 1, f] = rate * s[x, f] + keep * a + near_rate * near

        each(count, body)

    def start(x):
        for f in range(2):
            u[x + 1, f] = rate * s[x, f]

    each(count, start)
    sweep(u, v)
    sweep(v, r1, residual=True)

    count2 = count // 2
    i = lax.broadcasted_iota(jnp.int32, (128, 128), 0)
    j = lax.broadcasted_iota(jnp.int32, (128, 128), 1)
    rows = []
    for f in range(2):

        def lower(x):
            r1[2 * x, f] = r1[2 * x, f] + r1[2 * x + 1, f]
            r2[x, 8 * f : 8 * f + 8] = r1[2 * x, f, pl.ds(0, 8, 2)] + r1[2 * x, f, pl.ds(1, 8, 2)]

        each(count2, lower)
        rows.append(r2[:, 8 * f : 8 * f + 8].reshape(count2 * 8, 128))
    lowered = sum(
        dot(rows[f], jnp.where(i // 2 + 64 * f == j, 0.125, 0.0)) for f in range(2)
    )
    s2[...] = lowered.reshape(count2, 8, 128)
    first_sweep(u2, count2, 2, s2)
    packed_sweep(u2, count2, 2, s2, v2, cosine, lane_sine)
    packed_sweep(v2, count2, 2, s2, u2, cosine, lane_sine, residual=True)

    count3 = count2 // 2

    def lower3(x):
        total = u2[2 * x] + u2[2 * x + 1]
        r2[x, 0:8] = total
        r2[x, 8:16] = total
        s3[x] = r2[x, pl.ds(0, 8, 2)] + r2[x, pl.ds(1, 8, 2)]

    each(count3, lower3)
    same = i // 64 == j // 64
    lowered = dot(
        s3[...].reshape(count3 * 8, 128), jnp.where(same & (i % 64 // 2 == j % 32), 0.125, 0.0)
    )
    s3[...] = lowered.reshape(count3, 8, 128)
    first_sweep(u3, count3, 3, s3)
    a, b = u3, v3
    for _ in range(5):
        packed_sweep(a, count3, 3, s3, b, cosine, lane_sine)
        a, b = b, a

    raised = dot(
        a[1 : count3 + 1].reshape(count3 * 8, 128),
        jnp.where(same & (i % 64 == j % 64 // 2), 1.0, 0.0),
    )
    s3[...] = raised.reshape(count3, 8, 128)

    def raise3(x):
        r2[x, pl.ds(0, 8, 2)] = s3[x]
        r2[x, pl.ds(1, 8, 2)] = s3[x]
        for k in range(2):
            v2[2 * x + k + 1] = v2[2 * x + k + 1] + r2[x, 0:8]

    each(count3, raise3)
    packed_sweep(v2, count2, 2, s2, u2, cosine, lane_sine)
    packed_sweep(u2, count2, 2, s2, v2, cosine, lane_sine)

    rows = v2[1 : count2 + 1].reshape(count2 * 8, 128)
    for f in range(2):
        raised = dot(rows, jnp.where(i == j // 2 + 64 * f, 1.0, 0.0))
        s2[...] = raised.reshape(count2, 8, 128)

        def raise2(x):
            r1[x, f, pl.ds(0, 8, 2)] = s2[x]
            r1[x, f, pl.ds(1, 8, 2)] = s2[x]
            for k in range(2):
                v[2 * x + k + 1, f] = v[2 * x + k + 1, f] + r1[x, f]

        each(count2, raise2)
    sweep(v, u)
    sweep(u, v)

    for target, tile in ((own_ref, position), (send_ref, position + 1 - 2 * core)):
        for k in range(5):
            q = tile + k - 2
            low, high = q < 0, q >= count
            q = jnp.where(low, q + count, jnp.where(high, q - count, q))
            c = jnp.where(low | high, cosine, 1.0)
            t = jnp.where(low, -sine, jnp.where(high, sine, 0.0))
            target[k, 0], target[k, 1] = rotated(v[q + 1, 0], v[q + 1, 1], c, t)


def correct(w_ref, g_ref, e, b1, store):
    lines = w_ref.shape[2]
    wide = dot(w_ref[...].reshape(10 * lines, 128), spread_matrix(128, 256))
    for r in range(10):
        for h in range(2):
            value = wide[r * lines : (r + 1) * lines, 128 * h : 128 * (h + 1)]
            e[2 * r + h, pl.ds(0, lines, 2)] = value
            e[2 * r + h, pl.ds(1, lines, 2)] = value

    def expanded(x, f):
        place = (2 * (x // 2) + f) * 2
        return jnp.concatenate([e[place], e[place + 1]], axis=1)

    for x in range(6):
        for f in range(2):
            b1[x, f] = smooth_fine(expanded, x + 2, f)
    for x in range(2):
        for f in range(2):
            store(f, x, g_ref[x, f] + smooth_fine(lambda i, g: b1[i, g], x + 2, f))


def own_kernel(w_ref, g_ref, out_ref, e, b1):
    def store(part, x, value):
        out_ref[part, x] = value

    correct(w_ref, g_ref, e, b1, store)


def output_kernel(own_ref, w_ref, g_ref, out_ref, e, b1):
    core = lax.rem(lax.axis_index("grid"), 2)
    out_ref[core] = own_ref[...]

    def store(part, x, value):
        out_ref[1 - core, part, x] = value

    correct(w_ref, g_ref, e, b1, store)


def pair_phases(pair_table, k_fraction):
    kcount = k_fraction.shape[0]
    picks = pair_table[:, :, None] == jnp.arange(kcount, dtype=jnp.int32)[None, None, :]
    chosen = jnp.sum(jnp.where(picks, k_fraction[None, None, :], 0.0), axis=2)
    angle = 6.283185307179586 * (chosen[:, 0] - chosen[:, 1])
    return jnp.concatenate([jnp.cos(angle), jnp.sin(angle)])


def gather_blocks(value, blocks, block, permute_block):
    stride = 1
    while True:
        radix = min(4, blocks // stride)
        digit = block // stride % radix
        pieces = [value] + [
            permute_block(value, lambda b, k=k: b ^ k * stride) for k in range(1, radix)
        ]
        stride *= radix
        if stride == blocks:
            return pieces
        stacked = jnp.stack(pieces)[jnp.arange(radix) ^ digit]
        value = stacked.reshape(-1, *value.shape[1:])


def vmem(count):
    return [pl.BlockSpec(memory_space=pltpu.VMEM)] * count


smem = [pl.BlockSpec(memory_space=pltpu.SMEM)]


def call(kernel, out_shape, in_specs, scratch, flops):
    single = not isinstance(out_shape, (list, tuple))
    return pl.pallas_call(
        kernel,
        out_shape=out_shape,
        in_specs=in_specs,
        out_specs=vmem(1)[0] if single else vmem(len(out_shape)),
        scratch_shapes=[pltpu.VMEM(shape, jnp.float32) for shape in scratch],
        compiler_params=pltpu.CompilerParams(vmem_limit_bytes=48 * 2**20),
        cost_estimate=pl.CostEstimate(flops=flops, bytes_accessed=2**20, transcendentals=0),
    )


def shaped(*shape):
    return jax.ShapeDtypeStruct(shape, jnp.float32)


def per_device(
    pair_density, moments, shapes, slot_atom, slot_tile, slot_row, pair_table, k_fraction
):
    tile_count = lax.axis_size("grid")
    chips, blocks = tile_count // 2, tile_count // 4
    position = lax.axis_index("grid")
    core, block = position % 2, position // 4
    _, _, thick, lines, depth = pair_density.shape
    planes = 2 * thick
    slot_count = shapes.shape[0]
    capacity = max(2, 2 * slot_count // tile_count)
    devices = range(tile_count)

    def permute(value, target):
        return lax.ppermute(value, "grid", [(i, target(i)) for i in devices])

    def permute_block(value, target):
        return permute(value, lambda i: target(i // 4) * 4 + i % 4)

    def partner(i):
        return i ^ 1

    def even_side(i):
        return i ^ 2

    def odd_side(i):
        return (i // 2 + (1 if i // 2 % 2 else -1)) % chips * 2 + i % 2

    def next_block(i):
        return (i + (4 if i // 2 % 2 else -4)) % tile_count

    cs = pair_phases(pair_table, k_fraction)

    other = permute(lax.dynamic_index_in_dim(pair_density, 1 - core, 0, False), partner)
    slots = jnp.stack([slot_atom, slot_tile[:, 0], slot_row])
    fields = moments.reshape(moments.shape[0], 4, -1).transpose(1, 0, 2)
    row = 2 * depth
    kept, sent = call(
        rows_kernel,
        [shaped(slot_count, row), shaped(slot_count + 8, row)],
        vmem(3),
        [(2, slot_count, row)],
        10**7,
    )(fields, shapes.transpose(1, 0, 2), slots)
    got = permute(sent, partner)
    apart = chips <= 8
    height = 16 * capacity + 8
    packed = call(
        pack_kernel,
        [shaped(height, 128)] * chips if apart else [shaped(chips, height, 128)],
        vmem(3),
        [],
        10**8,
    )(kept, got, slots)
    if apart:
        received = [
            permute(packed[k], lambda i, k=k: i ^ (2 * k)) if k else packed[k]
            for k in message_order(chips)
        ]
    else:
        groups = [[2 * k + c for k in range(chips)] for c in range(2)]
        received = [
            lax.all_to_all(
                packed[0], "grid", split_axis=0, concat_axis=0, axis_index_groups=groups, tiled=True
            )
        ]

    full = (2, lines, depth)
    small = (2, lines // 2, depth // 2)
    f, straight, across = call(
        density_kernel,
        [shaped(planes, *full), shaped(10, lines, 128), shaped(2, *full)],
        vmem(2 + len(received)),
        [(planes + 4, *full), (8, lines, 128)],
        10**8,
    )(pair_density, other, *received)
    even = permute(f, even_side)
    odd = permute(f, odd_side)
    straight = permute(straight, next_block)
    across = permute(across, lambda i: (i + (-4 if i // 2 % 2 else 4)) % tile_count)
    source = call(
        source_kernel,
        shaped(planes, *small),
        vmem(4) + smem,
        [(4 * planes, *full), (2 * planes + 4, *full), (4 * planes, lines, 128)],
        10**7,
    )(even, odd, straight, f, cs)
    pieces = gather_blocks(source, blocks, block, permute_block)
    own, send = call(
        fine_kernel,
        [shaped(thick, *full)] * 2,
        vmem(5) + smem,
        [(3 * planes + 4, *full), (planes + 8, *full), (planes + 4, *full), (planes, *full)],
        10**7,
    )(even, odd, straight, across, f, cs)
    got = permute(send, partner)

    n1, n2, n3 = tile_count, tile_count // 2, tile_count // 4
    tile = (8, 128)
    w_own, w_send = call(
        cycle_kernel,
        [shaped(5, *small)] * 2,
        vmem(len(pieces)) + smem,
        [
            (n1, *small),
            (n1 + 2, *small),
            (n1 + 2, *small),
            (n1, *small),
            (n2, *tile),
            (n2 + 2, *tile),
            (n2 + 2, *tile),
            (n2, 16, 128),
            (n3, *tile),
            (n3 + 2, *tile),
            (n3 + 2, *tile),
        ],
        10**8,
    )(*pieces, cs)
    w_got = permute(w_send, partner)
    scratch = [(20, lines, 128), (6, *full)]
    result = call(own_kernel, shaped(2, thick, lines, depth), vmem(2), scratch, 10**7)(w_own, own)
    return call(output_kernel, shaped(*pair_density.shape), vmem(3), scratch, 10**7)(
        result, w_got, got
    )


def solution(mesh):
    return jax.shard_map(
        per_device,
        mesh=mesh,
        in_specs=(
            P("rep", None, "grid", None, None),
            P(("rep", "grid"), None, None, None),
            P(("rep", "grid"), None, None),
            P(("rep", "grid")),
            P(("rep", "grid"), None),
            P(("rep", "grid")),
            P(),
            P(),
        ),
        out_specs=P("rep", None, "grid", None, None),
        check_vma=False,
    )
```
